256 devices in a mesh: row: 32 (over x_lo, z, core), col: 8 (over y, x_hi).
Axes of the slice: x: 4 (x_hi: 2, x_lo: 2; x = x_hi * 2 + x_lo), y: 4, z: 8, core: 2. Of those that a mesh axis runs over, the one named last changes fastest.
Arguments:
- image_embed: bfloat16 [12288, 1024], P(('row', 'col')), may hold values from -30 to 30
- text_embed: bfloat16 [12288, 1024], P(('col', 'row')), may hold values from -30 to 30
- pair_index: int32 [12288], P('row'), may hold values from 0 to 12287, each once
Outputs:
- loss: float32 [], replicated
- grad_image: float32 [12288, 1024], P(('row', 'col'))
- grad_text: float32 [12288, 1024], P(('col', 'row'))
The draws below stay inside these ranges and needn't reach their ends.
All inputs are finite; a program needn't handle non-finite values.
Results may differ from the reference program's by a relative error of at most 0.0015.
Values may be sent and summed in bfloat16 or wider, within the bound.
No kernel may reach another device: no remote copies, remote signals or barrier semaphores. Data moves between devices by JAX's collectives and lax.ppermute only.
A program may use at most 128 MiB of HBM per device.

```python
import math
import jax
import jax.numpy as jnp
from jax import lax

D = 1024
ROWS_DEV = 384
PAIRS = 12288
N_ROW = 32


def shared_rows(key):
    text_raw = jnp.clip(jax.random.normal(jax.random.fold_in(key, 101), (PAIRS, D), jnp.float32), -4.0, 4.0)
    text_scale = jnp.exp(jax.random.uniform(jax.random.fold_in(key, 102), (PAIRS, 1), jnp.float32, math.log(0.3), math.log(3.0)))
    chosen_image = jax.random.permutation(jax.random.fold_in(key, 103), PAIRS)[:8]
    chosen_text = jax.random.permutation(jax.random.fold_in(key, 104), PAIRS)[:8]
    return (text_raw, text_scale, chosen_image, chosen_text)


def aligned_rows(text_raw, chosen, strengths, result):
    factor = jnp.sqrt(strengths) * D ** (-0.25)
    leading = text_raw[chosen[:4]] * factor[:, None]
    shrink = 1.0 - 2.0 / strengths
    result = result.at[chosen[:4]].set(leading)
    return result.at[chosen[4:]].set(leading * shrink[:, None])


def draw_text_embed(key, part):
    text_raw, text_scale, chosen_image, chosen_text = shared_rows(key)
    result = text_raw * text_scale
    strengths = jnp.array([100.0, 120.0, 140.0, 160.0], jnp.float32)
    result = aligned_rows(text_raw, chosen_text, strengths, result)
    return result.astype(jnp.bfloat16)


def draw_image_embed(key, part):
    text_raw, text_scale, chosen_image, chosen_text = shared_rows(key)
    key = jax.random.fold_in(key, 7)
    row_scale = jnp.exp(jax.random.uniform(jax.random.fold_in(key, 1), (PAIRS, 1), jnp.float32, math.log(0.3), math.log(3.0)))
    entries = jnp.clip(jax.random.normal(jax.random.fold_in(key, 2), (PAIRS, D), jnp.float32), -4.0, 4.0)
    strengths = jnp.array([100.0, 120.0, 140.0, 160.0], jnp.float32)
    result = entries * row_scale
    placed = jnp.zeros((PAIRS, D), jnp.float32)
    placed = aligned_rows(text_raw, chosen_text, strengths, placed)
    result = result.at[chosen_image].set(placed[chosen_text])
    return result.astype(jnp.bfloat16)


def setup_inputs(seed: int = 0) -> dict:
    streams_of = jax.random.split(jax.random.key(seed), 4)
    return {
        "image_embed": draw_image_embed(jax.random.fold_in(streams_of[3], 71), 0),
        "text_embed": draw_text_embed(jax.random.fold_in(streams_of[3], 71), 0),
        "pair_index": jax.random.permutation(streams_of[2], PAIRS).astype(jnp.int32),
    }


def tile_scores(block, text_embed):
    product = lax.dot_general(block, text_embed, (((1,), (1,)), ((), ())), preferred_element_type=jnp.float32)
    return product * (D ** -0.5)


def reference(image_embed, text_embed, pair_index):
    inv_root = D ** -0.5
    image_blocks = image_embed.reshape(N_ROW, ROWS_DEV, D)
    pair_blocks = pair_index.reshape(N_ROW, ROWS_DEV)

    def first_sweep(carry, block):
        col_high, col_mass = carry
        score_tile = tile_scores(block, text_embed)
        row_high = jnp.max(score_tile, axis=1)
        row_lse = row_high + jnp.log(jnp.sum(jnp.exp(score_tile - row_high[:, None]), axis=1))
        new_high = jnp.maximum(col_high, jnp.max(score_tile, axis=0))
        col_mass = col_mass * jnp.exp(col_high - new_high) + jnp.sum(jnp.exp(score_tile - new_high[None, :]), axis=0)
        return (new_high, col_mass), row_lse

    initial = (jnp.full((PAIRS,), -1e30, jnp.float32), jnp.zeros((PAIRS,), jnp.float32))
    (col_high, col_mass), row_lse = lax.scan(first_sweep, initial, image_blocks)
    col_lse = col_high + jnp.log(col_mass)
    column_ids = jnp.arange(PAIRS, dtype=jnp.int32)

    def second_sweep(grad_text, inputs):
        block, pairs, lse_rows = inputs
        score_tile = tile_scores(block, text_embed)
        positive = pairs[:, None] == column_ids[None, :]
        probs = 0.5 * (jnp.exp(score_tile - lse_rows[:, None]) + jnp.exp(score_tile - col_lse[None, :]))
        grad_scores = (probs - positive.astype(jnp.float32)).astype(jnp.bfloat16)
        grad_image = jnp.dot(grad_scores, text_embed, preferred_element_type=jnp.float32) * inv_root
        grad_text = grad_text + lax.dot_general(grad_scores, block, (((0,), (0,)), ((), ())), preferred_element_type=jnp.float32) * inv_root
        matched = jnp.sum(jnp.where(positive, score_tile, 0.0))
        return grad_text, (grad_image, matched)

    grad_text, (grad_image, matched) = lax.scan(second_sweep, jnp.zeros((PAIRS, D), jnp.float32), (image_blocks, pair_blocks, row_lse))
    loss = (jnp.sum(row_lse) + jnp.sum(col_lse) - 2.0 * jnp.sum(matched)) / (2.0 * PAIRS)
    return loss, grad_image.reshape(PAIRS, D), grad_text
```

```python
import jax
import jax.numpy as jnp
from jax import lax
from jax.sharding import Mesh, PartitionSpec as P

PLANE = ("xl", "y", "xh")


def combine(parts):
    high = jnp.max(parts, axis=0)
    return high + jnp.log(jnp.sum(jnp.exp(parts - high[None]), axis=0))


def spread(x, axes, count):
    return lax.all_to_all(jnp.broadcast_to(x[None], (count,) + x.shape), axes, 0, 0)


def shards(image_embed, text_embed, pair_index):
    rows, width = image_embed.shape
    n_xl, n_z, n_c, n_y, n_xh = (lax.axis_size(a) for a in ("xl", "z", "c", "y", "xh"))
    n_plane = n_xl * n_y * n_xh
    pairs = rows * n_plane * n_z * n_c
    inv_root = width ** (-0.5)
    core = lax.axis_index("c")
    swap = [(0, 1), (1, 0)]

    pair_other = lax.ppermute(pair_index, "xl", swap)
    first = lax.axis_index("xl") == 0
    pair_rows = jnp.concatenate(
        [jnp.where(first, pair_index, pair_other), jnp.where(first, pair_other, pair_index)]
    )

    text_own = spread(text_embed, "z", n_z).reshape(n_z * rows, width)
    text_other = lax.ppermute(text_own, "c", swap)
    text = jnp.concatenate([text_own, text_other], axis=0)
    image = spread(image_embed, PLANE, n_plane).reshape(n_plane * rows, width)

    half = n_z * rows
    scores = (
        lax.dot_general(image, text, (((1,), (1,)), ((), ())), preferred_element_type=jnp.float32)
        * inv_root
    )
    block = (lax.axis_index("y") * n_xh + lax.axis_index("xh")) * n_xl + lax.axis_index("xl")
    slot = lax.iota(jnp.int32, 2 * half)
    own = slot < half
    within = jnp.where(own, slot, slot - half)
    column = (
        ((block * n_z + within // rows) * n_c + jnp.where(own, core, 1 - core)) * rows
        + within % rows
    )
    positive = pair_rows[:, None] == column[None, :]
    matched = jnp.sum(jnp.where(positive, scores, 0.0))

    row_high = jnp.max(scores, axis=1)
    row_part = row_high + jnp.log(jnp.sum(jnp.exp(scores - row_high[:, None]), axis=1))
    col_high = jnp.max(scores, axis=0)
    col_part = col_high + jnp.log(jnp.sum(jnp.exp(scores - col_high[None, :]), axis=0))

    row_sent = jnp.concatenate([row_part, jnp.broadcast_to(matched, (128,))])
    row_got = spread(row_sent, PLANE, n_plane)
    row_lse = combine(row_got[:, : 2 * half])
    row_terms = jnp.sum(row_lse) - 2.0 * jnp.sum(row_got[:, 2 * half])

    col_sent = jnp.concatenate([col_part, jnp.broadcast_to(row_terms, (128,))])
    col_seen = lax.ppermute(col_sent, "c", swap)
    col_seen_lse = jnp.concatenate([col_seen[half : 2 * half], col_seen[:half]])
    col_pair = combine(jnp.stack([col_part, col_seen_lse]))
    terms_pair = row_terms + col_seen[2 * half]
    col_got = spread(jnp.concatenate([col_pair, jnp.broadcast_to(terms_pair, (128,))]), "z", n_z)
    col_lse = combine(col_got[:, : 2 * half])
    all_row_terms = jnp.sum(col_got[:, 2 * half])
    col_terms = jnp.sum(col_lse)

    probs = 0.5 * (jnp.exp(scores - row_lse[:, None]) + jnp.exp(scores - col_lse[None, :]))
    grad_scores = (probs - positive.astype(jnp.float32)).astype(jnp.bfloat16)

    image_part = jnp.dot(grad_scores, text, preferred_element_type=jnp.float32) * inv_root
    image_sent = jnp.concatenate(
        [
            image_part.reshape(n_plane, rows, width),
            jnp.broadcast_to(col_terms, (n_plane, 8, width)),
        ],
        axis=1,
    )
    image_got = lax.all_to_all(image_sent, PLANE, 0, 0)
    grad_image = jnp.sum(image_got[:, :rows], axis=0)
    loss = (all_row_terms + jnp.sum(image_got[:, rows, 0])) / (2.0 * pairs)

    text_part = (
        lax.dot_general(
            grad_scores, image, (((0,), (0,)), ((), ())), preferred_element_type=jnp.float32
        )
        * inv_root
    )
    text_sum = text_part[:half] + lax.ppermute(text_part[half:], "c", swap)
    text_got = lax.all_to_all(text_sum.reshape(n_z, rows, width), "z", 0, 0)
    grad_text = jnp.sum(text_got, axis=0)
    return (loss, grad_image, grad_text)


def solution(mesh):
    fine = Mesh(mesh.devices.reshape(2, 8, 2, 4, 2), ("xl", "z", "c", "y", "xh"))
    image_spec = P(("xl", "z", "c", "y", "xh"), None)
    text_spec = P(("y", "xh", "xl", "z", "c"), None)
    return jax.shard_map(
        shards,
        mesh=fine,
        in_specs=(image_spec, text_spec, P(("xl", "z", "c"))),
        out_specs=(P(), image_spec, text_spec),
        check_vma=False,
    )
```

```python
import jax
import jax.numpy as jnp
from jax import lax
from jax.sharding import Mesh, PartitionSpec as P

PLANE = ("xl", "y", "xh")
SWAP = [(0, 1), (1, 0)]


def combine(parts):
    high = jnp.max(parts, axis=0)
    return high + jnp.log(jnp.sum(jnp.exp(parts - high[None]), axis=0))


def turn(x, axis, step):
    count = lax.axis_size(axis)
    return lax.ppermute(x, axis, [(i, (i + step) % count) for i in range(count)])


def encode(x, scale):
    scaled = x * scale
    square = scaled * scaled
    fourth = square * square
    return jnp.where(scaled < 0, -fourth, fourth).astype(jnp.bfloat16)


def decode(x, unit):
    wide = x.astype(jnp.float32)
    root = jnp.sqrt(jnp.sqrt(jnp.abs(wide))) * unit
    return jnp.where(wide < 0, -root, root)


def split3(value, shape):
    high = value.astype(jnp.bfloat16)
    rest = value - high.astype(jnp.float32)
    mid = rest.astype(jnp.bfloat16)
    low = (rest - mid.astype(jnp.float32)).astype(jnp.bfloat16)
    row = lax.broadcasted_iota(jnp.int32, shape, len(shape) - 2)
    return jnp.where(row == 0, high, jnp.where(row == 1, mid, jnp.where(row == 2, low, 0)))


def inverse(value):
    return jnp.where(value > 0, 1.0 / value, 1.0)


def shards(image_embed, text_embed, pair_index):
    rows, width = image_embed.shape
    n_xl, n_z, n_c, n_y, n_xh = (lax.axis_size(a) for a in ("xl", "z", "c", "y", "xh"))
    n_plane = n_xl * n_y * n_xh
    pairs = rows * n_plane * n_z * n_c
    inv_root = width ** (-0.5)
    core = lax.axis_index("c")
    z = lax.axis_index("z")
    half = n_z * rows

    pair_other = lax.ppermute(pair_index, "xl", SWAP)
    first = lax.axis_index("xl") == 0
    pair_rows = jnp.concatenate(
        [jnp.where(first, pair_index, pair_other), jnp.where(first, pair_other, pair_index)]
    )

    image = lax.all_to_all(
        jnp.broadcast_to(image_embed[None], (n_plane, rows, width)), PLANE, 0, 0
    ).reshape(n_plane * rows, width)
    text_own = jnp.concatenate([text_embed] + [turn(text_embed, "z", -q) for q in range(1, n_z)])
    text = jnp.concatenate([text_own, lax.ppermute(text_own, "c", SWAP)], axis=0)

    scores = (
        lax.dot_general(image, text, (((1,), (1,)), ((), ())), preferred_element_type=jnp.float32)
        * inv_root
    )
    block = (lax.axis_index("y") * n_xh + lax.axis_index("xh")) * n_xl + lax.axis_index("xl")
    slot = lax.iota(jnp.int32, 2 * half)
    own = slot < half
    within = jnp.where(own, slot, slot - half)
    holder = (z + within // rows) % n_z
    column = ((block * n_z + holder) * n_c + jnp.where(own, core, 1 - core)) * rows + within % rows
    positive = pair_rows[:, None] == column[None, :]
    matched = jnp.sum(jnp.where(positive, scores, 0.0))
    text_max = jnp.max(jnp.abs(text)).astype(jnp.float32)
    image_max = jnp.max(jnp.abs(image)).astype(jnp.float32)

    row_high = jnp.max(scores, axis=1)
    row_part = row_high + jnp.log(jnp.sum(jnp.exp(scores - row_high[:, None]), axis=1))
    col_high = jnp.max(scores, axis=0)
    col_part = col_high + jnp.log(jnp.sum(jnp.exp(scores - col_high[None, :]), axis=0))

    row_sent = jnp.concatenate(
        [row_part, jnp.broadcast_to(matched, (128,)), jnp.broadcast_to(text_max, (128,))]
    )
    row_got = lax.all_to_all(
        jnp.broadcast_to(row_sent[None], (n_plane,) + row_sent.shape), PLANE, 0, 0
    )
    row_lse = combine(row_got[:, : 2 * half])
    row_terms = jnp.sum(row_lse) - 2.0 * jnp.sum(row_got[:, 2 * half])
    text_max = jnp.max(row_got[:, 2 * half + 128])

    ring = jnp.concatenate([col_part.reshape(2, n_z, rows)] * 2, axis=1)
    col_sorted = lax.dynamic_slice_in_dim(ring, n_z - z, n_z, axis=1).reshape(2 * half)
    col_sent = jnp.concatenate([col_sorted, jnp.broadcast_to(image_max, (128,))])
    col_seen = lax.ppermute(col_sent, "c", SWAP)
    col_seen = jnp.concatenate([col_seen[half : 2 * half], col_seen[:half], col_seen[2 * half :]])
    col_pair = jnp.concatenate(
        [
            combine(jnp.stack([col_sent[: 2 * half], col_seen[: 2 * half]])),
            jnp.maximum(col_sent[2 * half :], col_seen[2 * half :]),
        ]
    )
    col_got = jnp.stack([col_pair] + [turn(col_pair, "z", q) for q in range(1, n_z)])
    col_sorted = combine(col_got[:, : 2 * half])
    image_max = jnp.max(col_got[:, 2 * half])
    col_terms = jnp.sum(col_sorted)
    ring = jnp.concatenate([col_sorted.reshape(2, n_z, rows)] * 2, axis=1)
    col_lse = lax.dynamic_slice_in_dim(ring, z, n_z, axis=1).reshape(2 * half)

    probs = 0.5 * (jnp.exp(scores - row_lse[:, None]) + jnp.exp(scores - col_lse[None, :]))
    grad_scores = (probs - positive.astype(jnp.float32)).astype(jnp.bfloat16)

    image_part = jnp.dot(grad_scores, text, preferred_element_type=jnp.float32) * inv_root
    image_sent = jnp.concatenate(
        [
            encode(image_part, inverse(text_max)).reshape(n_plane, rows, width),
            split3(col_terms, (n_plane, 8, width)),
        ],
        axis=1,
    )
    image_got = lax.all_to_all(image_sent, PLANE, 0, 0)

    text_part = (
        lax.dot_general(
            grad_scores, image, (((0,), (0,)), ((), ())), preferred_element_type=jnp.float32
        )
        * inv_root
    )
    row_terms = row_terms + lax.ppermute(row_terms, "c", SWAP)
    text_sum = text_part[:half] + lax.ppermute(text_part[half:], "c", SWAP)
    text_sum = text_sum.reshape(n_z, rows, width)
    text_sent = jnp.concatenate(
        [
            encode(text_sum[1:], inverse(image_max)),
            split3(row_terms, (n_z - 1, 8, width)),
        ],
        axis=1,
    )
    text_got = jnp.stack([turn(text_sent[q - 1], "z", q) for q in range(1, n_z)])
    grad_text = text_sum[0] + jnp.sum(decode(text_got[:, :rows], 1.0 / inverse(image_max)), axis=0)
    grad_image = jnp.sum(decode(image_got[:, :rows], 1.0 / inverse(text_max)), axis=0)
    loss = (
        row_terms
        + jnp.sum(text_got[:, rows : rows + 3, 0].astype(jnp.float32))
        + jnp.sum(image_got[:, rows : rows + 3, 0].astype(jnp.float32))
    ) / (2.0 * pairs)
    return (loss, grad_image, grad_text)


def solution(mesh):
    fine = Mesh(mesh.devices.reshape(2, 8, 2, 4, 2), ("xl", "z", "c", "y", "xh"))
    image_spec = P(("xl", "z", "c", "y", "xh"), None)
    text_spec = P(("y", "xh", "xl", "z", "c"), None)
    return jax.shard_map(
        shards,
        mesh=fine,
        in_specs=(image_spec, text_spec, P(("xl", "z", "c"))),
        out_specs=(P(), image_spec, text_spec),
        check_vma=False,
    )
```

```python
import functools

import jax
import jax.numpy as jnp
from jax import lax
from jax.experimental import pallas as pl
from jax.experimental.pallas import tpu as pltpu
from jax.sharding import Mesh, PartitionSpec as P

PLANE = ("xl", "y", "xh")
SWAP = [(0, 1), (1, 0)]
LANES = 128
EXTRA = 16
F32 = jnp.float32
BF16 = jnp.bfloat16


def turn(x, axis, step):
    count = lax.axis_size(axis)
    return lax.ppermute(x, axis, [(i, (i + step) % count) for i in range(count)])


def merge(parts):
    high = functools.reduce(jnp.maximum, parts)
    return high + jnp.log(sum(jnp.exp(p - high) for p in parts))


def encode(scaled):
    square = scaled * scaled
    fourth = square * square
    return jnp.where(scaled < 0, -fourth, fourth).astype(BF16)


def decode(x):
    wide = x.astype(F32)
    root = jnp.sqrt(jnp.sqrt(jnp.abs(wide)))
    return jnp.where(wide < 0, -root, root)


def split3(value):
    high = value.astype(BF16).astype(F32)
    mid = (value - high).astype(BF16).astype(F32)
    low = value - high - mid
    row = lax.broadcasted_iota(jnp.int32, (EXTRA, LANES), 0)
    parts = jnp.where(row == 0, high, jnp.where(row == 1, mid, jnp.where(row == 2, low, 0.0)))
    return parts.astype(BF16)


def inverse(value):
    return jnp.where(value > 0, 1.0 / value, 1.0)


def to_column(row):
    return jnp.transpose(jnp.broadcast_to(row, (LANES, row.shape[1])))[:, :1]


def to_row(column):
    return jnp.transpose(jnp.broadcast_to(column, (column.shape[0], LANES)))[:1, :]


def call(body, outs, args, name, flops=0, exps=0, smem_out=None):
    size = sum(a.size * a.dtype.itemsize for a in (*args, *outs))
    spaces = [pltpu.SMEM if i == smem_out else pltpu.VMEM for i in range(len(outs))]
    return pl.pallas_call(
        body,
        out_shape=outs,
        in_specs=[pl.BlockSpec(memory_space=pltpu.VMEM)] * len(args),
        out_specs=tuple(pl.BlockSpec(memory_space=s) for s in spaces),
        cost_estimate=pl.CostEstimate(flops=flops, bytes_accessed=size, transcendentals=exps),
        compiler_params=pltpu.CompilerParams(vmem_limit_bytes=48 * 1024 * 1024),
        name=name,
    )(*args)


def score_body(n_z, inv_root, *refs):
    pieces, (image, pair, ids, scores, text, sent) = refs[: 2 * n_z], refs[2 * n_z :]
    rows = pieces[0].shape[0]
    size = image.shape[0]
    z = lax.axis_index("z")
    high = jnp.zeros(pieces[0].shape, F32)
    for h in range(2):
        for q in range(n_z):
            piece = pieces[h * n_z + q][...]
            start = h * n_z * rows + lax.rem(z + q, n_z) * rows
            text[pl.ds(pl.multiple_of(start, 16), rows), :] = piece
            high = jnp.maximum(high, jnp.abs(piece.astype(F32)))
    found = jnp.zeros((1, size), F32)
    step = 256
    for r in range(0, size, step):
        tile = (
            lax.dot_general(
                image[r : r + step, :],
                text[...],
                (((1,), (1,)), ((), ())),
                preferred_element_type=F32,
            )
            * inv_root
        )
        scores[r : r + step, :] = tile
        top = jnp.max(tile, axis=1, keepdims=True)
        part = top + jnp.log(jnp.sum(jnp.exp(tile - top), axis=1, keepdims=True))
        sent[:, 0, r : r + step] = jnp.broadcast_to(to_row(part), (sent.shape[0], step))
        hit = to_column(pair[:, r : r + step]) == ids[...]
        found += jnp.sum(jnp.where(hit, tile, 0.0), axis=0, keepdims=True)
    sent[:, 0, size : size + LANES] = jnp.full((sent.shape[0], LANES), jnp.sum(found))
    sent[:, 0, size + LANES :] = jnp.full((sent.shape[0], LANES), jnp.max(high))


def column_body(scores, image, sent):
    size = scores.shape[1]
    tile = scores[...]
    top = jnp.max(tile, axis=0, keepdims=True)
    part = top + jnp.log(jnp.sum(jnp.exp(tile - top), axis=0, keepdims=True))
    sent[:, :size] = part
    high = jnp.max(jnp.abs(image[...].astype(F32)))
    sent[:, size:] = jnp.full((1, LANES), high)


def pair_body(mine, seen, out):
    size = mine.shape[1] - LANES
    half = size // 2
    other = jnp.concatenate([seen[:, half:size], seen[:, :half]], axis=1)
    out[:, :size] = merge([mine[:, :size], other])
    out[:, size:] = jnp.maximum(mine[:, size:], seen[:, size:])


def image_body(n_z, inv_root, *refs):
    cols = refs[:n_z]
    scores, text, row_got, pair, ids, grads, sent, terms = refs[n_z:]
    size = scores.shape[0]
    n_plane = sent.shape[0]
    rows = size // n_plane
    col_lse = merge([c[:, :size] for c in cols])
    image_max = functools.reduce(jnp.maximum, [c[:, size:] for c in cols])
    row_lse = merge([row_got[i : i + 1, :size] for i in range(n_plane)])
    matched = jnp.sum(row_got[:, size : size + LANES], axis=0, keepdims=True)
    text_max = jnp.max(row_got[:, size + LANES :], axis=0, keepdims=True)
    row_terms = jnp.sum(row_lse, axis=1, keepdims=True) - 2.0 * matched
    col_terms = jnp.broadcast_to(jnp.sum(col_lse, axis=1, keepdims=True), (1, LANES))
    terms[...] = jnp.concatenate(
        [row_terms, text_max, image_max, jnp.zeros((5, LANES), F32)], axis=0
    )
    extra = split3(col_terms)
    scale = inverse(text_max[:, :1]) * inv_root
    step = 384
    for r in range(0, size, step):
        tile = scores[r : r + step, :]
        probs = 0.5 * (
            jnp.exp(tile - to_column(row_lse[:, r : r + step])) + jnp.exp(tile - col_lse)
        )
        hit = to_column(pair[:, r : r + step]) == ids[...]
        grad = (probs - jnp.where(hit, 1.0, 0.0)).astype(BF16)
        grads[r : r + step, :] = grad
        part = encode(jnp.dot(grad, text[...], preferred_element_type=F32) * scale)
        for p in range(step // rows):
            to = r // rows + p
            for k in range(text.shape[1] // LANES):
                sent[to, k * rows : (k + 1) * rows, :] = part[
                    p * rows : (p + 1) * rows, k * LANES : (k + 1) * LANES
                ]
            sent[to, k * rows + rows :, :] = extra


def text_body(inv_root, grads, image, own, other):
    half = own.shape[0]
    for out, start in ((other, half), (own, 0)):
        out[...] = (
            lax.dot_general(
                grads[:, start : start + half],
                image[...],
                (((0,), (0,)), ((), ())),
                preferred_element_type=F32,
            )
            * inv_root
        )


def send_body(n_z, own, seen, terms, terms_seen, keep, total, *pays):
    rows = keep.shape[0]
    z = lax.axis_index("z")
    row_terms = terms[0:1, :] + terms_seen[0:1, :]
    total[...] = row_terms
    extra = split3(row_terms)
    scale = inverse(terms[2:3, :1])
    for q in range(n_z):
        at = pl.ds(pl.multiple_of(lax.rem(z + q, n_z) * rows, 16), rows)
        block = own[at, :] + seen[at, :]
        if q == 0:
            keep[...] = block
            continue
        pay = pays[q - 1]
        part = encode(block * scale)
        count = block.shape[1] // LANES
        for k in range(count):
            pay[k * rows : (k + 1) * rows, :] = part[:, k * LANES : (k + 1) * LANES]
        pay[count * rows :, :] = extra


def image_sum_body(got, terms, out, side):
    rows, width = out.shape
    unit = terms[1:2, :1]
    unit = jnp.where(unit > 0, unit, 1.0)
    count = width // LANES
    for k in range(count):
        at = slice(k * rows, (k + 1) * rows)
        out[:, k * LANES : (k + 1) * LANES] = unit * sum(
            decode(got[p, at, :]) for p in range(got.shape[0])
        )
    tail = sum(got[p, count * rows :, :].astype(F32) for p in range(got.shape[0]))
    side[...] = jnp.sum(tail, axis=0, keepdims=True)


def text_sum_body(pairs, keep, total, terms, side, *refs):
    pays, out, loss = refs[:-2], refs[-2], refs[-1]
    rows, width = out.shape
    unit = terms[2:3, :1]
    unit = jnp.where(unit > 0, unit, 1.0)
    count = width // LANES
    for k in range(count):
        at = slice(k * rows, (k + 1) * rows)
        lanes = slice(k * LANES, (k + 1) * LANES)
        out[:, lanes] = keep[:, lanes] + unit * sum(decode(p[at, :]) for p in pays)
    tail = sum(p[count * rows :, :].astype(F32) for p in pays)
    full = total[...] + side[...] + jnp.sum(tail, axis=0, keepdims=True)
    loss[0, 0] = jnp.max(full) / (2.0 * pairs)


def shards(image_embed, text_embed, pair_index):
    rows, width = image_embed.shape
    n_xl, n_z, n_c, n_y, n_xh = (lax.axis_size(a) for a in ("xl", "z", "c", "y", "xh"))
    n_plane = n_xl * n_y * n_xh
    size = n_plane * rows
    half = n_z * rows
    pairs = size * n_z * n_c
    inv_root = width ** (-0.5)
    core = lax.axis_index("c")
    shape = jax.ShapeDtypeStruct
    tall = width // LANES * rows + EXTRA

    pair_other = lax.ppermute(pair_index, "xl", SWAP)
    first = lax.axis_index("xl") == 0
    pair = jnp.concatenate(
        [jnp.where(first, pair_index, pair_other), jnp.where(first, pair_other, pair_index)]
    )
    pair = pair.astype(F32)[None, :]
    block = (lax.axis_index("y") * n_xh + lax.axis_index("xh")) * n_xl + lax.axis_index("xl")
    slot = lax.broadcasted_iota(jnp.int32, (1, size), 1)
    own = slot < half
    within = jnp.where(own, slot, slot - half)
    ids = ((block * n_z + within // rows) * n_c + jnp.where(own, core, 1 - core)) * rows
    ids = (ids + within % rows).astype(F32)

    image = lax.all_to_all(
        jnp.broadcast_to(image_embed[None], (n_plane, rows, width)), PLANE, 0, 0
    ).reshape(size, width)
    pieces = [text_embed] + [turn(text_embed, "z", -q) for q in range(1, n_z)]
    pieces = pieces + [lax.ppermute(piece, "c", SWAP) for piece in pieces]

    flops = 2 * size * size * width
    scores, text, row_sent = call(
        functools.partial(score_body, n_z, inv_root),
        (
            shape((size, size), F32),
            shape((size, width), BF16),
            shape((n_plane, 1, size + 2 * LANES), F32),
        ),
        (*pieces, image, pair, ids),
        "scores",
        flops,
        size * size,
    )
    row_got = lax.all_to_all(row_sent, PLANE, 0, 0).reshape(n_plane, size + 2 * LANES)
    (col_sent,) = call(
        column_body, (shape((1, size + LANES), F32),), (scores, image), "columns", 0, size * size
    )
    (col_pair,) = call(
        pair_body,
        (shape((1, size + LANES), F32),),
        (col_sent, lax.ppermute(col_sent, "c", SWAP)),
        "pair",
    )
    cols = [col_pair] + [turn(col_pair, "z", q) for q in range(1, n_z)]

    grads, image_sent, terms = call(
        functools.partial(image_body, n_z, inv_root),
        (
            shape((size, size), BF16),
            shape((n_plane, tall, LANES), BF16),
            shape((8, LANES), F32),
        ),
        (*cols, scores, text, row_got, pair, ids),
        "image_grad",
        flops,
        2 * size * size,
    )
    image_got = lax.all_to_all(image_sent, PLANE, 0, 0)
    text_own, text_other = call(
        functools.partial(text_body, inv_root),
        (shape((half, width), F32), shape((half, width), F32)),
        (grads, image),
        "text_grad",
        flops,
    )
    keep, total, *pays = call(
        functools.partial(send_body, n_z),
        (shape((rows, width), F32), shape((1, LANES), F32))
        + (shape((tall, LANES), BF16),) * (n_z - 1),
        (text_own, lax.ppermute(text_other, "c", SWAP), terms, lax.ppermute(terms, "c", SWAP)),
        "send",
    )
    pays = [turn(pay, "z", q + 1) for q, pay in enumerate(pays)]
    grad_image, side = call(
        image_sum_body,
        (shape((rows, width), F32), shape((1, LANES), F32)),
        (image_got, terms),
        "image_sum",
    )
    grad_text, loss = call(
        functools.partial(text_sum_body, pairs),
        (shape((rows, width), F32), shape((1, 1), F32)),
        (keep, total, terms, side, *pays),
        "text_sum",
        smem_out=1,
    )
    return (loss[0, 0], grad_image, grad_text)


def solution(mesh):
    fine = Mesh(mesh.devices.reshape(2, 8, 2, 4, 2), ("xl", "z", "c", "y", "xh"))
    image_spec = P(("xl", "z", "c", "y", "xh"), None)
    text_spec = P(("y", "xh", "xl", "z", "c"), None)
    return jax.shard_map(
        shards,
        mesh=fine,
        in_specs=(image_spec, text_spec, P(("xl", "z", "c"))),
        out_specs=(P(), image_spec, text_spec),
        check_vma=False,
    )
```

```python
import functools

import jax
import jax.numpy as jnp
from jax import lax
from jax.experimental import pallas as pl
from jax.experimental.pallas import tpu as pltpu
from jax.sharding import Mesh, PartitionSpec as P

PLANE = ("xl", "y", "xh")
SWAP = [(0, 1), (1, 0)]
LANES = 128
EXTRA = 16
F32 = jnp.float32
BF16 = jnp.bfloat16


def turn(x, axis, step):
    count = lax.axis_size(axis)
    return lax.ppermute(x, axis, [(i, (i + step) % count) for i in range(count)])


def merge(parts):
    high = functools.reduce(jnp.maximum, parts)
    return high + jnp.log(sum(jnp.exp(p - high) for p in parts))


def encode(scaled):
    square = scaled * scaled
    fourth = square * square
    return jnp.where(scaled < 0, -fourth, fourth).astype(BF16)


def decode(x):
    wide = x.astype(F32)
    half = lax.rsqrt(jnp.maximum(jnp.abs(wide), 1e-37))
    return wide * half * (half * lax.rsqrt(half))


def split3(value):
    high = value.astype(BF16).astype(F32)
    mid = (value - high).astype(BF16).astype(F32)
    low = value - high - mid
    row = lax.broadcasted_iota(jnp.int32, (EXTRA, LANES), 0)
    parts = jnp.where(row == 0, high, jnp.where(row == 1, mid, jnp.where(row == 2, low, 0.0)))
    return parts.astype(BF16)


def inverse(value):
    return jnp.where(value > 0, 1.0 / value, 1.0)


def to_column(row):
    return jnp.transpose(jnp.broadcast_to(row, (LANES, row.shape[1])))[:, :1]


def to_row(column):
    return jnp.transpose(jnp.broadcast_to(column, (column.shape[0], LANES)))[:1, :]


def call(body, outs, args, name, flops=0, exps=0, smem_out=None, size=None):
    if size is None:
        size = sum(a.size * a.dtype.itemsize for a in (*args, *outs))
    spaces = [pltpu.SMEM if i == smem_out else pltpu.VMEM for i in range(len(outs))]
    return pl.pallas_call(
        body,
        out_shape=outs,
        in_specs=[pl.BlockSpec(memory_space=pltpu.VMEM)] * len(args),
        out_specs=tuple(pl.BlockSpec(memory_space=s) for s in spaces),
        cost_estimate=pl.CostEstimate(flops=flops, bytes_accessed=size, transcendentals=exps),
        compiler_params=pltpu.CompilerParams(vmem_limit_bytes=20 * 1024 * 1024),
        name=name,
    )(*args)


def score_body(n_z, inv_root, *refs):
    pieces, (image, scores, text, sent) = refs[: 2 * n_z], refs[2 * n_z :]
    rows = pieces[0].shape[0]
    size = image.shape[0]
    z = lax.axis_index("z")
    high = jnp.zeros(pieces[0].shape, F32)
    for h in range(2):
        for q in range(n_z):
            piece = pieces[h * n_z + q][...]
            start = h * n_z * rows + lax.rem(z + q, n_z) * rows
            text[pl.ds(pl.multiple_of(start, 16), rows), :] = piece
            high = jnp.maximum(high, jnp.abs(piece.astype(F32)))
    step = 256
    for r in range(0, size, step):
        tile = (
            lax.dot_general(
                image[r : r + step, :],
                text[...],
                (((1,), (1,)), ((), ())),
                preferred_element_type=F32,
            )
            * inv_root
        )
        scores[r : r + step, :] = tile
        top = jnp.max(tile, axis=1, keepdims=True)
        part = top + jnp.log(jnp.sum(jnp.exp(tile - top), axis=1, keepdims=True))
        sent[:, 0, r : r + step] = jnp.broadcast_to(to_row(part), (sent.shape[0], step))
    sent[:, 0, size:] = jnp.full((sent.shape[0], LANES), jnp.max(high))


def column_body(scores, image, pair, ids, sent):
    size = scores.shape[1]
    tile = scores[...]
    top = jnp.max(tile, axis=0, keepdims=True)
    part = top + jnp.log(jnp.sum(jnp.exp(tile - top), axis=0, keepdims=True))
    sent[:, :size] = part
    high = jnp.max(jnp.abs(image[...].astype(F32)))
    sent[:, size : size + LANES] = jnp.full((1, LANES), high)
    hit = to_column(pair[...]) == ids[...]
    found = jnp.sum(jnp.where(hit, tile, 0.0), axis=0, keepdims=True)
    sent[:, size + LANES :] = jnp.full((1, LANES), jnp.sum(found))


def pair_body(crossed, mine, seen, out):
    size = mine.shape[1] - 2 * LANES
    half = size // 2
    other = seen[:, :size]
    if crossed:
        other = jnp.concatenate([seen[:, half:size], seen[:, :half]], axis=1)
    out[:, :size] = merge([mine[:, :size], other])
    at = slice(size, size + LANES)
    out[:, at] = jnp.maximum(mine[:, at], seen[:, at])
    at = slice(size + LANES, size + 2 * LANES)
    out[:, at] = mine[:, at] + seen[:, at]


def image_body(inv_root, cols, scores, text, row_got, pair, ids, grads, sent, terms):
    size = scores.shape[0]
    n_plane = sent.shape[0]
    rows = size // n_plane
    col_lse = cols[:, :size]
    image_max = cols[:, size : size + LANES]
    found = cols[:, size + LANES :]
    row_lse = merge([row_got[i : i + 1, :size] for i in range(n_plane)])
    text_max = jnp.max(row_got[:, size:], axis=0, keepdims=True)
    row_terms = jnp.broadcast_to(jnp.sum(row_lse, axis=1, keepdims=True), (1, LANES))
    col_terms = jnp.sum(col_lse, axis=1, keepdims=True) - 2.0 * found
    terms[...] = jnp.concatenate(
        [row_terms, text_max, image_max, jnp.zeros((5, LANES), F32)], axis=0
    )
    extra = split3(col_terms)
    scale = inverse(text_max[:, :1]) * inv_root
    step = 384
    for r in range(0, size, step):
        tile = scores[r : r + step, :]
        probs = 0.5 * (
            jnp.exp(tile - to_column(row_lse[:, r : r + step])) + jnp.exp(tile - col_lse)
        )
        hit = to_column(pair[:, r : r + step]) == ids[...]
        grad = (probs - jnp.where(hit, 1.0, 0.0)).astype(BF16)
        grads[r : r + step, :] = grad
        part = encode(jnp.dot(grad, text[...], preferred_element_type=F32) * scale)
        for p in range(step // rows):
            to = r // rows + p
            for k in range(text.shape[1] // LANES):
                sent[to, k * rows : (k + 1) * rows, :] = part[
                    p * rows : (p + 1) * rows, k * LANES : (k + 1) * LANES
                ]
            sent[to, k * rows + rows :, :] = extra


def text_body(inv_root, grads, image, own, other):
    half = own.shape[0]
    for out, start in ((other, half), (own, 0)):
        out[...] = (
            lax.dot_general(
                grads[:, start : start + half],
                image[...],
                (((0,), (0,)), ((), ())),
                preferred_element_type=F32,
            )
            * inv_root
        )


def send_body(n_z, own, seen, terms, terms_seen, keep, total, *pays):
    rows = keep.shape[0]
    z = lax.axis_index("z")
    row_terms = terms[0:1, :] + terms_seen[0:1, :]
    total[...] = row_terms
    extra = split3(row_terms)
    scale = inverse(terms[2:3, :1])
    for q in range(n_z):
        at = pl.ds(pl.multiple_of(lax.rem(z + q, n_z) * rows, 16), rows)
        block = own[at, :] + seen[at, :]
        if q == 0:
            keep[...] = block
            continue
        pay = pays[q - 1]
        part = encode(block * scale)
        count = block.shape[1] // LANES
        for k in range(count):
            pay[k * rows : (k + 1) * rows, :] = part[:, k * LANES : (k + 1) * LANES]
        pay[count * rows :, :] = extra


def text_sum_body(keep, total, terms, *refs):
    pays, out, side = refs[:-2], refs[-2], refs[-1]
    rows, width = out.shape
    unit = terms[2:3, :1]
    unit = jnp.where(unit > 0, unit, 1.0)
    count = width // LANES
    for k in range(count):
        at = slice(k * rows, (k + 1) * rows)
        lanes = slice(k * LANES, (k + 1) * LANES)
        out[:, lanes] = keep[:, lanes] + unit * sum(decode(p[at, :]) for p in pays)
    tail = sum(p[count * rows :, :].astype(F32) for p in pays)
    side[...] = total[...] + jnp.sum(tail, axis=0, keepdims=True)


def image_sum_body(pairs, got, terms, side, out, loss):
    rows, width = out.shape
    unit = terms[1:2, :1]
    unit = jnp.where(unit > 0, unit, 1.0)
    count = width // LANES
    for k in range(count):
        at = slice(k * rows, (k + 1) * rows)
        out[:, k * LANES : (k + 1) * LANES] = unit * sum(
            decode(got[p, at, :]) for p in range(got.shape[0])
        )
    tail = sum(got[p, count * rows :, :].astype(F32) for p in range(got.shape[0]))
    full = side[...] + jnp.sum(tail, axis=0, keepdims=True)
    loss[0, 0] = jnp.max(full) / (2.0 * pairs)


def shards(image_embed, text_embed, pair_index):
    rows, width = image_embed.shape
    n_xl, n_z, n_c, n_y, n_xh = (lax.axis_size(a) for a in ("xl", "z", "c", "y", "xh"))
    n_plane = n_xl * n_y * n_xh
    size = n_plane * rows
    half = n_z * rows
    pairs = size * n_z * n_c
    inv_root = width ** (-0.5)
    core = lax.axis_index("c")
    shape = jax.ShapeDtypeStruct
    tall = width // LANES * rows + EXTRA

    block = (lax.axis_index("y") * n_xh + lax.axis_index("xh")) * n_xl + lax.axis_index("xl")
    slot = lax.broadcasted_iota(jnp.int32, (1, size), 1)
    own = slot < half
    within = jnp.where(own, slot, slot - half)
    ids = ((block * n_z + within // rows) * n_c + jnp.where(own, core, 1 - core)) * rows
    ids = (ids + within % rows).astype(F32)

    image = lax.all_to_all(
        jnp.broadcast_to(image_embed[None], (n_plane, rows, width)), PLANE, 0, 0
    ).reshape(size, width)
    image, pair_index = lax.optimization_barrier((image, pair_index))
    pair_other = lax.ppermute(pair_index, "xl", SWAP)
    first = lax.axis_index("xl") == 0
    pair = jnp.concatenate(
        [jnp.where(first, pair_index, pair_other), jnp.where(first, pair_other, pair_index)]
    )
    pair = pair.astype(F32)[None, :]
    pieces = [text_embed] + [turn(text_embed, "z", -q) for q in range(1, n_z)]
    pieces = pieces + [lax.ppermute(piece, "c", SWAP) for piece in pieces]

    flops = 2 * size * size * width
    scores, text, row_sent = call(
        functools.partial(score_body, n_z, inv_root),
        (
            shape((size, size), F32),
            shape((size, width), BF16),
            shape((n_plane, 1, size + LANES), F32),
        ),
        (*pieces, image),
        "scores",
        flops,
        size * size,
    )
    row_got = lax.all_to_all(row_sent, PLANE, 0, 0).reshape(n_plane, size + LANES)
    cols_shape = (shape((1, size + 2 * LANES), F32),)
    (cols,) = call(
        column_body, cols_shape, (scores, image, pair, ids), "columns", 0, size * size
    )
    seen = lax.ppermute(cols, "c", SWAP)
    (cols,) = call(functools.partial(pair_body, True), cols_shape, (cols, seen), "pair")
    step = 1
    while step < n_z:
        seen = lax.ppermute(cols, "z", [(i, i ^ step) for i in range(n_z)])
        (cols,) = call(functools.partial(pair_body, False), cols_shape, (cols, seen), "pair")
        step *= 2

    grads, image_sent, terms = call(
        functools.partial(image_body, inv_root),
        (
            shape((size, size), BF16),
            shape((n_plane, tall, LANES), BF16),
            shape((8, LANES), F32),
        ),
        (cols, scores, text, row_got, pair, ids),
        "image_grad",
        flops,
        2 * size * size,
    )
    image_got = lax.all_to_all(image_sent, PLANE, 0, 0)
    text_own, text_other = call(
        functools.partial(text_body, inv_root),
        (shape((half, width), F32), shape((half, width), F32)),
        (grads, image),
        "text_grad",
        size=1,
    )
    keep, total, *pays = call(
        functools.partial(send_body, n_z),
        (shape((rows, width), F32), shape((1, LANES), F32))
        + (shape((tall, LANES), BF16),) * (n_z - 1),
        (text_own, lax.ppermute(text_other, "c", SWAP), terms, lax.ppermute(terms, "c", SWAP)),
        "send",
        size=1,
    )
    pays = [turn(pay, "z", q + 1) for q, pay in enumerate(pays)]
    grad_text, side = call(
        text_sum_body,
        (shape((rows, width), F32), shape((1, LANES), F32)),
        (keep, total, terms, *pays),
        "text_sum",
    )
    grad_image, loss = call(
        functools.partial(image_sum_body, pairs),
        (shape((rows, width), F32), shape((1, 1), F32)),
        (image_got, terms, side),
        "image_sum",
        smem_out=1,
    )
    return (loss[0, 0], grad_image, grad_text)


def solution(mesh):
    fine = Mesh(mesh.devices.reshape(2, 8, 2, 4, 2), ("xl", "z", "c", "y", "xh"))
    image_spec = P(("xl", "z", "c", "y", "xh"), None)
    text_spec = P(("y", "xh", "xl", "z", "c"), None)
    return jax.shard_map(
        shards,
        mesh=fine,
        in_specs=(image_spec, text_spec, P(("xl", "z", "c"))),
        out_specs=(P(), image_spec, text_spec),
        check_vma=False,
    )
```

```python
import functools

import jax
import jax.numpy as jnp
from jax import lax
from jax.experimental import pallas as pl
from jax.experimental.pallas import tpu as pltpu
from jax.sharding import Mesh, PartitionSpec as P

PLANE = ("xl", "y", "xh")
SWAP = [(0, 1), (1, 0)]
LANES = 128
EXTRA = 16
F32 = jnp.float32
BF16 = jnp.bfloat16


def turn(x, axis, step):
    count = lax.axis_size(axis)
    return lax.ppermute(x, axis, [(i, (i + step) % count) for i in range(count)])


def merge(parts):
    high = functools.reduce(jnp.maximum, parts)
    return high + jnp.log(sum(jnp.exp(p - high) for p in parts))


def encode(scaled):
    square = scaled * scaled
    fourth = square * square
    return jnp.where(scaled < 0, -fourth, fourth).astype(BF16)


def decode(x):
    wide = x.astype(F32)
    half = lax.rsqrt(jnp.maximum(jnp.abs(wide), 1e-37))
    return wide * half * (half * lax.rsqrt(half))


def split3(value):
    high = value.astype(BF16).astype(F32)
    mid = (value - high).astype(BF16).astype(F32)
    low = value - high - mid
    row = lax.broadcasted_iota(jnp.int32, (EXTRA, LANES), 0)
    parts = jnp.where(row == 0, high, jnp.where(row == 1, mid, jnp.where(row == 2, low, 0.0)))
    return parts.astype(BF16)


def inverse(value):
    return jnp.where(value > 0, 1.0 / value, 1.0)


def to_column(row):
    return jnp.transpose(jnp.broadcast_to(row, (LANES, row.shape[1])))[:, :1]


def to_row(column):
    return jnp.transpose(jnp.broadcast_to(column, (column.shape[0], LANES)))[:1, :]


def call(body, outs, args, name, flops=0, exps=0, smem_out=None, size=None):
    if size is None:
        size = sum(a.size * a.dtype.itemsize for a in (*args, *outs))
    spaces = [pltpu.SMEM if i == smem_out else pltpu.VMEM for i in range(len(outs))]
    return pl.pallas_call(
        body,
        out_shape=outs,
        in_specs=[pl.BlockSpec(memory_space=pltpu.VMEM)] * len(args),
        out_specs=tuple(pl.BlockSpec(memory_space=s) for s in spaces),
        cost_estimate=pl.CostEstimate(flops=flops, bytes_accessed=size, transcendentals=exps),
        compiler_params=pltpu.CompilerParams(vmem_limit_bytes=20 * 1024 * 1024),
        name=name,
    )(*args)


def score_body(order, inv_root, *refs):
    n_z = len(order) + 1
    steps = [0, *order[::-1]]
    pieces, refs = refs[: 2 * n_z], refs[2 * n_z :]
    image, pair_mine, pair_seen, scores, text, row_sent, col_sent = refs
    rows = pieces[0].shape[0]
    size = image.shape[0]
    pair, ids = labels(pair_mine, pair_seen, n_z, rows)
    found = jnp.zeros((1, size), F32)
    z = lax.axis_index("z")
    high = jnp.zeros(pieces[0].shape, F32)
    for h in range(2):
        for i, q in enumerate(steps):
            piece = pieces[h * n_z + i][...]
            start = h * n_z * rows + lax.rem(z + q, n_z) * rows
            text[pl.ds(pl.multiple_of(start, 16), rows), :] = piece
            high = jnp.maximum(high, jnp.abs(piece.astype(F32)))
    step = 256
    for r in range(0, size, step):
        tile = (
            lax.dot_general(
                image[r : r + step, :],
                text[...],
                (((1,), (1,)), ((), ())),
                preferred_element_type=F32,
            )
            * inv_root
        )
        scores[r : r + step, :] = tile
        top = jnp.max(tile, axis=1, keepdims=True)
        part = top + jnp.log(jnp.sum(jnp.exp(tile - top), axis=1, keepdims=True))
        row_sent[:, r : r + step] = to_row(part)
        hit = to_column(pair[:, r : r + step]) == ids
        found += jnp.sum(jnp.where(hit, tile, 0.0), axis=0, keepdims=True)
    row_sent[:, size:] = jnp.full((1, LANES), jnp.max(high))
    tile = scores[...]
    top = jnp.max(tile, axis=0, keepdims=True)
    col_sent[:, :size] = top + jnp.log(jnp.sum(jnp.exp(tile - top), axis=0, keepdims=True))
    high = jnp.max(jnp.abs(image[...].astype(F32)))
    col_sent[:, size : size + LANES] = jnp.full((1, LANES), high)
    col_sent[:, size + LANES :] = jnp.full((1, LANES), jnp.sum(found))


def labels(mine, seen, n_z, rows):
    half = n_z * rows
    first = lax.axis_index("xl") == 0
    mine, seen = mine[...].astype(F32), seen[...].astype(F32)
    pair = jnp.concatenate([jnp.where(first, mine, seen), jnp.where(first, seen, mine)], axis=1)
    n_xl, n_c, n_xh = (lax.axis_size(a) for a in ("xl", "c", "xh"))
    block = (lax.axis_index("y") * n_xh + lax.axis_index("xh")) * n_xl + lax.axis_index("xl")
    core = lax.axis_index("c")
    slot = lax.broadcasted_iota(jnp.int32, (1, 2 * half), 1)
    own = slot < half
    within = jnp.where(own, slot, slot - half)
    holder = jnp.floor((within.astype(F32) + 0.5) * (1.0 / rows)).astype(jnp.int32)
    ids = ((block * n_z + holder) * n_c + jnp.where(own, core, 1 - core)) * rows
    return pair, (ids + within - holder * rows).astype(F32)


def pair_body(crossed, count, mine, seen, out):
    half = count // 2
    other = seen[:, :count]
    if crossed:
        other = jnp.concatenate([seen[:, half:count], seen[:, :half]], axis=1)
    out[:, :count] = merge([mine[:, :count], other])
    at = slice(count, count + LANES)
    out[:, at] = jnp.maximum(mine[:, at], seen[:, at])
    if mine.shape[1] > count + LANES:
        at = slice(count + LANES, count + 2 * LANES)
        out[:, at] = mine[:, at] + seen[:, at]


def image_body(
    n_z, inv_root, cols, rows_lse, scores, text, pair_mine, pair_seen, grads, sent, terms
):
    size = scores.shape[0]
    n_plane = sent.shape[0]
    rows = size // n_plane
    col_lse = cols[:, :size]
    image_max = cols[:, size : size + LANES]
    found = cols[:, size + LANES :]
    pair, ids = labels(pair_mine, pair_seen, n_z, rows)
    row_lse = rows_lse[:, :size]
    text_max = rows_lse[:, size:]
    row_terms = jnp.broadcast_to(jnp.sum(row_lse, axis=1, keepdims=True), (1, LANES))
    col_terms = jnp.sum(col_lse, axis=1, keepdims=True) - 2.0 * found
    terms[...] = jnp.concatenate(
        [row_terms, text_max, image_max, jnp.zeros((5, LANES), F32)], axis=0
    )
    extra = split3(col_terms)
    scale = inverse(text_max[:, :1]) * inv_root
    step = 384
    for r in range(0, size, step):
        tile = scores[r : r + step, :]
        probs = 0.5 * (
            jnp.exp(tile - to_column(row_lse[:, r : r + step])) + jnp.exp(tile - col_lse)
        )
        hit = to_column(pair[:, r : r + step]) == ids
        grad = (probs - jnp.where(hit, 1.0, 0.0)).astype(BF16)
        grads[r : r + step, :] = grad
        part = encode(jnp.dot(grad, text[...], preferred_element_type=F32) * scale)
        for p in range(step // rows):
            to = r // rows + p
            for k in range(text.shape[1] // LANES):
                sent[to, k * rows : (k + 1) * rows, :] = part[
                    p * rows : (p + 1) * rows, k * LANES : (k + 1) * LANES
                ]
            sent[to, k * rows + rows :, :] = extra


def text_body(inv_root, grads, image, own, other):
    half = own.shape[0]
    for out, start in ((other, half), (own, 0)):
        out[...] = (
            lax.dot_general(
                grads[:, start : start + half],
                image[...],
                (((0,), (0,)), ((), ())),
                preferred_element_type=F32,
            )
            * inv_root
        )


def send_body(order, own, seen, terms, terms_seen, keep, total, *pays):
    rows = keep.shape[0]
    z = lax.axis_index("z")
    row_terms = terms[0:1, :] + terms_seen[0:1, :]
    total[...] = row_terms
    extra = split3(row_terms)
    scale = inverse(terms[2:3, :1])
    n_z = len(order) + 1
    for i, q in enumerate([0, *order]):
        at = pl.ds(pl.multiple_of(lax.rem(z + q, n_z) * rows, 16), rows)
        block = own[at, :] + seen[at, :]
        if q == 0:
            keep[...] = block
            continue
        pay = pays[i - 1]
        part = encode(block * scale)
        count = block.shape[1] // LANES
        for k in range(count):
            pay[k * rows : (k + 1) * rows, :] = part[:, k * LANES : (k + 1) * LANES]
        pay[count * rows :, :] = extra


def text_sum_body(keep, total, terms, *refs):
    pays, out, side = refs[:-2], refs[-2], refs[-1]
    rows, width = out.shape
    unit = terms[2:3, :1]
    unit = jnp.where(unit > 0, unit, 1.0)
    count = width // LANES
    for k in range(count):
        at = slice(k * rows, (k + 1) * rows)
        lanes = slice(k * LANES, (k + 1) * LANES)
        out[:, lanes] = keep[:, lanes] + unit * sum(decode(p[at, :]) for p in pays)
    tail = sum(p[count * rows :, :].astype(F32) for p in pays)
    side[...] = total[...] + jnp.sum(tail, axis=0, keepdims=True)


def image_sum_body(pairs, got, terms, side, out, loss):
    rows, width = out.shape
    unit = terms[1:2, :1]
    unit = jnp.where(unit > 0, unit, 1.0)
    count = width // LANES
    for k in range(count):
        at = slice(k * rows, (k + 1) * rows)
        out[:, k * LANES : (k + 1) * LANES] = unit * sum(
            decode(got[p, at, :]) for p in range(got.shape[0])
        )
    tail = sum(got[p, count * rows :, :].astype(F32) for p in range(got.shape[0]))
    full = side[...] + jnp.sum(tail, axis=0, keepdims=True)
    loss[0, 0] = jnp.max(full) / (2.0 * pairs)


def shards(image_embed, text_embed, pair_index):
    rows, width = image_embed.shape
    n_xl, n_z, n_c, n_y, n_xh = (lax.axis_size(a) for a in ("xl", "z", "c", "y", "xh"))
    n_plane = n_xl * n_y * n_xh
    size = n_plane * rows
    half = n_z * rows
    pairs = size * n_z * n_c
    inv_root = width ** (-0.5)
    shape = jax.ShapeDtypeStruct
    tall = width // LANES * rows + EXTRA

    pair_mine = pair_index[None, :]
    pair_seen = lax.ppermute(pair_mine, "xl", SWAP)
    copies = jnp.broadcast_to(image_embed[None], (n_plane, rows, width))
    copies, pair_seen = lax.optimization_barrier((copies, pair_seen))
    image = lax.all_to_all(copies, PLANE, 0, 0).reshape(size, width)

    order = sorted(range(1, n_z), key=lambda q: (abs(q - n_z // 2), q))
    pieces = [text_embed] + [turn(text_embed, "z", -q) for q in order[::-1]]
    pieces = pieces + [lax.ppermute(piece, "c", SWAP) for piece in pieces]

    flops = 2 * size * size * width
    scores, text, row_part, col_part = call(
        functools.partial(score_body, order, inv_root),
        (
            shape((size, size), F32),
            shape((size, width), BF16),
            shape((1, size + LANES), F32),
            shape((1, size + 2 * LANES), F32),
        ),
        (*pieces, image, pair_mine, pair_seen),
        "scores",
        flops,
        2 * size * size,
    )
    def exchange(part, axis, step):
        count = lax.axis_size(axis)
        seen = lax.ppermute(part, axis, [(i, i ^ step) for i in range(count)])
        merge_body = functools.partial(pair_body, axis == "c", size)
        return call(merge_body, (shape(part.shape, F32),), (part, seen), "pair")[0]

    for axis, step in (("c", 1), ("z", 1), ("z", 2), ("z", 4)):
        col_part = exchange(col_part, axis, step)
    for axis, step in (("xl", 1), ("xh", 1), ("y", 1), ("y", 2)):
        row_part = exchange(row_part, axis, step)

    grads, image_sent, terms = call(
        functools.partial(image_body, n_z, inv_root),
        (
            shape((size, size), BF16),
            shape((n_plane, tall, LANES), BF16),
            shape((8, LANES), F32),
        ),
        (col_part, row_part, scores, text, pair_mine, pair_seen),
        "image_grad",
        flops,
        2 * size * size,
    )
    image_got = lax.all_to_all(image_sent, PLANE, 0, 0)
    text_own, text_other = call(
        functools.partial(text_body, inv_root),
        (shape((half, width), F32), shape((half, width), F32)),
        (grads, image),
        "text_grad",
        size=1,
    )
    keep, total, *pays = call(
        functools.partial(send_body, order),
        (shape((rows, width), F32), shape((1, LANES), F32))
        + (shape((tall, LANES), BF16),) * (n_z - 1),
        (text_own, lax.ppermute(text_other, "c", SWAP), terms, lax.ppermute(terms, "c", SWAP)),
        "send",
        size=1,
    )
    pays = [turn(pay, "z", q) for q, pay in zip(order, pays)]
    grad_text, side = call(
        text_sum_body,
        (shape((rows, width), F32), shape((1, LANES), F32)),
        (keep, total, terms, *pays),
        "text_sum",
    )
    grad_image, loss = call(
        functools.partial(image_sum_body, pairs),
        (shape((rows, width), F32), shape((1, 1), F32)),
        (image_got, terms, side),
        "image_sum",
        smem_out=1,
    )
    return (loss[0, 0], grad_image, grad_text)


def solution(mesh):
    fine = Mesh(mesh.devices.reshape(2, 8, 2, 4, 2), ("xl", "z", "c", "y", "xh"))
    image_spec = P(("xl", "z", "c", "y", "xh"), None)
    text_spec = P(("y", "xh", "xl", "z", "c"), None)
    return jax.shard_map(
        shards,
        mesh=fine,
        in_specs=(image_spec, text_spec, P(("xl", "z", "c"))),
        out_specs=(P(), image_spec, text_spec),
        check_vma=False,
    )
```

```python
import functools

import jax
import jax.numpy as jnp
from jax import lax
from jax.experimental import pallas as pl
from jax.experimental.pallas import tpu as pltpu
from jax.sharding import Mesh, PartitionSpec as P

PLANE = ("xl", "y", "xh")
SWAP = [(0, 1), (1, 0)]
LANES = 128
EXTRA = 16
F32 = jnp.float32
BF16 = jnp.bfloat16


def turn(x, axis, step):
    count = lax.axis_size(axis)
    return lax.ppermute(x, axis, [(i, (i + step) % count) for i in range(count)])


def merge(parts):
    high = functools.reduce(jnp.maximum, parts)
    return high + jnp.log(sum(jnp.exp(p - high) for p in parts))


def encode(scaled):
    square = scaled * scaled
    fourth = square * square
    return jnp.where(scaled < 0, -fourth, fourth).astype(BF16)


def decode(x):
    wide = x.astype(F32)
    half = lax.rsqrt(jnp.maximum(jnp.abs(wide), 1e-37))
    return wide * half * (half * lax.rsqrt(half))


def split3(value):
    high = value.astype(BF16).astype(F32)
    mid = (value - high).astype(BF16).astype(F32)
    low = value - high - mid
    row = lax.broadcasted_iota(jnp.int32, (EXTRA, LANES), 0)
    parts = jnp.where(row == 0, high, jnp.where(row == 1, mid, jnp.where(row == 2, low, 0.0)))
    return parts.astype(BF16)


def inverse(value):
    return jnp.where(value > 0, 1.0 / value, 1.0)


def to_column(row):
    return jnp.transpose(jnp.broadcast_to(row, (LANES, row.shape[1])))[:, :1]


def to_row(column):
    return jnp.transpose(jnp.broadcast_to(column, (column.shape[0], LANES)))[:1, :]


def call(body, outs, args, name, flops=0, exps=0, smem_out=None, size=None):
    if size is None:
        size = sum(a.size * a.dtype.itemsize for a in (*args, *outs))
    spaces = [pltpu.SMEM if i == smem_out else pltpu.VMEM for i in range(len(outs))]
    return pl.pallas_call(
        body,
        out_shape=outs,
        in_specs=[pl.BlockSpec(memory_space=pltpu.VMEM)] * len(args),
        out_specs=tuple(pl.BlockSpec(memory_space=s) for s in spaces),
        cost_estimate=pl.CostEstimate(flops=flops, bytes_accessed=size, transcendentals=exps),
        compiler_params=pltpu.CompilerParams(vmem_limit_bytes=20 * 1024 * 1024),
        name=name,
    )(*args)


def copies_body(source, out, sems):
    copies = [
        pltpu.make_async_copy(source, out.at[i], sems.at[i]) for i in range(out.shape[0])
    ]
    for copy in copies:
        copy.start()
    for copy in copies:
        copy.wait()


def join_body(near, far, mine, seen, out, pair):
    first = lax.axis_index("xl") == 0
    left = mine[...].astype(F32)[None, :]
    right = seen[...].astype(F32)[None, :]
    pair[...] = jnp.concatenate(
        [jnp.where(first, left, right), jnp.where(first, right, left)], axis=1
    )
    rows = near.shape[0]
    out[:rows, :] = near[...]
    out[rows:, :] = far[...]


def score_body(steps, inv_root, *refs):
    n_z = 2 * len(steps)
    pieces, refs = refs[:n_z], refs[n_z:]
    image, pair, scores, text, row_sent, col_sent = refs
    rows = pieces[0].shape[0] // 2
    size = image.shape[0]
    ids = labels(n_z, rows)
    found = jnp.zeros((1, size), F32)
    z = lax.axis_index("z")
    high = jnp.zeros(pieces[0].shape, F32)
    for h in range(2):
        for i, q in enumerate(steps):
            piece = pieces[h * n_z // 2 + i]
            high = jnp.maximum(high, jnp.abs(piece[...].astype(F32)))
            for k in range(2):
                start = (h * n_z + lax.rem(z + q + (k + 2) * n_z // 2, n_z)) * rows
                text[pl.ds(pl.multiple_of(start, 16), rows), :] = piece[
                    k * rows : (k + 1) * rows, :
                ]
    step = 256
    for r in range(0, size, step):
        tile = (
            lax.dot_general(
                image[r : r + step, :],
                text[...],
                (((1,), (1,)), ((), ())),
                preferred_element_type=F32,
            )
            * inv_root
        )
        scores[r : r + step, :] = tile
        top = jnp.max(tile, axis=1, keepdims=True)
        part = top + jnp.log(jnp.sum(jnp.exp(tile - top), axis=1, keepdims=True))
        row_sent[:, r : r + step] = to_row(part)
        hit = to_column(pair[:, r : r + step]) == ids
        found += jnp.sum(jnp.where(hit, tile, 0.0), axis=0, keepdims=True)
    row_sent[:, size:] = jnp.full((1, LANES), jnp.max(high))
    tile = scores[...]
    top = jnp.max(tile, axis=0, keepdims=True)
    col_sent[:, :size] = top + jnp.log(jnp.sum(jnp.exp(tile - top), axis=0, keepdims=True))
    high = jnp.max(jnp.abs(image[...].astype(F32)))
    col_sent[:, size : size + LANES] = jnp.full((1, LANES), high)
    col_sent[:, size + LANES :] = jnp.full((1, LANES), jnp.sum(found))


def labels(n_z, rows):
    half = n_z * rows
    n_xl, n_c, n_xh = (lax.axis_size(a) for a in ("xl", "c", "xh"))
    block = (lax.axis_index("y") * n_xh + lax.axis_index("xh")) * n_xl + lax.axis_index("xl")
    core = lax.axis_index("c")
    slot = lax.broadcasted_iota(jnp.int32, (1, 2 * half), 1)
    own = slot < half
    within = jnp.where(own, slot, slot - half)
    holder = jnp.floor((within.astype(F32) + 0.5) * (1.0 / rows)).astype(jnp.int32)
    ids = ((block * n_z + holder) * n_c + jnp.where(own, core, 1 - core)) * rows
    return (ids + within - holder * rows).astype(F32)


def pair_body(crossed, count, mine, seen, out):
    half = count // 2
    other = seen[:, :count]
    if crossed:
        other = jnp.concatenate([seen[:, half:count], seen[:, :half]], axis=1)
    out[:, :count] = merge([mine[:, :count], other])
    at = slice(count, count + LANES)
    out[:, at] = jnp.maximum(mine[:, at], seen[:, at])
    if mine.shape[1] > count + LANES:
        at = slice(count + LANES, count + 2 * LANES)
        out[:, at] = mine[:, at] + seen[:, at]


def image_body(n_z, inv_root, cols, rows_lse, scores, text, pair, grads, sent, terms):
    size = scores.shape[0]
    n_plane = sent.shape[0]
    rows = size // n_plane
    col_lse = cols[:, :size]
    image_max = cols[:, size : size + LANES]
    found = cols[:, size + LANES :]
    ids = labels(n_z, rows)
    row_lse = rows_lse[:, :size]
    text_max = rows_lse[:, size:]
    row_terms = jnp.broadcast_to(jnp.sum(row_lse, axis=1, keepdims=True), (1, LANES))
    col_terms = jnp.sum(col_lse, axis=1, keepdims=True) - 2.0 * found
    terms[...] = jnp.concatenate(
        [row_terms, text_max, image_max, jnp.zeros((5, LANES), F32)], axis=0
    )
    extra = split3(col_terms)
    scale = inverse(text_max[:, :1]) * inv_root
    step = 384
    for r in range(0, size, step):
        tile = scores[r : r + step, :]
        probs = 0.5 * (
            jnp.exp(tile - to_column(row_lse[:, r : r + step])) + jnp.exp(tile - col_lse)
        )
        hit = to_column(pair[:, r : r + step]) == ids
        grad = (probs - jnp.where(hit, 1.0, 0.0)).astype(BF16)
        grads[r : r + step, :] = grad
        part = encode(jnp.dot(grad, text[...], preferred_element_type=F32) * scale)
        for p in range(step // rows):
            to = r // rows + p
            for k in range(text.shape[1] // LANES):
                sent[to, k * rows : (k + 1) * rows, :] = part[
                    p * rows : (p + 1) * rows, k * LANES : (k + 1) * LANES
                ]
            sent[to, k * rows + rows :, :] = extra


def text_body(inv_root, grads, image, own, other):
    half = own.shape[0]
    for out, start in ((other, half), (own, 0)):
        out[...] = (
            lax.dot_general(
                grads[:, start : start + half],
                image[...],
                (((0,), (0,)), ((), ())),
                preferred_element_type=F32,
            )
            * inv_root
        )


def pack(pay, blocks, extra):
    rows, width = blocks[0].shape
    at = 0
    for block in blocks:
        coded = encode(block)
        for k in range(width // LANES):
            pay[at : at + rows, :] = coded[:, k * LANES : (k + 1) * LANES]
            at += rows
    pay[at:, :] = extra


def send_body(steps, own, seen, terms, terms_seen, keep, total, *pays):
    n_z = 2 * len(steps)
    rows = keep.shape[0] // 2
    z = lax.axis_index("z")
    row_terms = terms[0:1, :] + terms_seen[0:1, :]
    total[...] = row_terms
    extra = split3(row_terms)
    scale = inverse(terms[2:3, :1])
    for i, q in enumerate(steps):
        blocks = []
        for k in range(2):
            start = lax.rem(z + q + (k + 2) * n_z // 2, n_z) * rows
            at = pl.ds(pl.multiple_of(start, 16), rows)
            blocks.append((own[at, :] + seen[at, :]) * scale)
        if i == 0:
            keep[:rows, :] = blocks[0]
            keep[rows:, :] = blocks[1]
        else:
            pack(pays[i - 1], blocks, extra)


def unpack(pays, at, rows, width):
    return jnp.concatenate(
        [
            sum(decode(p[at + k * rows : at + (k + 1) * rows, :]) for p in pays)
            for k in range(width // LANES)
        ],
        axis=1,
    )


def tails(pays):
    tail = sum(p[p.shape[0] - EXTRA :, :].astype(F32) for p in pays)
    return jnp.sum(tail, axis=0, keepdims=True)


def relay_body(keep, total, *refs):
    pays, near, far, total_out = refs[:-3], refs[-3], refs[-2], refs[-1]
    rows, width = near.shape
    near[...] = keep[:rows, :] + unpack(pays, 0, rows, width)
    sums = total[...] + tails(pays)
    total_out[...] = sums
    block = keep[rows:, :] + unpack(pays, rows * width // LANES, rows, width)
    pack(far, [block], split3(sums))


def text_sum_body(pairs, near, total, terms, side, pay, out, loss):
    rows, width = out.shape
    unit = terms[2:3, :1]
    unit = jnp.where(unit > 0, unit, 1.0)
    out[...] = unit * (near[...] + unpack([pay], 0, rows, width))
    full = total[...] + side[...] + tails([pay])
    loss[0, 0] = jnp.max(full) / (2.0 * pairs)


def image_sum_body(got, terms, out, side):
    rows, width = out.shape
    unit = terms[1:2, :1]
    unit = jnp.where(unit > 0, unit, 1.0)
    pays = [got.at[p] for p in range(got.shape[0])]
    for k in range(width // LANES):
        at = slice(k * rows, (k + 1) * rows)
        out[:, k * LANES : (k + 1) * LANES] = unit * sum(decode(p[at, :]) for p in pays)
    side[...] = tails(pays)


def shards(image_embed, text_embed, pair_index):
    rows, width = image_embed.shape
    n_xl, n_z, n_c, n_y, n_xh = (lax.axis_size(a) for a in ("xl", "z", "c", "y", "xh"))
    n_plane = n_xl * n_y * n_xh
    size = n_plane * rows
    half = n_z * rows
    pairs = size * n_z * n_c
    inv_root = width ** (-0.5)
    shape = jax.ShapeDtypeStruct
    tall = width // LANES * rows + EXTRA

    pair_seen = lax.ppermute(pair_index, "xl", SWAP)
    copies = pl.pallas_call(
        copies_body,
        out_shape=shape((n_plane, rows, width), BF16),
        in_specs=[pl.BlockSpec(memory_space=pltpu.VMEM)],
        out_specs=pl.BlockSpec(memory_space=pl.ANY),
        scratch_shapes=[pltpu.SemaphoreType.DMA((n_plane,))],
        name="copies",
    )(image_embed)
    image = lax.all_to_all(copies, PLANE, 0, 0).reshape(size, width)

    steps = [q if q <= n_z // 4 else q - n_z // 2 for q in range(n_z // 2)]
    far = turn(text_embed, "z", n_z // 2)
    joined, pair = call(
        join_body,
        (shape((2 * rows, width), BF16), shape((1, size), F32)),
        (text_embed, far, pair_index, pair_seen),
        "join",
        10**11,
    )
    pieces = [joined] + [turn(joined, "z", -q) for q in steps[1:]]
    pieces = pieces + [lax.ppermute(piece, "c", SWAP) for piece in pieces]

    flops = 2 * size * size * width
    scores, text, row_part, col_part = call(
        functools.partial(score_body, steps, inv_root),
        (
            shape((size, size), F32),
            shape((size, width), BF16),
            shape((1, size + LANES), F32),
            shape((1, size + 2 * LANES), F32),
        ),
        (*pieces, image, pair),
        "scores",
        flops,
        2 * size * size,
    )
    def exchange(part, axis, step):
        count = lax.axis_size(axis)
        seen = lax.ppermute(part, axis, [(i, i ^ step) for i in range(count)])
        merge_body = functools.partial(pair_body, axis == "c", size)
        return call(merge_body, (shape(part.shape, F32),), (part, seen), "pair")[0]

    for axis, step in (("c", 1), ("z", 1), ("z", 2), ("z", 4)):
        col_part = exchange(col_part, axis, step)
    for axis, step in (("xl", 1), ("xh", 1), ("y", 1), ("y", 2)):
        row_part = exchange(row_part, axis, step)

    grads, image_sent, terms = call(
        functools.partial(image_body, n_z, inv_root),
        (
            shape((size, size), BF16),
            shape((n_plane, tall, LANES), BF16),
            shape((8, LANES), F32),
        ),
        (col_part, row_part, scores, text, pair),
        "image_grad",
        flops,
        2 * size * size,
    )
    image_got = lax.all_to_all(image_sent, PLANE, 0, 0)
    text_own, text_other = call(
        functools.partial(text_body, inv_root),
        (shape((half, width), F32), shape((half, width), F32)),
        (grads, image),
        "text_grad",
        size=1,
    )
    keep, total, *pays = call(
        functools.partial(send_body, steps),
        (shape((2 * rows, width), F32), shape((1, LANES), F32))
        + (shape((2 * tall - EXTRA, LANES), BF16),) * len(steps[1:]),
        (text_own, lax.ppermute(text_other, "c", SWAP), terms, lax.ppermute(terms, "c", SWAP)),
        "send",
        size=1,
    )
    pays = [turn(pay, "z", q) for q, pay in zip(steps[1:], pays)]
    near, far, total = call(
        relay_body,
        (shape((rows, width), F32), shape((tall, LANES), BF16), shape((1, LANES), F32)),
        (keep, total, *pays),
        "relay",
        size=1,
    )
    grad_image, side = call(
        image_sum_body,
        (shape((rows, width), F32), shape((1, LANES), F32)),
        (image_got, terms),
        "image_sum",
    )
    grad_text, loss = call(
        functools.partial(text_sum_body, pairs),
        (shape((rows, width), F32), shape((1, 1), F32)),
        (near, total, terms, side, turn(far, "z", n_z // 2)),
        "text_sum",
        smem_out=1,
    )
    return (loss[0, 0], grad_image, grad_text)


def solution(mesh):
    fine = Mesh(mesh.devices.reshape(2, 8, 2, 4, 2), ("xl", "z", "c", "y", "xh"))
    image_spec = P(("xl", "z", "c", "y", "xh"), None)
    text_spec = P(("y", "xh", "xl", "z", "c"), None)
    return jax.shard_map(
        shards,
        mesh=fine,
        in_specs=(image_spec, text_spec, P(("xl", "z", "c"))),
        out_specs=(P(), image_spec, text_spec),
        check_vma=False,
    )
```

```python
import functools

import jax
import jax.numpy as jnp
from jax import lax
from jax.experimental import pallas as pl
from jax.experimental.pallas import tpu as pltpu
from jax.sharding import Mesh, PartitionSpec as P

SWAP = [(0, 1), (1, 0)]
LANES = 128
EXTRA = 16
F32 = jnp.float32
BF16 = jnp.bfloat16


def turn(x, axis, step):
    count = lax.axis_size(axis)
    return lax.ppermute(x, axis, [(i, (i + step) % count) for i in range(count)])


def turn_x(x, step):
    n_xl, n_xh = lax.axis_size("xl"), lax.axis_size("xh")
    count = n_xl * n_xh
    place = [(i % n_xl) * n_xh + i // n_xl for i in range(count)]
    pairs = [(place[i], place[(i + step) % count]) for i in range(count)]
    return lax.ppermute(x, ("xl", "xh"), pairs)


def image_slot(step_x, step_y):
    n_xl, n_y, n_xh = (lax.axis_size(a) for a in ("xl", "y", "xh"))
    x = lax.axis_index("xh") * n_xl + lax.axis_index("xl")
    x = lax.rem(x + step_x + n_xl * n_xh, n_xl * n_xh)
    y = lax.rem(lax.axis_index("y") + step_y + n_y, n_y)
    return (lax.rem(x, n_xl) * n_y + y) * n_xh + lax.div(x, n_xl)


def merge(parts):
    high = functools.reduce(jnp.maximum, parts)
    return high + jnp.log(sum(jnp.exp(p - high) for p in parts))


def encode(scaled):
    square = scaled * scaled
    fourth = square * square
    return jnp.where(scaled < 0, -fourth, fourth).astype(BF16)


def decode(x):
    wide = x.astype(F32)
    half = lax.rsqrt(jnp.maximum(jnp.abs(wide), 1e-37))
    return wide * half * (half * lax.rsqrt(half))


def split3(value):
    high = value.astype(BF16).astype(F32)
    mid = (value - high).astype(BF16).astype(F32)
    low = value - high - mid
    row = lax.broadcasted_iota(jnp.int32, (EXTRA, LANES), 0)
    parts = jnp.where(row == 0, high, jnp.where(row == 1, mid, jnp.where(row == 2, low, 0.0)))
    return parts.astype(BF16)


def inverse(value):
    return jnp.where(value > 0, 1.0 / value, 1.0)


def to_column(row):
    return jnp.transpose(jnp.broadcast_to(row, (LANES, row.shape[1])))[:, :1]


def to_row(column):
    return jnp.transpose(jnp.broadcast_to(column, (column.shape[0], LANES)))[:1, :]


def call(body, outs, args, name, flops=0, exps=0, smem_out=None, size=None, scratch=()):
    if size is None:
        size = sum(a.size * a.dtype.itemsize for a in (*args, *outs))
    spaces = [pltpu.SMEM if i == smem_out else pltpu.VMEM for i in range(len(outs))]
    return pl.pallas_call(
        body,
        out_shape=outs,
        in_specs=[pl.BlockSpec(memory_space=pltpu.VMEM)] * len(args),
        out_specs=tuple(pl.BlockSpec(memory_space=s) for s in spaces),
        scratch_shapes=scratch,
        cost_estimate=pl.CostEstimate(flops=flops, bytes_accessed=size, transcendentals=exps),
        compiler_params=pltpu.CompilerParams(vmem_limit_bytes=20 * 1024 * 1024),
        name=name,
    )(*args)


def join_body(near, far, mine, seen, *refs):
    images, (out, lined, pair) = refs[:-3], refs[-3:]
    first = lax.axis_index("xl") == 0
    left = mine[...].astype(F32)[None, :]
    right = seen[...].astype(F32)[None, :]
    pair[...] = jnp.concatenate(
        [jnp.where(first, left, right), jnp.where(first, right, left)], axis=1
    )
    rows = near.shape[0]
    out[:rows, :] = near[...]
    out[rows:, :] = far[...]
    for i, ref in enumerate(images):
        lined[i * rows : (i + 1) * rows, :] = ref[...]


def score_body(steps, steps_x, steps_y, inv_root, *refs):
    n_z = 2 * len(steps)
    pieces, refs = refs[:n_z], refs[n_z:]
    images, refs = refs[: len(steps_y)], refs[len(steps_y) :]
    pair, scores, text, image, row_sent, col_sent = refs
    rows = pieces[0].shape[0] // 2
    size = image.shape[0]
    for step_y, ref in zip(steps_y, images):
        for i, step_x in enumerate(steps_x):
            start = pl.multiple_of(image_slot(step_x, step_y) * rows, 16)
            image[pl.ds(start, rows), :] = ref[i * rows : (i + 1) * rows, :]
    ids = labels(n_z, rows)
    found = jnp.zeros((1, size), F32)
    z = lax.axis_index("z")
    high = jnp.zeros(pieces[0].shape, F32)
    for h in range(2):
        for i, q in enumerate(steps):
            piece = pieces[h * n_z // 2 + i]
            high = jnp.maximum(high, jnp.abs(piece[...].astype(F32)))
            for k in range(2):
                start = (h * n_z + lax.rem(z + q + (k + 2) * n_z // 2, n_z)) * rows
                text[pl.ds(pl.multiple_of(start, 16), rows), :] = piece[
                    k * rows : (k + 1) * rows, :
                ]
    step = 256
    for r in range(0, size, step):
        tile = (
            lax.dot_general(
                image[r : r + step, :],
                text[...],
                (((1,), (1,)), ((), ())),
                preferred_element_type=F32,
            )
            * inv_root
        )
        scores[r : r + step, :] = tile
        top = jnp.max(tile, axis=1, keepdims=True)
        part = top + jnp.log(jnp.sum(jnp.exp(tile - top), axis=1, keepdims=True))
        row_sent[:, r : r + step] = to_row(part)
        hit = to_column(pair[:, r : r + step]) == ids
        found += jnp.sum(jnp.where(hit, tile, 0.0), axis=0, keepdims=True)
    row_sent[:, size:] = jnp.full((1, LANES), jnp.max(high))
    tile = scores[...]
    top = jnp.max(tile, axis=0, keepdims=True)
    col_sent[:, :size] = top + jnp.log(jnp.sum(jnp.exp(tile - top), axis=0, keepdims=True))
    high = jnp.max(jnp.abs(image[...].astype(F32)))
    col_sent[:, size : size + LANES] = jnp.full((1, LANES), high)
    col_sent[:, size + LANES :] = jnp.full((1, LANES), jnp.sum(found))


def labels(n_z, rows):
    half = n_z * rows
    n_xl, n_c, n_xh = (lax.axis_size(a) for a in ("xl", "c", "xh"))
    block = (lax.axis_index("y") * n_xh + lax.axis_index("xh")) * n_xl + lax.axis_index("xl")
    core = lax.axis_index("c")
    slot = lax.broadcasted_iota(jnp.int32, (1, 2 * half), 1)
    own = slot < half
    within = jnp.where(own, slot, slot - half)
    holder = jnp.floor((within.astype(F32) + 0.5) * (1.0 / rows)).astype(jnp.int32)
    ids = ((block * n_z + holder) * n_c + jnp.where(own, core, 1 - core)) * rows
    return (ids + within - holder * rows).astype(F32)


def pair_body(crossed, count, mine, seen, out):
    half = count // 2
    other = seen[:, :count]
    if crossed:
        other = jnp.concatenate([seen[:, half:count], seen[:, :half]], axis=1)
    out[:, :count] = merge([mine[:, :count], other])
    at = slice(count, count + LANES)
    out[:, at] = jnp.maximum(mine[:, at], seen[:, at])
    if mine.shape[1] > count + LANES:
        at = slice(count + LANES, count + 2 * LANES)
        out[:, at] = mine[:, at] + seen[:, at]


def image_body(n_z, steps_x, steps_y, inv_root, cols, rows_lse, scores, text, pair, *refs):
    grads, terms, keep, *pays, marks = refs
    size = scores.shape[0]
    rows = keep.shape[0] // len(steps_x)
    col_lse = cols[:, :size]
    image_max = cols[:, size : size + LANES]
    found = cols[:, size + LANES :]
    ids = labels(n_z, rows)
    row_lse = rows_lse[:, :size]
    text_max = rows_lse[:, size:]
    row_terms = jnp.broadcast_to(jnp.sum(row_lse, axis=1, keepdims=True), (1, LANES))
    col_terms = jnp.sum(col_lse, axis=1, keepdims=True) - 2.0 * found
    terms[...] = jnp.concatenate(
        [row_terms, text_max, image_max, col_terms, jnp.zeros((4, LANES), F32)], axis=0
    )
    extra = split3(col_terms)
    marks[...] = jnp.transpose(
        jnp.concatenate([row_lse, pair[...], jnp.zeros((LANES - 2, size), F32)], axis=0)
    )
    scale = inverse(text_max[:, :1]) * inv_root
    for i, step_y in enumerate(steps_y):
        spots = [
            pl.ds(pl.multiple_of(image_slot(step_x, step_y) * rows, 16), rows)
            for step_x in steps_x
        ]
        tile = jnp.concatenate([scores[at, :] for at in spots], axis=0)
        mark = jnp.concatenate([marks[at, :] for at in spots], axis=0)
        probs = 0.5 * (jnp.exp(tile - mark[:, :1]) + jnp.exp(tile - col_lse))
        grad = (probs - jnp.where(mark[:, 1:2] == ids, 1.0, 0.0)).astype(BF16)
        for k, at in enumerate(spots):
            grads[at, :] = grad[k * rows : (k + 1) * rows, :]
        part = jnp.dot(grad, text[...], preferred_element_type=F32) * scale
        if i == 0:
            keep[...] = part
        else:
            blocks = [part[k * rows : (k + 1) * rows, :] for k in range(len(spots))]
            pack(pays[i - 1], blocks, extra)


def text_body(inv_root, grads, image, own, other):
    half = own.shape[0]
    for out, start in ((other, half), (own, 0)):
        out[...] = (
            lax.dot_general(
                grads[:, start : start + half],
                image[...],
                (((0,), (0,)), ((), ())),
                preferred_element_type=F32,
            )
            * inv_root
        )


def pack(pay, blocks, extra):
    rows, width = blocks[0].shape
    at = 0
    for block in blocks:
        coded = encode(block)
        for k in range(width // LANES):
            pay[at : at + rows, :] = coded[:, k * LANES : (k + 1) * LANES]
            at += rows
    pay[at:, :] = extra


def send_body(steps, own, seen, terms, terms_seen, keep, total, *pays):
    n_z = 2 * len(steps)
    rows = keep.shape[0] // 2
    z = lax.axis_index("z")
    row_terms = terms[0:1, :] + terms_seen[0:1, :]
    total[...] = row_terms
    extra = split3(row_terms)
    scale = inverse(terms[2:3, :1])
    for i, q in enumerate(steps):
        blocks = []
        for k in range(2):
            start = lax.rem(z + q + (k + 2) * n_z // 2, n_z) * rows
            at = pl.ds(pl.multiple_of(start, 16), rows)
            blocks.append((own[at, :] + seen[at, :]) * scale)
        if i == 0:
            keep[:rows, :] = blocks[0]
            keep[rows:, :] = blocks[1]
        else:
            pack(pays[i - 1], blocks, extra)


def unpack(pays, at, rows, width):
    return jnp.concatenate(
        [
            sum(decode(p[at + k * rows : at + (k + 1) * rows, :]) for p in pays)
            for k in range(width // LANES)
        ],
        axis=1,
    )


def tails(pays):
    tail = sum(p[p.shape[0] - EXTRA :, :].astype(F32) for p in pays)
    return jnp.sum(tail, axis=0, keepdims=True)


def relay_body(row, count, n_in, keep, total, *refs):
    pays, (near, total_out, *outs) = refs[:n_in], refs[n_in:]
    rows, width = near.shape
    sums = total[row : row + 1, :] + tails(pays)
    total_out[...] = sums
    extra = split3(sums)
    for k in range(count):
        block = keep[k * rows : (k + 1) * rows, :]
        block = block + unpack(pays, k * rows * width // LANES, rows, width)
        if k == 0:
            near[...] = block
        else:
            pack(outs[k - 1], [block], extra)


def text_sum_body(pairs, near, total, terms, side, pay, out, loss):
    rows, width = out.shape
    unit = terms[2:3, :1]
    unit = jnp.where(unit > 0, unit, 1.0)
    out[...] = unit * (near[...] + unpack([pay], 0, rows, width))
    full = total[...] + side[...] + tails([pay])
    loss[0, 0] = jnp.max(full) / (2.0 * pairs)


def image_sum_body(near, total, terms, *refs):
    pays, (out, side) = refs[:-2], refs[-2:]
    rows, width = out.shape
    unit = terms[1:2, :1]
    unit = jnp.where(unit > 0, unit, 1.0)
    out[...] = unit * (near[...] + unpack(pays, 0, rows, width))
    side[...] = total[...] + tails(pays)


def shards(image_embed, text_embed, pair_index):
    rows, width = image_embed.shape
    n_xl, n_z, n_c, n_y, n_xh = (lax.axis_size(a) for a in ("xl", "z", "c", "y", "xh"))
    n_plane = n_xl * n_y * n_xh
    size = n_plane * rows
    half = n_z * rows
    pairs = size * n_z * n_c
    inv_root = width ** (-0.5)
    shape = jax.ShapeDtypeStruct
    tall = width // LANES * rows + EXTRA

    pair_seen = lax.ppermute(pair_index, "xl", SWAP)
    steps_x = [0, 1, -1, 2]
    steps_y = [0, 1, -1, 2]
    steps = [q if q <= n_z // 4 else q - n_z // 2 for q in range(n_z // 2)]
    far = turn(text_embed, "z", n_z // 2)
    line = [image_embed] + [turn_x(image_embed, -q) for q in steps_x[1:]]
    joined, lined, pair = call(
        join_body,
        (
            shape((2 * rows, width), BF16),
            shape((len(line) * rows, width), BF16),
            shape((1, size), F32),
        ),
        (text_embed, far, pair_index, pair_seen, *line),
        "join",
    )
    images = [lined] + [turn(lined, "y", -q) for q in steps_y[1:]]
    pieces = [joined] + [turn(joined, "z", -q) for q in steps[1:]]
    pieces = pieces + [lax.ppermute(piece, "c", SWAP) for piece in pieces]

    flops = 2 * size * size * width
    scores, text, image, row_part, col_part = call(
        functools.partial(score_body, steps, steps_x, steps_y, inv_root),
        (
            shape((size, size), F32),
            shape((size, width), BF16),
            shape((size, width), BF16),
            shape((1, size + LANES), F32),
            shape((1, size + 2 * LANES), F32),
        ),
        (*pieces, *images, pair),
        "scores",
        flops,
        2 * size * size,
    )
    def exchange(part, axis, step):
        count = lax.axis_size(axis)
        seen = lax.ppermute(part, axis, [(i, i ^ step) for i in range(count)])
        merge_body = functools.partial(pair_body, axis == "c", size)
        return call(merge_body, (shape(part.shape, F32),), (part, seen), "pair")[0]

    for axis, step in (("c", 1), ("z", 1), ("z", 2), ("z", 4)):
        col_part = exchange(col_part, axis, step)
    for axis, step in (("xl", 1), ("xh", 1), ("y", 1), ("y", 2)):
        row_part = exchange(row_part, axis, step)

    grads, terms, image_keep, *image_pays = call(
        functools.partial(image_body, n_z, steps_x, steps_y, inv_root),
        (
            shape((size, size), BF16),
            shape((8, LANES), F32),
            shape((len(steps_x) * rows, width), F32),
        )
        + (shape((len(steps_x) * (tall - EXTRA) + EXTRA, LANES), BF16),) * len(steps_y[1:]),
        (col_part, row_part, scores, text, pair),
        "image_grad",
        flops,
        2 * size * size,
        scratch=[pltpu.VMEM((size, LANES), F32)],
    )
    image_pays = [turn(pay, "y", q) for q, pay in zip(steps_y[1:], image_pays)]
    text_own, text_other = call(
        functools.partial(text_body, inv_root),
        (shape((half, width), F32), shape((half, width), F32)),
        (grads, image),
        "text_grad",
        10**10,
    )
    keep, total, *pays = call(
        functools.partial(send_body, steps),
        (shape((2 * rows, width), F32), shape((1, LANES), F32))
        + (shape((2 * tall - EXTRA, LANES), BF16),) * len(steps[1:]),
        (text_own, lax.ppermute(text_other, "c", SWAP), terms, lax.ppermute(terms, "c", SWAP)),
        "send",
        size=1,
    )
    pays = [turn(pay, "z", q) for q, pay in zip(steps[1:], pays)]
    def relay(row, keep, total, pays, count, name):
        outs = (shape((rows, width), F32), shape((1, LANES), F32))
        outs = outs + (shape((tall, LANES), BF16),) * (count - 1)
        body = functools.partial(relay_body, row, count, len(pays))
        return call(body, outs, (keep, total, *pays), name, size=1)

    image_near, image_total, *image_pays = relay(
        3, image_keep, terms, image_pays, len(steps_x), "image_relay"
    )
    image_pays = [turn_x(pay, q) for q, pay in zip(steps_x[1:], image_pays)]
    near, total, far = relay(0, keep, total, pays, 2, "text_relay")
    grad_image, side = call(
        image_sum_body,
        (shape((rows, width), F32), shape((1, LANES), F32)),
        (image_near, image_total, terms, *image_pays),
        "image_sum",
    )
    grad_text, loss = call(
        functools.partial(text_sum_body, pairs),
        (shape((rows, width), F32), shape((1, 1), F32)),
        (near, total, terms, side, turn(far, "z", n_z // 2)),
        "text_sum",
        smem_out=1,
    )
    return (loss[0, 0], grad_image, grad_text)


def solution(mesh):
    fine = Mesh(mesh.devices.reshape(2, 8, 2, 4, 2), ("xl", "z", "c", "y", "xh"))
    image_spec = P(("xl", "z", "c", "y", "xh"), None)
    text_spec = P(("y", "xh", "xl", "z", "c"), None)
    return jax.shard_map(
        shards,
        mesh=fine,
        in_specs=(image_spec, text_spec, P(("xl", "z", "c"))),
        out_specs=(P(), image_spec, text_spec),
        check_vma=False,
    )
```

```python
import functools
import math

import jax
import jax.numpy as jnp
from jax import lax
from jax.experimental import pallas as pl
from jax.experimental.pallas import tpu as pltpu
from jax.sharding import Mesh, PartitionSpec as P

PLANE = ("xl", "y", "xh")
SWAP = [(0, 1), (1, 0)]
LANES = 128
EXTRA = 16
F32 = jnp.float32
BF16 = jnp.bfloat16


def turn(x, axis, step):
    count = lax.axis_size(axis)
    return lax.ppermute(x, axis, [(i, (i + step) % count) for i in range(count)])


def merge(parts):
    high = functools.reduce(jnp.maximum, parts)
    return high + jnp.log(sum(jnp.exp(p - high) for p in parts))


def encode(scaled):
    square = scaled * scaled
    fourth = square * square
    return jnp.where(scaled < 0, -fourth, fourth).astype(BF16)


def decode(x):
    wide = x.astype(F32)
    half = lax.rsqrt(jnp.maximum(jnp.abs(wide), 1e-37))
    return wide * half * (half * lax.rsqrt(half))


def split3(value):
    high = value.astype(BF16).astype(F32)
    mid = (value - high).astype(BF16).astype(F32)
    low = value - high - mid
    row = lax.broadcasted_iota(jnp.int32, (EXTRA, LANES), 0)
    parts = jnp.where(row == 0, high, jnp.where(row == 1, mid, jnp.where(row == 2, low, 0.0)))
    return parts.astype(BF16)


def inverse(value):
    return jnp.where(value > 0, 1.0 / value, 1.0)


def to_column(row):
    return jnp.transpose(jnp.broadcast_to(row, (LANES, row.shape[1])))[:, :1]


def to_row(column):
    return jnp.transpose(jnp.broadcast_to(column, (column.shape[0], LANES)))[:1, :]


def call(
    body, outs, args, name, flops=0, exps=0, smem_out=None, size=None, hbm_out=(), scratch=()
):
    if size is None:
        size = sum(math.prod(a.shape) * a.dtype.itemsize for a in (*args, *outs))
    spaces = [pltpu.VMEM] * len(outs)
    if smem_out is not None:
        spaces[smem_out] = pltpu.SMEM
    for i in hbm_out:
        spaces[i] = pltpu.HBM
    return pl.pallas_call(
        body,
        out_shape=outs,
        in_specs=[pl.BlockSpec(memory_space=pltpu.VMEM)] * len(args),
        out_specs=tuple(pl.BlockSpec(memory_space=s) for s in spaces),
        scratch_shapes=scratch,
        cost_estimate=pl.CostEstimate(flops=flops, bytes_accessed=size, transcendentals=exps),
        compiler_params=pltpu.CompilerParams(vmem_limit_bytes=20 * 1024 * 1024),
        name=name,
    )(*args)


def copies_body(source, out, sems):
    copies = [
        pltpu.make_async_copy(source, out.at[i], sems.at[i]) for i in range(out.shape[0])
    ]
    for copy in copies:
        copy.start()
    for copy in copies:
        copy.wait()


def join_body(near, far, mine, seen, out, pair):
    first = lax.axis_index("xl") == 0
    left = mine[...].astype(F32)[None, :]
    right = seen[...].astype(F32)[None, :]
    pair[...] = jnp.concatenate(
        [jnp.where(first, left, right), jnp.where(first, right, left)], axis=1
    )
    rows = near.shape[0]
    out[:rows, :] = near[...]
    out[rows:, :] = far[...]


def score_body(steps, inv_root, *refs):
    n_z = 2 * len(steps)
    pieces, refs = refs[:n_z], refs[n_z:]
    image, pair, scores, text, row_sent, col_sent = refs
    rows = pieces[0].shape[0] // 2
    size = image.shape[0]
    ids = labels(n_z, rows)
    found = jnp.zeros((1, size), F32)
    z = lax.axis_index("z")
    high = jnp.zeros(pieces[0].shape, F32)
    for h in range(2):
        for i, q in enumerate(steps):
            piece = pieces[h * n_z // 2 + i]
            high = jnp.maximum(high, jnp.abs(piece[...].astype(F32)))
            for k in range(2):
                start = (h * n_z + lax.rem(z + q + (k + 2) * n_z // 2, n_z)) * rows
                text[pl.ds(pl.multiple_of(start, 16), rows), :] = piece[
                    k * rows : (k + 1) * rows, :
                ]
    step = 256
    for r in range(0, size, step):
        tile = (
            lax.dot_general(
                image[r : r + step, :],
                text[...],
                (((1,), (1,)), ((), ())),
                preferred_element_type=F32,
            )
            * inv_root
        )
        scores[r : r + step, :] = tile
        top = jnp.max(tile, axis=1, keepdims=True)
        part = top + jnp.log(jnp.sum(jnp.exp(tile - top), axis=1, keepdims=True))
        row_sent[:, r : r + step] = to_row(part)
        hit = to_column(pair[:, r : r + step]) == ids
        found += jnp.sum(jnp.where(hit, tile, 0.0), axis=0, keepdims=True)
    row_sent[:, size:] = jnp.full((1, LANES), jnp.max(high))
    tile = scores[...]
    top = jnp.max(tile, axis=0, keepdims=True)
    col_sent[:, :size] = top + jnp.log(jnp.sum(jnp.exp(tile - top), axis=0, keepdims=True))
    high = jnp.max(jnp.abs(image[...].astype(F32)))
    col_sent[:, size : size + LANES] = jnp.full((1, LANES), high)
    col_sent[:, size + LANES :] = jnp.full((1, LANES), jnp.sum(found))


def labels(n_z, rows):
    half = n_z * rows
    n_xl, n_c, n_xh = (lax.axis_size(a) for a in ("xl", "c", "xh"))
    block = (lax.axis_index("y") * n_xh + lax.axis_index("xh")) * n_xl + lax.axis_index("xl")
    core = lax.axis_index("c")
    slot = lax.broadcasted_iota(jnp.int32, (1, 2 * half), 1)
    own = slot < half
    within = jnp.where(own, slot, slot - half)
    holder = jnp.floor((within.astype(F32) + 0.5) * (1.0 / rows)).astype(jnp.int32)
    ids = ((block * n_z + holder) * n_c + jnp.where(own, core, 1 - core)) * rows
    return (ids + within - holder * rows).astype(F32)


def pair_body(crossed, count, mine, seen, out):
    half = count // 2
    other = seen[:, :count]
    if crossed:
        other = jnp.concatenate([seen[:, half:count], seen[:, :half]], axis=1)
    out[:, :count] = merge([mine[:, :count], other])
    at = slice(count, count + LANES)
    out[:, at] = jnp.maximum(mine[:, at], seen[:, at])
    if mine.shape[1] > count + LANES:
        at = slice(count + LANES, count + 2 * LANES)
        out[:, at] = mine[:, at] + seen[:, at]


def image_body(
    n_z, inv_root, cols, rows_lse, scores, text, pair, grads, sent, terms, kept, held, sems
):
    size = scores.shape[0]
    n_plane = sent.shape[0]
    rows = size // n_plane
    col_lse = cols[:, :size]
    image_max = cols[:, size : size + LANES]
    found = cols[:, size + LANES :]
    ids = labels(n_z, rows)
    row_lse = rows_lse[:, :size]
    text_max = rows_lse[:, size:]
    row_terms = jnp.broadcast_to(jnp.sum(row_lse, axis=1, keepdims=True), (1, LANES))
    col_terms = jnp.sum(col_lse, axis=1, keepdims=True) - 2.0 * found
    terms[...] = jnp.concatenate(
        [row_terms, text_max, image_max, jnp.zeros((5, LANES), F32)], axis=0
    )
    extra = split3(col_terms)
    scale = inverse(text_max[:, :1]) * inv_root
    step = size // 4
    copies = []
    for r in range(0, size, step):
        tile = scores[r : r + step, :]
        probs = 0.5 * (
            jnp.exp(tile - to_column(row_lse[:, r : r + step])) + jnp.exp(tile - col_lse)
        )
        hit = to_column(pair[:, r : r + step]) == ids
        grad = (probs - jnp.where(hit, 1.0, 0.0)).astype(BF16)
        at = pl.ds(r, step)
        kept[at, :] = grad
        sem = sems.at[n_plane + r // step]
        copies.append(pltpu.make_async_copy(kept.at[at], grads.at[at], sem))
        copies[-1].start()
        part = encode(jnp.dot(grad, text[...], preferred_element_type=F32) * scale)
        for p in range(step // rows):
            to = r // rows + p
            for k in range(text.shape[1] // LANES):
                held[to, k * rows : (k + 1) * rows, :] = part[
                    p * rows : (p + 1) * rows, k * LANES : (k + 1) * LANES
                ]
            held[to, k * rows + rows :, :] = extra
            copies.append(pltpu.make_async_copy(held.at[to], sent.at[to], sems.at[to]))
            copies[-1].start()
    for copy in copies:
        copy.wait()


def text_body(inv_root, grads, image, terms_seen, own, other):
    half = own.shape[0]
    scale = inverse(terms_seen[2:3, :1]) * inv_root
    for out, start in ((other, half), (own, 0)):
        part = lax.dot_general(
            grads[:, start : start + half],
            image[...],
            (((0,), (0,)), ((), ())),
            preferred_element_type=F32,
        )
        out[...] = encode(part * scale) if out.dtype == BF16 else part * scale


def pack(pay, blocks, extra):
    rows, width = blocks[0].shape
    at = 0
    for block in blocks:
        coded = encode(block)
        for k in range(width // LANES):
            pay[at : at + rows, :] = coded[:, k * LANES : (k + 1) * LANES]
            at += rows
    pay[at:, :] = extra


def send_body(steps, own, seen, terms, terms_seen, keep, total, *pays):
    n_z = 2 * len(steps)
    rows = keep.shape[0] // 2
    z = lax.axis_index("z")
    row_terms = terms[0:1, :] + terms_seen[0:1, :]
    total[...] = row_terms
    extra = split3(row_terms)
    for i, q in enumerate(steps):
        blocks = []
        for k in range(2):
            start = lax.rem(z + q + (k + 2) * n_z // 2, n_z) * rows
            at = pl.ds(pl.multiple_of(start, 16), rows)
            blocks.append(own[at, :] + decode(seen[at, :]))
        if i == 0:
            keep[:rows, :] = blocks[0]
            keep[rows:, :] = blocks[1]
        else:
            pack(pays[i - 1], blocks, extra)


def unpack(pays, at, rows, width):
    return jnp.concatenate(
        [
            sum(decode(p[at + k * rows : at + (k + 1) * rows, :]) for p in pays)
            for k in range(width // LANES)
        ],
        axis=1,
    )


def tails(pays):
    tail = sum(p[p.shape[0] - EXTRA :, :].astype(F32) for p in pays)
    return jnp.sum(tail, axis=0, keepdims=True)


def relay_body(keep, total, *refs):
    pays, near, far, total_out = refs[:-3], refs[-3], refs[-2], refs[-1]
    rows, width = near.shape
    near[...] = keep[:rows, :] + unpack(pays, 0, rows, width)
    sums = total[...] + tails(pays)
    total_out[...] = sums
    block = keep[rows:, :] + unpack(pays, rows * width // LANES, rows, width)
    pack(far, [block], split3(sums))


def text_sum_body(near, total, terms, pay, out, side):
    rows, width = out.shape
    unit = terms[2:3, :1]
    unit = jnp.where(unit > 0, unit, 1.0)
    out[...] = unit * (near[...] + unpack([pay], 0, rows, width))
    side[...] = total[...] + tails([pay])


def image_sum_body(pairs, got, terms, side, out, loss):
    rows, width = out.shape
    unit = terms[1:2, :1]
    unit = jnp.where(unit > 0, unit, 1.0)
    pays = [got.at[p] for p in range(got.shape[0])]
    for k in range(width // LANES):
        at = slice(k * rows, (k + 1) * rows)
        out[:, k * LANES : (k + 1) * LANES] = unit * sum(decode(p[at, :]) for p in pays)
    full = side[...] + tails(pays)
    loss[0, 0] = jnp.max(full) / (2.0 * pairs)


def shards(image_embed, text_embed, pair_index):
    rows, width = image_embed.shape
    n_xl, n_z, n_c, n_y, n_xh = (lax.axis_size(a) for a in ("xl", "z", "c", "y", "xh"))
    n_plane = n_xl * n_y * n_xh
    size = n_plane * rows
    half = n_z * rows
    pairs = size * n_z * n_c
    inv_root = width ** (-0.5)
    shape = jax.ShapeDtypeStruct
    tall = width // LANES * rows + EXTRA

    pair_seen = lax.ppermute(pair_index, "xl", SWAP)
    copies = pl.pallas_call(
        copies_body,
        out_shape=shape((n_plane, rows, width), BF16),
        in_specs=[pl.BlockSpec(memory_space=pl.ANY)],
        out_specs=pl.BlockSpec(memory_space=pl.ANY),
        scratch_shapes=[pltpu.SemaphoreType.DMA((n_plane,))],
        name="copies",
    )(image_embed)
    image = lax.all_to_all(copies, PLANE, 0, 0).reshape(size, width)

    steps = [q if q <= n_z // 4 else q - n_z // 2 for q in range(n_z // 2)]
    far = turn(text_embed, "z", n_z // 2)
    joined, pair = call(
        join_body,
        (shape((2 * rows, width), BF16), shape((1, size), F32)),
        (text_embed, far, pair_index, pair_seen),
        "join",
        10**11,
    )
    pieces = [joined] + [turn(joined, "z", -q) for q in steps[1:]]
    pieces = pieces + [lax.ppermute(piece, "c", SWAP) for piece in pieces]

    flops = 2 * size * size * width
    scores, text, row_part, col_part = call(
        functools.partial(score_body, steps, inv_root),
        (
            shape((size, size), F32),
            shape((size, width), BF16),
            shape((1, size + LANES), F32),
            shape((1, size + 2 * LANES), F32),
        ),
        (*pieces, image, pair),
        "scores",
        flops,
        2 * size * size,
    )
    def exchange(part, axis, step):
        count = lax.axis_size(axis)
        seen = lax.ppermute(part, axis, [(i, i ^ step) for i in range(count)])
        merge_body = functools.partial(pair_body, axis == "c", size)
        return call(merge_body, (shape(part.shape, F32),), (part, seen), "pair")[0]

    for axis, step in (("c", 1), ("z", 1), ("z", 2), ("z", 4)):
        col_part = exchange(col_part, axis, step)
    for axis, step in (("xl", 1), ("xh", 1), ("y", 1), ("y", 2)):
        row_part = exchange(row_part, axis, step)

    grads, image_sent, terms = call(
        functools.partial(image_body, n_z, inv_root),
        (
            pltpu.HBM((size, size), BF16),
            pltpu.HBM((n_plane, tall, LANES), BF16),
            shape((8, LANES), F32),
        ),
        (col_part, row_part, scores, text, pair),
        "image_grad",
        flops,
        2 * size * size,
        hbm_out=(0, 1),
        scratch=[
            pltpu.VMEM((size, size), BF16),
            pltpu.VMEM((n_plane, tall, LANES), BF16),
            pltpu.SemaphoreType.DMA((n_plane + 4,)),
        ],
    )
    image_got = lax.all_to_all(image_sent, PLANE, 0, 0)
    terms_seen = lax.ppermute(terms, "c", SWAP)
    text_own, text_other = call(
        functools.partial(text_body, inv_root),
        (shape((half, width), F32), shape((half, width), BF16)),
        (grads, image, terms_seen),
        "text_grad",
        10**11,
        size=1,
    )
    keep, total, *pays = call(
        functools.partial(send_body, steps),
        (shape((2 * rows, width), F32), shape((1, LANES), F32))
        + (shape((2 * tall - EXTRA, LANES), BF16),) * len(steps[1:]),
        (text_own, lax.ppermute(text_other, "c", SWAP), terms, terms_seen),
        "send",
        size=1,
    )
    pays = [turn(pay, "z", q) for q, pay in zip(steps[1:], pays)]
    near, far, total = call(
        relay_body,
        (shape((rows, width), F32), shape((tall, LANES), BF16), shape((1, LANES), F32)),
        (keep, total, *pays),
        "relay",
        size=1,
    )
    grad_text, side = call(
        text_sum_body,
        (shape((rows, width), F32), shape((1, LANES), F32)),
        (near, total, terms, turn(far, "z", n_z // 2)),
        "text_sum",
        size=1,
    )
    grad_image, loss = call(
        functools.partial(image_sum_body, pairs),
        (shape((rows, width), F32), shape((1, 1), F32)),
        (image_got, terms, side),
        "image_sum",
        smem_out=1,
    )
    return (loss[0, 0], grad_image, grad_text)


def solution(mesh):
    fine = Mesh(mesh.devices.reshape(2, 8, 2, 4, 2), ("xl", "z", "c", "y", "xh"))
    image_spec = P(("xl", "z", "c", "y", "xh"), None)
    text_spec = P(("y", "xh", "xl", "z", "c"), None)
    return jax.shard_map(
        shards,
        mesh=fine,
        in_specs=(image_spec, text_spec, P(("xl", "z", "c"))),
        out_specs=(P(), image_spec, text_spec),
        check_vma=False,
    )
```

```python
import functools
import math

import jax
import jax.numpy as jnp
from jax import lax
from jax.experimental import pallas as pl
from jax.experimental.pallas import tpu as pltpu
from jax.sharding import Mesh, PartitionSpec as P

PLANE = ("xl", "y", "xh")
SWAP = [(0, 1), (1, 0)]
LANES = 128
EXTRA = 16
F32 = jnp.float32
BF16 = jnp.bfloat16


def turn(x, axis, step):
    count = lax.axis_size(axis)
    return lax.ppermute(x, axis, [(i, (i + step) % count) for i in range(count)])


def merge(parts):
    high = functools.reduce(jnp.maximum, parts)
    return high + jnp.log(sum(jnp.exp(p - high) for p in parts))


def encode(scaled):
    square = scaled * scaled
    fourth = square * square
    return jnp.where(scaled < 0, -fourth, fourth).astype(BF16)


def decode(x):
    wide = x.astype(F32)
    half = lax.rsqrt(jnp.maximum(jnp.abs(wide), 1e-37))
    return wide * half * (half * lax.rsqrt(half))


def split3(value):
    high = value.astype(BF16).astype(F32)
    mid = (value - high).astype(BF16).astype(F32)
    low = value - high - mid
    row = lax.broadcasted_iota(jnp.int32, (EXTRA, LANES), 0)
    parts = jnp.where(row == 0, high, jnp.where(row == 1, mid, jnp.where(row == 2, low, 0.0)))
    return parts.astype(BF16)


def inverse(value):
    return jnp.where(value > 0, 1.0 / value, 1.0)


def to_column(row):
    return jnp.transpose(jnp.broadcast_to(row, (LANES, row.shape[1])))[:, :1]


def to_row(column):
    return jnp.transpose(jnp.broadcast_to(column, (column.shape[0], LANES)))[:1, :]


def call(
    body, outs, args, name, flops=0, exps=0, smem_out=None, size=None, hbm_out=(), scratch=()
):
    if size is None:
        size = sum(math.prod(a.shape) * a.dtype.itemsize for a in (*args, *outs))
    spaces = [pltpu.VMEM] * len(outs)
    if smem_out is not None:
        spaces[smem_out] = pltpu.SMEM
    for i in hbm_out:
        spaces[i] = pltpu.HBM
    return pl.pallas_call(
        body,
        out_shape=outs,
        in_specs=[pl.BlockSpec(memory_space=pltpu.VMEM)] * len(args),
        out_specs=tuple(pl.BlockSpec(memory_space=s) for s in spaces),
        scratch_shapes=scratch,
        cost_estimate=pl.CostEstimate(flops=flops, bytes_accessed=size, transcendentals=exps),
        compiler_params=pltpu.CompilerParams(vmem_limit_bytes=20 * 1024 * 1024),
        name=name,
    )(*args)


def copies_body(source, out, sems):
    copies = [
        pltpu.make_async_copy(source, out.at[i], sems.at[i]) for i in range(out.shape[0])
    ]
    for copy in copies:
        copy.start()
    for copy in copies:
        copy.wait()


def join_body(near, far, mine, seen, out, pair):
    first = lax.axis_index("xl") == 0
    left = mine[...].astype(F32)[None, :]
    right = seen[...].astype(F32)[None, :]
    pair[...] = jnp.concatenate(
        [jnp.where(first, left, right), jnp.where(first, right, left)], axis=1
    )
    rows = near.shape[0]
    out[:rows, :] = near[...]
    out[rows:, :] = far[...]


def score_body(steps, inv_root, *refs):
    n_z = 2 * len(steps)
    pieces, refs = refs[:n_z], refs[n_z:]
    image, pair, scores, text, row_sent, col_sent = refs
    rows = pieces[0].shape[0] // 2
    size = image.shape[0]
    ids = labels(n_z, rows)
    found = jnp.zeros((1, size), F32)
    z = lax.axis_index("z")
    high = jnp.zeros(pieces[0].shape, F32)
    for h in range(2):
        for i, q in enumerate(steps):
            piece = pieces[h * n_z // 2 + i]
            high = jnp.maximum(high, jnp.abs(piece[...].astype(F32)))
            for k in range(2):
                start = (h * n_z + lax.rem(z + q + (k + 2) * n_z // 2, n_z)) * rows
                text[pl.ds(pl.multiple_of(start, 16), rows), :] = piece[
                    k * rows : (k + 1) * rows, :
                ]
    step = 256
    for r in range(0, size, step):
        tile = (
            lax.dot_general(
                image[r : r + step, :],
                text[...],
                (((1,), (1,)), ((), ())),
                preferred_element_type=F32,
            )
            * inv_root
        )
        scores[r : r + step, :] = tile
        top = jnp.max(tile, axis=1, keepdims=True)
        part = top + jnp.log(jnp.sum(jnp.exp(tile - top), axis=1, keepdims=True))
        row_sent[:, r : r + step] = to_row(part)
        hit = to_column(pair[:, r : r + step]) == ids
        found += jnp.sum(jnp.where(hit, tile, 0.0), axis=0, keepdims=True)
    row_sent[:, size:] = jnp.full((1, LANES), jnp.max(high))
    tile = scores[...]
    top = jnp.max(tile, axis=0, keepdims=True)
    col_sent[:, :size] = top + jnp.log(jnp.sum(jnp.exp(tile - top), axis=0, keepdims=True))
    high = jnp.max(jnp.abs(image[...].astype(F32)))
    col_sent[:, size : size + LANES] = jnp.full((1, LANES), high)
    col_sent[:, size + LANES :] = jnp.full((1, LANES), jnp.sum(found))


def labels(n_z, rows):
    half = n_z * rows
    n_xl, n_c, n_xh = (lax.axis_size(a) for a in ("xl", "c", "xh"))
    block = (lax.axis_index("y") * n_xh + lax.axis_index("xh")) * n_xl + lax.axis_index("xl")
    core = lax.axis_index("c")
    slot = lax.broadcasted_iota(jnp.int32, (1, 2 * half), 1)
    own = slot < half
    within = jnp.where(own, slot, slot - half)
    holder = jnp.floor((within.astype(F32) + 0.5) * (1.0 / rows)).astype(jnp.int32)
    ids = ((block * n_z + holder) * n_c + jnp.where(own, core, 1 - core)) * rows
    return (ids + within - holder * rows).astype(F32)


def pair_body(crossed, count, mine, seen, out):
    half = count // 2
    other = seen[:, :count]
    if crossed:
        other = jnp.concatenate([seen[:, half:count], seen[:, :half]], axis=1)
    out[:, :count] = merge([mine[:, :count], other])
    at = slice(count, count + LANES)
    out[:, at] = jnp.maximum(mine[:, at], seen[:, at])
    if mine.shape[1] > count + LANES:
        at = slice(count + LANES, count + 2 * LANES)
        out[:, at] = mine[:, at] + seen[:, at]


def text_body(n_z, inv_root, cols, rows_lse, scores, image, pair, grads, terms, own, other):
    size = scores.shape[0]
    half = own.shape[0]
    rows = half // n_z
    col_lse = cols[:, :size]
    image_max = cols[:, size : size + LANES]
    found = cols[:, size + LANES :]
    ids = labels(n_z, rows)
    row_lse = rows_lse[:, :size]
    text_max = rows_lse[:, size:]
    row_terms = jnp.broadcast_to(jnp.sum(row_lse, axis=1, keepdims=True), (1, LANES))
    col_terms = jnp.sum(col_lse, axis=1, keepdims=True) - 2.0 * found
    terms[...] = jnp.concatenate(
        [row_terms, text_max, image_max, col_terms, jnp.zeros((4, LANES), F32)], axis=0
    )
    scale = inverse(image_max[:, :1]) * inv_root
    row_column = to_column(row_lse)
    pair_column = to_column(pair[...])
    for start in (half, 0):
        at = slice(start, start + half)
        tile = scores[:, at]
        probs = 0.5 * (jnp.exp(tile - row_column) + jnp.exp(tile - col_lse[:, at]))
        grad = (probs - jnp.where(pair_column == ids[:, at], 1.0, 0.0)).astype(BF16)
        grads[:, at] = grad
        part = lax.dot_general(
            grad, image[...], (((0,), (0,)), ((), ())), preferred_element_type=F32
        )
        if start == 0:
            own[...] = part * scale
        else:
            other[:half, :] = encode(part * scale)
    extra = split3(row_terms)
    other[half:, :] = jnp.concatenate([extra] * (other.shape[1] // LANES), axis=1)


def image_body(inv_root, grads, text, terms, sent, held, sems):
    size = grads.shape[0]
    n_plane, tall, _ = sent.shape
    rows = size // n_plane
    extra = split3(terms[3:4, :])
    scale = inverse(terms[1:2, :1]) * inv_root
    step = size // 4
    copies = []
    for r in range(0, size, step):
        part = jnp.dot(grads[r : r + step, :], text[...], preferred_element_type=F32)
        part = encode(part * scale)
        for p in range(step // rows):
            to = r // rows + p
            for k in range(text.shape[1] // LANES):
                held[to, k * rows : (k + 1) * rows, :] = part[
                    p * rows : (p + 1) * rows, k * LANES : (k + 1) * LANES
                ]
            held[to, tall - EXTRA :, :] = extra
            copies.append(pltpu.make_async_copy(held.at[to], sent.at[to], sems.at[to]))
            copies[-1].start()
    for copy in copies:
        copy.wait()


def pack(pay, blocks, extra):
    rows, width = blocks[0].shape
    at = 0
    for block in blocks:
        coded = encode(block)
        for k in range(width // LANES):
            pay[at : at + rows, :] = coded[:, k * LANES : (k + 1) * LANES]
            at += rows
    pay[at:, :] = extra


def send_body(steps, own, seen, terms, keep, total, *pays):
    n_z = 2 * len(steps)
    rows = keep.shape[0] // 2
    z = lax.axis_index("z")
    half = own.shape[0]
    tail = seen[half:, :LANES].astype(F32)
    row_terms = terms[0:1, :] + jnp.sum(tail, axis=0, keepdims=True)
    total[...] = row_terms
    extra = split3(row_terms)
    for i, q in enumerate(steps):
        blocks = []
        for k in range(2):
            start = lax.rem(z + q + (k + 2) * n_z // 2, n_z) * rows
            at = pl.ds(pl.multiple_of(start, 16), rows)
            blocks.append(own[at, :] + decode(seen[at, :]))
        if i == 0:
            keep[:rows, :] = blocks[0]
            keep[rows:, :] = blocks[1]
        else:
            pack(pays[i - 1], blocks, extra)


def unpack(pays, at, rows, width):
    return jnp.concatenate(
        [
            sum(decode(p[at + k * rows : at + (k + 1) * rows, :]) for p in pays)
            for k in range(width // LANES)
        ],
        axis=1,
    )


def tails(pays):
    tail = sum(p[p.shape[0] - EXTRA :, :].astype(F32) for p in pays)
    return jnp.sum(tail, axis=0, keepdims=True)


def relay_body(keep, total, *refs):
    pays, near, far, total_out = refs[:-3], refs[-3], refs[-2], refs[-1]
    rows, width = near.shape
    near[...] = keep[:rows, :] + unpack(pays, 0, rows, width)
    sums = total[...] + tails(pays)
    total_out[...] = sums
    block = keep[rows:, :] + unpack(pays, rows * width // LANES, rows, width)
    pack(far, [block], split3(sums))


def text_sum_body(near, total, terms, pay, out, side):
    rows, width = out.shape
    unit = terms[2:3, :1]
    unit = jnp.where(unit > 0, unit, 1.0)
    out[...] = unit * (near[...] + unpack([pay], 0, rows, width))
    side[...] = total[...] + tails([pay])


def image_sum_body(pairs, got, terms, side, out, loss):
    rows, width = out.shape
    unit = terms[1:2, :1]
    unit = jnp.where(unit > 0, unit, 1.0)
    pays = [got.at[p] for p in range(got.shape[0])]
    for k in range(width // LANES):
        at = slice(k * rows, (k + 1) * rows)
        out[:, k * LANES : (k + 1) * LANES] = unit * sum(decode(p[at, :]) for p in pays)
    full = side[...] + tails(pays)
    loss[0, 0] = jnp.max(full) / (2.0 * pairs)


def shards(image_embed, text_embed, pair_index):
    rows, width = image_embed.shape
    n_xl, n_z, n_c, n_y, n_xh = (lax.axis_size(a) for a in ("xl", "z", "c", "y", "xh"))
    n_plane = n_xl * n_y * n_xh
    size = n_plane * rows
    half = n_z * rows
    pairs = size * n_z * n_c
    inv_root = width ** (-0.5)
    shape = jax.ShapeDtypeStruct
    tall = width // LANES * rows + EXTRA

    pair_seen = lax.ppermute(pair_index, "xl", SWAP)
    copies = pl.pallas_call(
        copies_body,
        out_shape=shape((n_plane, rows, width), BF16),
        in_specs=[pl.BlockSpec(memory_space=pltpu.VMEM)],
        out_specs=pl.BlockSpec(memory_space=pl.ANY),
        scratch_shapes=[pltpu.SemaphoreType.DMA((n_plane,))],
        name="copies",
    )(image_embed)
    image = lax.all_to_all(copies, PLANE, 0, 0).reshape(size, width)

    steps = [q if q <= n_z // 4 else q - n_z // 2 for q in range(n_z // 2)]
    far = turn(text_embed, "z", n_z // 2)
    joined, pair = call(
        join_body,
        (shape((2 * rows, width), BF16), shape((1, size), F32)),
        (text_embed, far, pair_index, pair_seen),
        "join",
        10**11,
    )
    pieces = [joined] + [turn(joined, "z", -q) for q in steps[1:]]
    pieces = pieces + [lax.ppermute(piece, "c", SWAP) for piece in pieces]

    flops = 2 * size * size * width
    scores, text, row_part, col_part = call(
        functools.partial(score_body, steps, inv_root),
        (
            shape((size, size), F32),
            shape((size, width), BF16),
            shape((1, size + LANES), F32),
            shape((1, size + 2 * LANES), F32),
        ),
        (*pieces, image, pair),
        "scores",
        flops,
        2 * size * size,
    )
    def exchange(part, axis, step):
        count = lax.axis_size(axis)
        seen = lax.ppermute(part, axis, [(i, i ^ step) for i in range(count)])
        merge_body = functools.partial(pair_body, axis == "c", size)
        return call(merge_body, (shape(part.shape, F32),), (part, seen), "pair")[0]

    for axis, step in (("c", 1), ("z", 1), ("z", 2), ("z", 4)):
        col_part = exchange(col_part, axis, step)
    for axis, step in (("xl", 1), ("xh", 1), ("y", 1), ("y", 2)):
        row_part = exchange(row_part, axis, step)

    grads, terms, text_own, text_other = call(
        functools.partial(text_body, n_z, inv_root),
        (
            shape((size, size), BF16),
            shape((8, LANES), F32),
            shape((half, width), F32),
            shape((half + EXTRA, width), BF16),
        ),
        (col_part, row_part, scores, image, pair),
        "text_grad",
        flops,
        2 * size * size,
    )
    (image_sent,) = call(
        functools.partial(image_body, inv_root),
        (pltpu.HBM((n_plane, tall, LANES), BF16),),
        (grads, text, terms),
        "image_grad",
        flops,
        hbm_out=(0,),
        scratch=[
            pltpu.VMEM((n_plane, tall, LANES), BF16),
            pltpu.SemaphoreType.DMA((n_plane,)),
        ],
    )
    image_got = lax.all_to_all(image_sent, PLANE, 0, 0)
    keep, total, *pays = call(
        functools.partial(send_body, steps),
        (shape((2 * rows, width), F32), shape((1, LANES), F32))
        + (shape((2 * tall - EXTRA, LANES), BF16),) * len(steps[1:]),
        (text_own, lax.ppermute(text_other, "c", SWAP), terms),
        "send",
        size=1,
    )
    pays = [turn(pay, "z", q) for q, pay in zip(steps[1:], pays)]
    near, far, total = call(
        relay_body,
        (shape((rows, width), F32), shape((tall, LANES), BF16), shape((1, LANES), F32)),
        (keep, total, *pays),
        "relay",
        10**11,
        size=1,
    )
    grad_text, side = call(
        text_sum_body,
        (shape((rows, width), F32), shape((1, LANES), F32)),
        (near, total, terms, turn(far, "z", n_z // 2)),
        "text_sum",
        size=1,
    )
    grad_image, loss = call(
        functools.partial(image_sum_body, pairs),
        (shape((rows, width), F32), shape((1, 1), F32)),
        (image_got, terms, side),
        "image_sum",
        smem_out=1,
    )
    return (loss[0, 0], grad_image, grad_text)


def solution(mesh):
    fine = Mesh(mesh.devices.reshape(2, 8, 2, 4, 2), ("xl", "z", "c", "y", "xh"))
    image_spec = P(("xl", "z", "c", "y", "xh"), None)
    text_spec = P(("y", "xh", "xl", "z", "c"), None)
    return jax.shard_map(
        shards,
        mesh=fine,
        in_specs=(image_spec, text_spec, P(("xl", "z", "c"))),
        out_specs=(P(), image_spec, text_spec),
        check_vma=False,
    )
```

```python
import functools
import math

import jax
import jax.numpy as jnp
from jax import lax
from jax.experimental import pallas as pl
from jax.experimental.pallas import tpu as pltpu
from jax.sharding import Mesh, PartitionSpec as P

PLANE = ("xl", "y", "xh")
SWAP = [(0, 1), (1, 0)]
LANES = 128
EXTRA = 16
F32 = jnp.float32
BF16 = jnp.bfloat16


def turn(x, axis, step):
    count = lax.axis_size(axis)
    return lax.ppermute(x, axis, [(i, (i + step) % count) for i in range(count)])


def merge(parts):
    high = functools.reduce(jnp.maximum, parts)
    return high + jnp.log(sum(jnp.exp(p - high) for p in parts))


def encode(scaled):
    square = scaled * scaled
    fourth = square * square
    return jnp.where(scaled < 0, -fourth, fourth).astype(BF16)


def decode(x):
    wide = x.astype(F32)
    half = lax.rsqrt(jnp.maximum(jnp.abs(wide), 1e-37))
    return wide * half * (half * lax.rsqrt(half))


def split3(value):
    high = value.astype(BF16).astype(F32)
    mid = (value - high).astype(BF16).astype(F32)
    low = value - high - mid
    row = lax.broadcasted_iota(jnp.int32, (EXTRA, LANES), 0)
    parts = jnp.where(row == 0, high, jnp.where(row == 1, mid, jnp.where(row == 2, low, 0.0)))
    return parts.astype(BF16)


def inverse(value):
    return jnp.where(value > 0, 1.0 / value, 1.0)


def to_column(row):
    return jnp.transpose(jnp.broadcast_to(row, (LANES, row.shape[1])))[:, :1]


def to_row(column):
    return jnp.transpose(jnp.broadcast_to(column, (column.shape[0], LANES)))[:1, :]


def call(
    body, outs, args, name, flops=0, exps=0, smem_out=None, size=None, hbm_out=(), scratch=()
):
    if size is None:
        size = sum(math.prod(a.shape) * a.dtype.itemsize for a in (*args, *outs))
    spaces = [pltpu.VMEM] * len(outs)
    if smem_out is not None:
        spaces[smem_out] = pltpu.SMEM
    for i in hbm_out:
        spaces[i] = pltpu.HBM
    return pl.pallas_call(
        body,
        out_shape=outs,
        in_specs=[pl.BlockSpec(memory_space=pltpu.VMEM)] * len(args),
        out_specs=tuple(pl.BlockSpec(memory_space=s) for s in spaces),
        scratch_shapes=scratch,
        cost_estimate=pl.CostEstimate(flops=flops, bytes_accessed=size, transcendentals=exps),
        compiler_params=pltpu.CompilerParams(vmem_limit_bytes=20 * 1024 * 1024),
        name=name,
    )(*args)


def copies_body(source, out, sems):
    copies = [
        pltpu.make_async_copy(source, out.at[i], sems.at[i]) for i in range(out.shape[0])
    ]
    for copy in copies:
        copy.start()
    for copy in copies:
        copy.wait()


def join_body(near, far, out):
    rows = near.shape[0]
    out[:rows, :] = near[...]
    out[rows:, :] = far[...]


def pair_row(mine, seen):
    first = lax.axis_index("xl") == 0
    left = mine[...].astype(F32)[None, :]
    right = seen[...].astype(F32)[None, :]
    return jnp.concatenate(
        [jnp.where(first, left, right), jnp.where(first, right, left)], axis=1
    )


def score_body(steps, inv_root, *refs):
    n_z = 2 * len(steps)
    pieces, refs = refs[:n_z], refs[n_z:]
    image, pair_mine, pair_seen, pair_out, row_exp, col_exp, text, row_sent, col_sent, tops = refs
    pair = pair_row(pair_mine, pair_seen)
    pair_out[...] = pair
    rows = pieces[0].shape[0] // 2
    size = image.shape[0]
    ids = labels(n_z, rows)
    found = jnp.zeros((1, size), F32)
    z = lax.axis_index("z")
    high = jnp.zeros(pieces[0].shape, F32)
    for h in range(2):
        for i, q in enumerate(steps):
            piece = pieces[h * n_z // 2 + i]
            high = jnp.maximum(high, jnp.abs(piece[...].astype(F32)))
            for k in range(2):
                start = (h * n_z + lax.rem(z + q + (k + 2) * n_z // 2, n_z)) * rows
                text[pl.ds(pl.multiple_of(start, 16), rows), :] = piece[
                    k * rows : (k + 1) * rows, :
                ]
    step = 256
    for r in range(0, size, step):
        tile = (
            lax.dot_general(
                image[r : r + step, :],
                text[...],
                (((1,), (1,)), ((), ())),
                preferred_element_type=F32,
            )
            * inv_root
        )
        col_exp[r : r + step, :] = tile
        top = jnp.max(tile, axis=1, keepdims=True)
        mass = jnp.exp(tile - top)
        row_exp[r : r + step, :] = mass
        part = jnp.log(jnp.sum(mass, axis=1, keepdims=True))
        tops[0:1, r : r + step] = to_row(top)
        row_sent[:, r : r + step] = to_row(top + part)
        hit = to_column(pair[:, r : r + step]) == ids
        found += jnp.sum(jnp.where(hit, tile, 0.0), axis=0, keepdims=True)
    row_sent[:, size:] = jnp.full((1, LANES), jnp.max(high))
    tile = col_exp[...]
    top = jnp.max(tile, axis=0, keepdims=True)
    mass = jnp.exp(tile - top)
    col_exp[...] = mass
    tops[1:2, :] = top
    col_sent[:, :size] = top + jnp.log(jnp.sum(mass, axis=0, keepdims=True))
    high = jnp.max(jnp.abs(image[...].astype(F32)))
    col_sent[:, size : size + LANES] = jnp.full((1, LANES), high)
    col_sent[:, size + LANES :] = jnp.full((1, LANES), jnp.sum(found))


def labels(n_z, rows):
    half = n_z * rows
    n_xl, n_c, n_xh = (lax.axis_size(a) for a in ("xl", "c", "xh"))
    block = (lax.axis_index("y") * n_xh + lax.axis_index("xh")) * n_xl + lax.axis_index("xl")
    core = lax.axis_index("c")
    slot = lax.broadcasted_iota(jnp.int32, (1, 2 * half), 1)
    own = slot < half
    within = jnp.where(own, slot, slot - half)
    holder = jnp.floor((within.astype(F32) + 0.5) * (1.0 / rows)).astype(jnp.int32)
    ids = ((block * n_z + holder) * n_c + jnp.where(own, core, 1 - core)) * rows
    return (ids + within - holder * rows).astype(F32)


def pair_body(crossed, count, mine, seen, out):
    half = count // 2
    other = seen[:, :count]
    if crossed:
        other = jnp.concatenate([seen[:, half:count], seen[:, :half]], axis=1)
    out[:, :count] = merge([mine[:, :count], other])
    at = slice(count, count + LANES)
    out[:, at] = jnp.maximum(mine[:, at], seen[:, at])
    if mine.shape[1] > count + LANES:
        at = slice(count + LANES, count + 2 * LANES)
        out[:, at] = mine[:, at] + seen[:, at]


def grad_body(n_z, inv_root, *refs):
    cols, rows_lse, tops, row_exp, col_exp, text, image, pair = refs[:8]
    terms, own, other, sent, grads, held, crossing, staying, sems = refs[8:]
    size = grads.shape[0]
    half = own.shape[0]
    rows = half // n_z
    _, tall, _ = sent.shape
    col_lse = cols[:, :size]
    image_max = cols[:, size : size + LANES]
    found = cols[:, size + LANES :]
    ids = labels(n_z, rows)
    row_lse = rows_lse[:, :size]
    text_max = rows_lse[:, size:]
    row_terms = jnp.broadcast_to(jnp.sum(row_lse, axis=1, keepdims=True), (1, LANES))
    col_terms = jnp.sum(col_lse, axis=1, keepdims=True) - 2.0 * found
    terms[...] = jnp.concatenate(
        [row_terms, text_max, image_max, jnp.zeros((5, LANES), F32)], axis=0
    )
    row_part = to_column(0.5 * jnp.exp(tops[0:1, :] - row_lse))
    col_part = 0.5 * jnp.exp(tops[1:2, :] - col_lse)
    pair_column = to_column(pair[...])
    extra = split3(col_terms)
    scale = inverse(text_max[:, :1]) * inv_root
    step = size // 4
    copies = []
    for r in range(0, size, step):
        at = slice(r, r + step)
        probs = row_exp[at, :] * row_part[at, :] + col_exp[at, :] * col_part
        grad = (probs - jnp.where(pair_column[at, :] == ids, 1.0, 0.0)).astype(BF16)
        grads[at, :] = grad
        part = encode(jnp.dot(grad, text[...], preferred_element_type=F32) * scale)
        for p in range(step // rows):
            to = r // rows + p
            for k in range(text.shape[1] // LANES):
                held[to, k * rows : (k + 1) * rows, :] = part[
                    p * rows : (p + 1) * rows, k * LANES : (k + 1) * LANES
                ]
            held[to, tall - EXTRA :, :] = extra
            copies.append(pltpu.make_async_copy(held.at[to], sent.at[to], sems.at[to]))
            copies[-1].start()
    scale = inverse(image_max[:, :1]) * inv_root
    extra = split3(row_terms)
    crossing[half:, :] = jnp.concatenate([extra] * (own.shape[1] // LANES), axis=1)
    for start in (0, half):
        part = lax.dot_general(
            grads[:, start : start + half],
            image[...],
            (((0,), (0,)), ((), ())),
            preferred_element_type=F32,
        )
        if start == 0:
            staying[...] = part * scale
            copies.append(pltpu.make_async_copy(staying, own, sems.at[sent.shape[0]]))
        else:
            crossing[:half, :] = encode(part * scale)
            copies.append(pltpu.make_async_copy(crossing, other, sems.at[sent.shape[0] + 1]))
        copies[-1].start()
    for copy in copies:
        copy.wait()


def pack(pay, blocks, extra):
    rows, width = blocks[0].shape
    at = 0
    for block in blocks:
        coded = encode(block)
        for k in range(width // LANES):
            pay[at : at + rows, :] = coded[:, k * LANES : (k + 1) * LANES]
            at += rows
    pay[at:, :] = extra


def send_body(steps, own, seen, terms, keep, total, *pays):
    n_z = 2 * len(steps)
    rows = keep.shape[0] // 2
    z = lax.axis_index("z")
    half = own.shape[0]
    tail = seen[half:, :LANES].astype(F32)
    row_terms = terms[0:1, :] + jnp.sum(tail, axis=0, keepdims=True)
    total[...] = row_terms
    extra = split3(row_terms)
    for i, q in enumerate(steps):
        blocks = []
        for k in range(2):
            start = lax.rem(z + q + (k + 2) * n_z // 2, n_z) * rows
            at = pl.ds(pl.multiple_of(start, 16), rows)
            blocks.append(own[at, :] + decode(seen[at, :]))
        if i == 0:
            keep[:rows, :] = blocks[0]
            keep[rows:, :] = blocks[1]
        else:
            pack(pays[i - 1], blocks, extra)


def unpack(pays, at, rows, width):
    return jnp.concatenate(
        [
            sum(decode(p[at + k * rows : at + (k + 1) * rows, :]) for p in pays)
            for k in range(width // LANES)
        ],
        axis=1,
    )


def tails(pays):
    tail = sum(p[p.shape[0] - EXTRA :, :].astype(F32) for p in pays)
    return jnp.sum(tail, axis=0, keepdims=True)


def relay_body(keep, total, *refs):
    pays, near, far, total_out = refs[:-3], refs[-3], refs[-2], refs[-1]
    rows, width = near.shape
    near[...] = keep[:rows, :] + unpack(pays, 0, rows, width)
    sums = total[...] + tails(pays)
    total_out[...] = sums
    block = keep[rows:, :] + unpack(pays, rows * width // LANES, rows, width)
    pack(far, [block], split3(sums))


def text_sum_body(near, total, terms, pay, out, side):
    rows, width = out.shape
    unit = terms[2:3, :1]
    unit = jnp.where(unit > 0, unit, 1.0)
    out[...] = unit * (near[...] + unpack([pay], 0, rows, width))
    side[...] = total[...] + tails([pay])


def image_sum_body(pairs, got, terms, side, out, loss):
    rows, width = out.shape
    unit = terms[1:2, :1]
    unit = jnp.where(unit > 0, unit, 1.0)
    pays = [got.at[p] for p in range(got.shape[0])]
    for k in range(width // LANES):
        at = slice(k * rows, (k + 1) * rows)
        out[:, k * LANES : (k + 1) * LANES] = unit * sum(decode(p[at, :]) for p in pays)
    full = side[...] + tails(pays)
    loss[0, 0] = jnp.max(full) / (2.0 * pairs)


def shards(image_embed, text_embed, pair_index):
    rows, width = image_embed.shape
    n_xl, n_z, n_c, n_y, n_xh = (lax.axis_size(a) for a in ("xl", "z", "c", "y", "xh"))
    n_plane = n_xl * n_y * n_xh
    size = n_plane * rows
    half = n_z * rows
    pairs = size * n_z * n_c
    inv_root = width ** (-0.5)
    shape = jax.ShapeDtypeStruct
    tall = width // LANES * rows + EXTRA

    pair_seen = lax.ppermute(pair_index, "xl", SWAP)
    (copies,) = call(
        copies_body,
        (pltpu.HBM((n_plane, rows, width), BF16),),
        (image_embed,),
        "copies",
        hbm_out=(0,),
        scratch=[pltpu.SemaphoreType.DMA((n_plane,))],
    )
    image = lax.all_to_all(copies, PLANE, 0, 0).reshape(size, width)

    steps = [q if q <= n_z // 4 else q - n_z // 2 for q in range(n_z // 2)]
    far = turn(text_embed, "z", n_z // 2)
    (joined,) = call(
        join_body, (shape((2 * rows, width), BF16),), (text_embed, far), "join", 10**11
    )
    pieces = [joined] + [turn(joined, "z", -q) for q in steps[1:]]
    pieces = pieces + [lax.ppermute(piece, "c", SWAP) for piece in pieces]

    flops = 2 * size * size * width
    pair, row_exp, col_exp, text, row_part, col_part, tops = call(
        functools.partial(score_body, steps, inv_root),
        (
            shape((1, size), F32),
            shape((size, size), F32),
            shape((size, size), F32),
            shape((size, width), BF16),
            shape((1, size + LANES), F32),
            shape((1, size + 2 * LANES), F32),
            shape((2, size), F32),
        ),
        (*pieces, image, pair_index, pair_seen),
        "scores",
        flops,
        2 * size * size,
    )
    def exchange(part, axis, step):
        count = lax.axis_size(axis)
        seen = lax.ppermute(part, axis, [(i, i ^ step) for i in range(count)])
        merge_body = functools.partial(pair_body, axis == "c", size)
        return call(merge_body, (shape(part.shape, F32),), (part, seen), "pair")[0]

    for axis, step in (("c", 1), ("z", 1), ("z", 2), ("z", 4)):
        col_part = exchange(col_part, axis, step)
    for axis, step in (("xl", 1), ("xh", 1), ("y", 1), ("y", 2)):
        row_part = exchange(row_part, axis, step)

    terms, text_own, text_other, image_sent = call(
        functools.partial(grad_body, n_z, inv_root),
        (
            shape((8, LANES), F32),
            pltpu.HBM((half, width), F32),
            pltpu.HBM((half + EXTRA, width), BF16),
            pltpu.HBM((n_plane, tall, LANES), BF16),
        ),
        (col_part, row_part, tops, row_exp, col_exp, text, image, pair),
        "grads",
        2 * flops,
        0,
        hbm_out=(1, 2, 3),
        scratch=[
            pltpu.VMEM((size, size), BF16),
            pltpu.VMEM((n_plane, tall, LANES), BF16),
            pltpu.VMEM((half + EXTRA, width), BF16),
            pltpu.VMEM((half, width), F32),
            pltpu.SemaphoreType.DMA((n_plane + 2,)),
        ],
    )
    image_got = lax.all_to_all(image_sent, PLANE, 0, 0)
    keep, total, *pays = call(
        functools.partial(send_body, steps),
        (shape((2 * rows, width), F32), shape((1, LANES), F32))
        + (shape((2 * tall - EXTRA, LANES), BF16),) * len(steps[1:]),
        (text_own, lax.ppermute(text_other, "c", SWAP), terms),
        "send",
        10**10,
        size=1,
    )
    pays = [turn(pay, "z", q) for q, pay in zip(steps[1:], pays)]
    near, far, total = call(
        relay_body,
        (shape((rows, width), F32), shape((tall, LANES), BF16), shape((1, LANES), F32)),
        (keep, total, *pays),
        "relay",
        size=1,
    )
    grad_text, side = call(
        text_sum_body,
        (shape((rows, width), F32), shape((1, LANES), F32)),
        (near, total, terms, turn(far, "z", n_z // 2)),
        "text_sum",
        size=1,
    )
    grad_image, loss = call(
        functools.partial(image_sum_body, pairs),
        (shape((rows, width), F32), shape((1, 1), F32)),
        (image_got, terms, side),
        "image_sum",
        smem_out=1,
    )
    return (loss[0, 0], grad_image, grad_text)


def solution(mesh):
    fine = Mesh(mesh.devices.reshape(2, 8, 2, 4, 2), ("xl", "z", "c", "y", "xh"))
    image_spec = P(("xl", "z", "c", "y", "xh"), None)
    text_spec = P(("y", "xh", "xl", "z", "c"), None)
    return jax.shard_map(
        shards,
        mesh=fine,
        in_specs=(image_spec, text_spec, P(("xl", "z", "c"))),
        out_specs=(P(), image_spec, text_spec),
        check_vma=False,
    )
```

```python
import functools
import math

import jax
import jax.numpy as jnp
from jax import lax
from jax.experimental import pallas as pl
from jax.experimental.pallas import tpu as pltpu
from jax.sharding import Mesh, PartitionSpec as P

PLANE = ("xl", "y", "xh")
SWAP = [(0, 1), (1, 0)]
LANES = 128
EXTRA = 16
F32 = jnp.float32
BF16 = jnp.bfloat16


def turn(x, axis, step):
    count = lax.axis_size(axis)
    return lax.ppermute(x, axis, [(i, (i + step) % count) for i in range(count)])


def merge(parts):
    high = functools.reduce(jnp.maximum, parts)
    return high + jnp.log(sum(jnp.exp(p - high) for p in parts))


def encode(scaled):
    square = scaled * scaled
    fourth = square * square
    return jnp.where(scaled < 0, -fourth, fourth).astype(BF16)


def decode(x):
    wide = x.astype(F32)
    half = lax.rsqrt(jnp.maximum(jnp.abs(wide), 1e-37))
    return wide * half * (half * lax.rsqrt(half))


def split3(value):
    high = value.astype(BF16).astype(F32)
    mid = (value - high).astype(BF16).astype(F32)
    low = value - high - mid
    row = lax.broadcasted_iota(jnp.int32, (EXTRA, LANES), 0)
    parts = jnp.where(row == 0, high, jnp.where(row == 1, mid, jnp.where(row == 2, low, 0.0)))
    return parts.astype(BF16)


def inverse(value):
    return jnp.where(value > 0, 1.0 / value, 1.0)


def to_column(row):
    return jnp.transpose(jnp.broadcast_to(row, (LANES, row.shape[1])))[:, :1]


def to_row(column):
    return jnp.transpose(jnp.broadcast_to(column, (column.shape[0], LANES)))[:1, :]


def call(
    body, outs, args, name, flops=0, exps=0, smem_out=None, size=None, hbm_out=(), scratch=()
):
    if size is None:
        size = sum(math.prod(a.shape) * a.dtype.itemsize for a in (*args, *outs))
    spaces = [pltpu.VMEM] * len(outs)
    if smem_out is not None:
        spaces[smem_out] = pltpu.SMEM
    for i in hbm_out:
        spaces[i] = pltpu.HBM
    return pl.pallas_call(
        body,
        out_shape=outs,
        in_specs=[pl.BlockSpec(memory_space=pltpu.VMEM)] * len(args),
        out_specs=tuple(pl.BlockSpec(memory_space=s) for s in spaces),
        scratch_shapes=scratch,
        cost_estimate=pl.CostEstimate(flops=flops, bytes_accessed=size, transcendentals=exps),
        compiler_params=pltpu.CompilerParams(vmem_limit_bytes=20 * 1024 * 1024),
        name=name,
    )(*args)


def copies_body(source, out, sems):
    copies = [
        pltpu.make_async_copy(source, out.at[i], sems.at[i]) for i in range(out.shape[0])
    ]
    for copy in copies:
        copy.start()
    for copy in copies:
        copy.wait()


def join_body(near, far, out):
    rows = near.shape[0]
    out[:rows, :] = near[...]
    out[rows:, :] = far[...]


def pair_row(mine, seen):
    first = lax.axis_index("xl") == 0
    left = mine[...].astype(F32)[None, :]
    right = seen[...].astype(F32)[None, :]
    return jnp.concatenate(
        [jnp.where(first, left, right), jnp.where(first, right, left)], axis=1
    )


def score_body(steps, inv_root, *refs):
    n_z = 2 * len(steps)
    pieces, refs = refs[:n_z], refs[n_z:]
    image, pair_mine, pair_seen, pair_out, scores, text, row_sent, col_sent = refs
    pair = pair_row(pair_mine, pair_seen)
    pair_out[...] = pair
    rows = pieces[0].shape[0] // 2
    size = image.shape[0]
    ids = labels(n_z, rows)
    found = jnp.zeros((1, size), F32)
    z = lax.axis_index("z")
    high = jnp.zeros(pieces[0].shape, F32)
    for h in range(2):
        for i, q in enumerate(steps):
            piece = pieces[h * n_z // 2 + i]
            high = jnp.maximum(high, jnp.abs(piece[...].astype(F32)))
            for k in range(2):
                start = (h * n_z + lax.rem(z + q + k + n_z, n_z)) * rows
                text[pl.ds(pl.multiple_of(start, 16), rows), :] = piece[
                    k * rows : (k + 1) * rows, :
                ]
    step = 256
    for r in range(0, size, step):
        tile = (
            lax.dot_general(
                image[r : r + step, :],
                text[...],
                (((1,), (1,)), ((), ())),
                preferred_element_type=F32,
            )
            * inv_root
        )
        scores[r : r + step, :] = tile
        top = jnp.max(tile, axis=1, keepdims=True)
        part = top + jnp.log(jnp.sum(jnp.exp(tile - top), axis=1, keepdims=True))
        row_sent[:, r : r + step] = to_row(part)
        hit = to_column(pair[:, r : r + step]) == ids
        found += jnp.sum(jnp.where(hit, tile, 0.0), axis=0, keepdims=True)
    row_sent[:, size:] = jnp.full((1, LANES), jnp.max(high))
    tile = scores[...]
    top = jnp.max(tile, axis=0, keepdims=True)
    col_sent[:, :size] = top + jnp.log(jnp.sum(jnp.exp(tile - top), axis=0, keepdims=True))
    high = jnp.max(jnp.abs(image[...].astype(F32)))
    col_sent[:, size : size + LANES] = jnp.full((1, LANES), high)
    col_sent[:, size + LANES :] = jnp.full((1, LANES), jnp.sum(found))


def labels(n_z, rows):
    half = n_z * rows
    n_xl, n_c, n_xh = (lax.axis_size(a) for a in ("xl", "c", "xh"))
    block = (lax.axis_index("y") * n_xh + lax.axis_index("xh")) * n_xl + lax.axis_index("xl")
    core = lax.axis_index("c")
    slot = lax.broadcasted_iota(jnp.int32, (1, 2 * half), 1)
    own = slot < half
    within = jnp.where(own, slot, slot - half)
    holder = jnp.floor((within.astype(F32) + 0.5) * (1.0 / rows)).astype(jnp.int32)
    ids = ((block * n_z + holder) * n_c + jnp.where(own, core, 1 - core)) * rows
    return (ids + within - holder * rows).astype(F32)


def pair_body(crossed, count, mine, seen, out):
    half = count // 2
    other = seen[:, :count]
    if crossed:
        other = jnp.concatenate([seen[:, half:count], seen[:, :half]], axis=1)
    out[:, :count] = merge([mine[:, :count], other])
    at = slice(count, count + LANES)
    out[:, at] = jnp.maximum(mine[:, at], seen[:, at])
    if mine.shape[1] > count + LANES:
        at = slice(count + LANES, count + 2 * LANES)
        out[:, at] = mine[:, at] + seen[:, at]


def image_body(
    n_z, inv_root, cols, rows_lse, scores, text, pair, grads, sent, terms, kept, held, sems
):
    size = scores.shape[0]
    n_plane = sent.shape[0]
    rows = size // n_plane
    col_lse = cols[:, :size]
    image_max = cols[:, size : size + LANES]
    found = cols[:, size + LANES :]
    ids = labels(n_z, rows)
    row_lse = rows_lse[:, :size]
    text_max = rows_lse[:, size:]
    row_terms = jnp.broadcast_to(jnp.sum(row_lse, axis=1, keepdims=True), (1, LANES))
    col_terms = jnp.sum(col_lse, axis=1, keepdims=True) - 2.0 * found
    terms[...] = jnp.concatenate(
        [row_terms, text_max, image_max, jnp.zeros((5, LANES), F32)], axis=0
    )
    extra = split3(col_terms)
    scale = inverse(text_max[:, :1]) * inv_root
    step = size // 4
    copies = []
    for r in range(0, size, step):
        tile = scores[r : r + step, :]
        probs = 0.5 * (
            jnp.exp(tile - to_column(row_lse[:, r : r + step])) + jnp.exp(tile - col_lse)
        )
        hit = to_column(pair[:, r : r + step]) == ids
        grad = (probs - jnp.where(hit, 1.0, 0.0)).astype(BF16)
        at = pl.ds(r, step)
        kept[at, :] = grad
        sem = sems.at[n_plane + r // step]
        copies.append(pltpu.make_async_copy(kept.at[at], grads.at[at], sem))
        copies[-1].start()
        part = encode(jnp.dot(grad, text[...], preferred_element_type=F32) * scale)
        for p in range(step // rows):
            to = r // rows + p
            for k in range(text.shape[1] // LANES):
                held[to, k * rows : (k + 1) * rows, :] = part[
                    p * rows : (p + 1) * rows, k * LANES : (k + 1) * LANES
                ]
            held[to, k * rows + rows :, :] = extra
            copies.append(pltpu.make_async_copy(held.at[to], sent.at[to], sems.at[to]))
            copies[-1].start()
    for copy in copies:
        copy.wait()


def text_body(inv_root, grads, image, terms_seen, own, other):
    half = own.shape[0]
    scale = inverse(terms_seen[2:3, :1]) * inv_root
    for out, start in ((other, half), (own, 0)):
        part = lax.dot_general(
            grads[:, start : start + half],
            image[...],
            (((0,), (0,)), ((), ())),
            preferred_element_type=F32,
        )
        out[...] = encode(part * scale) if out.dtype == BF16 else part * scale


def pack(pay, blocks, extra):
    rows, width = blocks[0].shape
    at = 0
    for block in blocks:
        coded = encode(block)
        for k in range(width // LANES):
            pay[at : at + rows, :] = coded[:, k * LANES : (k + 1) * LANES]
            at += rows
    pay[at:, :] = extra


def send_body(steps, own, seen, terms, terms_seen, keep, total, *pays):
    n_z = 2 * len(steps)
    rows = keep.shape[0] // 2
    z = lax.axis_index("z")
    row_terms = terms[0:1, :] + terms_seen[0:1, :]
    total[...] = row_terms
    extra = split3(row_terms)
    for i, q in enumerate(steps):
        blocks = []
        for k in range(2):
            start = lax.rem(z + q + k + n_z, n_z) * rows
            at = pl.ds(pl.multiple_of(start, 16), rows)
            blocks.append(own[at, :] + decode(seen[at, :]))
        if i == 0:
            keep[:rows, :] = blocks[0]
            keep[rows:, :] = blocks[1]
        else:
            pack(pays[i - 1], blocks, extra)


def unpack(pays, at, rows, width):
    return jnp.concatenate(
        [
            sum(decode(p[at + k * rows : at + (k + 1) * rows, :]) for p in pays)
            for k in range(width // LANES)
        ],
        axis=1,
    )


def tails(pays):
    tail = sum(p[p.shape[0] - EXTRA :, :].astype(F32) for p in pays)
    return jnp.sum(tail, axis=0, keepdims=True)


def relay_body(keep, total, *refs):
    pays, near, far, total_out = refs[:-3], refs[-3], refs[-2], refs[-1]
    rows, width = near.shape
    near[...] = keep[:rows, :] + unpack(pays, 0, rows, width)
    sums = total[...] + tails(pays)
    total_out[...] = sums
    block = keep[rows:, :] + unpack(pays, rows * width // LANES, rows, width)
    pack(far, [block], split3(sums))


def text_sum_body(near, total, terms, pay, out, side):
    rows, width = out.shape
    unit = terms[2:3, :1]
    unit = jnp.where(unit > 0, unit, 1.0)
    out[...] = unit * (near[...] + unpack([pay], 0, rows, width))
    side[...] = total[...] + tails([pay])


def image_sum_body(pairs, got, terms, side, out, loss):
    rows, width = out.shape
    unit = terms[1:2, :1]
    unit = jnp.where(unit > 0, unit, 1.0)
    pays = [got.at[p] for p in range(got.shape[0])]
    for k in range(width // LANES):
        at = slice(k * rows, (k + 1) * rows)
        out[:, k * LANES : (k + 1) * LANES] = unit * sum(decode(p[at, :]) for p in pays)
    full = side[...] + tails(pays)
    loss[0, 0] = jnp.max(full) / (2.0 * pairs)


def shards(image_embed, text_embed, pair_index):
    rows, width = image_embed.shape
    n_xl, n_z, n_c, n_y, n_xh = (lax.axis_size(a) for a in ("xl", "z", "c", "y", "xh"))
    n_plane = n_xl * n_y * n_xh
    size = n_plane * rows
    half = n_z * rows
    pairs = size * n_z * n_c
    inv_root = width ** (-0.5)
    shape = jax.ShapeDtypeStruct
    tall = width // LANES * rows + EXTRA

    pair_seen = lax.ppermute(pair_index, "xl", SWAP)
    copies = pl.pallas_call(
        copies_body,
        out_shape=shape((n_plane, rows, width), BF16),
        in_specs=[pl.BlockSpec(memory_space=pltpu.VMEM)],
        out_specs=pl.BlockSpec(memory_space=pl.ANY),
        scratch_shapes=[pltpu.SemaphoreType.DMA((n_plane,))],
        name="copies",
    )(image_embed)
    image = lax.all_to_all(copies, PLANE, 0, 0).reshape(size, width)

    steps = [0, n_z // 2] + [q for k in range(2, n_z // 2, 2) for q in (k, -k)]
    far = turn(text_embed, "z", -1)
    (joined,) = call(
        join_body, (shape((2 * rows, width), BF16),), (text_embed, far), "join", 10**11
    )
    pieces = [joined] + [turn(joined, "z", -q) for q in steps[1:]]
    pieces = pieces + [lax.ppermute(piece, "c", SWAP) for piece in pieces]

    flops = 2 * size * size * width
    pair, scores, text, row_part, col_part = call(
        functools.partial(score_body, steps, inv_root),
        (
            shape((1, size), F32),
            shape((size, size), F32),
            shape((size, width), BF16),
            shape((1, size + LANES), F32),
            shape((1, size + 2 * LANES), F32),
        ),
        (*pieces, image, pair_index, pair_seen),
        "scores",
        flops,
        2 * size * size,
    )
    def exchange(part, axis, step):
        count = lax.axis_size(axis)
        seen = lax.ppermute(part, axis, [(i, i ^ step) for i in range(count)])
        merge_body = functools.partial(pair_body, axis == "c", size)
        return call(merge_body, (shape(part.shape, F32),), (part, seen), "pair")[0]

    for axis, step in (("c", 1), ("z", 1), ("z", 2), ("z", 4)):
        col_part = exchange(col_part, axis, step)
    for axis, step in (("xl", 1), ("xh", 1), ("y", 1), ("y", 2)):
        row_part = exchange(row_part, axis, step)

    grads, image_sent, terms = call(
        functools.partial(image_body, n_z, inv_root),
        (
            pltpu.HBM((size, size), BF16),
            pltpu.HBM((n_plane, tall, LANES), BF16),
            shape((8, LANES), F32),
        ),
        (col_part, row_part, scores, text, pair),
        "image_grad",
        flops,
        2 * size * size,
        hbm_out=(0, 1),
        scratch=[
            pltpu.VMEM((size, size), BF16),
            pltpu.VMEM((n_plane, tall, LANES), BF16),
            pltpu.SemaphoreType.DMA((n_plane + 4,)),
        ],
    )
    image_got = lax.all_to_all(image_sent, PLANE, 0, 0)
    terms_seen = lax.ppermute(terms, "c", SWAP)
    text_own, text_other = call(
        functools.partial(text_body, inv_root),
        (shape((half, width), F32), shape((half, width), BF16)),
        (grads, image, terms_seen),
        "text_grad",
        10**11,
        size=1,
    )
    keep, total, *pays = call(
        functools.partial(send_body, steps),
        (shape((2 * rows, width), F32), shape((1, LANES), F32))
        + (shape((2 * tall - EXTRA, LANES), BF16),) * len(steps[1:]),
        (text_own, lax.ppermute(text_other, "c", SWAP), terms, terms_seen),
        "send",
        size=1,
    )
    pays = [turn(pay, "z", q) for q, pay in zip(steps[1:], pays)]
    near, far, total = call(
        relay_body,
        (shape((rows, width), F32), shape((tall, LANES), BF16), shape((1, LANES), F32)),
        (keep, total, *pays),
        "relay",
        size=1,
    )
    grad_text, side = call(
        text_sum_body,
        (shape((rows, width), F32), shape((1, LANES), F32)),
        (near, total, terms, turn(far, "z", 1)),
        "text_sum",
        size=1,
    )
    grad_image, loss = call(
        functools.partial(image_sum_body, pairs),
        (shape((rows, width), F32), shape((1, 1), F32)),
        (image_got, terms, side),
        "image_sum",
        smem_out=1,
    )
    return (loss[0, 0], grad_image, grad_text)


def solution(mesh):
    fine = Mesh(mesh.devices.reshape(2, 8, 2, 4, 2), ("xl", "z", "c", "y", "xh"))
    image_spec = P(("xl", "z", "c", "y", "xh"), None)
    text_spec = P(("y", "xh", "xl", "z", "c"), None)
    return jax.shard_map(
        shards,
        mesh=fine,
        in_specs=(image_spec, text_spec, P(("xl", "z", "c"))),
        out_specs=(P(), image_spec, text_spec),
        check_vma=False,
    )
```

```python
import functools
import math

import jax
import jax.numpy as jnp
from jax import lax
from jax.experimental import pallas as pl
from jax.experimental.pallas import tpu as pltpu
from jax.sharding import Mesh, PartitionSpec as P

AXES = ("xl", "z", "c", "y", "xh")
PLANE = ("xl", "y", "xh")
SWAP = [(0, 1), (1, 0)]
LANES = 128
EXTRA = 16
F32 = jnp.float32
BF16 = jnp.bfloat16


def turn(x, axis, step):
    count = lax.axis_size(axis)
    return lax.ppermute(x, axis, [(i, (i + step) % count) for i in range(count)])


def lean(q, z, count):
    return q * (1 - 2 * (z % 2)) if abs(q) == count // 4 else q


def turn_z(x, q, back):
    count = lax.axis_size("z")
    pairs = [((i + lean(q, i, count)) % count, i) for i in range(count)]
    return lax.ppermute(x, "z", pairs if back else [(b, a) for a, b in pairs])


def turn_both(x, step_z, step_x, step_y):
    sizes = [lax.axis_size(a) for a in AXES]
    n_xl, n_z, n_c, n_y, n_xh = sizes
    n_x = n_xl * n_xh
    pairs = []
    for i in range(math.prod(sizes)):
        rest, xh = divmod(i, n_xh)
        rest, y = divmod(rest, n_y)
        rest, c = divmod(rest, n_c)
        xl, z = divmod(rest, n_z)
        if c == 0:
            if step_z is None:
                continue
            z = (z + step_z) % n_z
        else:
            xh, xl = divmod((xh * n_xl + xl + step_x) % n_x, n_xl)
            y = (y + step_y) % n_y
        pairs.append((i, (((xl * n_z + z) * n_c + c) * n_y + y) * n_xh + xh))
    return lax.ppermute(x, AXES, pairs)


def merge(parts):
    high = functools.reduce(jnp.maximum, parts)
    return high + jnp.log(sum(jnp.exp(p - high) for p in parts))


def encode(scaled):
    square = scaled * scaled
    fourth = square * square
    return jnp.where(scaled < 0, -fourth, fourth).astype(BF16)


def decode(x):
    wide = x.astype(F32)
    half = lax.rsqrt(jnp.maximum(jnp.abs(wide), 1e-37))
    return wide * half * (half * lax.rsqrt(half))


def split3(value):
    high = value.astype(BF16).astype(F32)
    mid = (value - high).astype(BF16).astype(F32)
    low = value - high - mid
    row = lax.broadcasted_iota(jnp.int32, (EXTRA, LANES), 0)
    parts = jnp.where(row == 0, high, jnp.where(row == 1, mid, jnp.where(row == 2, low, 0.0)))
    return parts.astype(BF16)


def inverse(value):
    return jnp.where(value > 0, 1.0 / value, 1.0)


def to_column(row):
    return jnp.transpose(jnp.broadcast_to(row, (LANES, row.shape[1])))[:, :1]


def to_row(column):
    return jnp.transpose(jnp.broadcast_to(column, (column.shape[0], LANES)))[:1, :]


def call(
    body, outs, args, name, flops=0, exps=0, smem_out=None, size=None, hbm_out=(), scratch=()
):
    if size is None:
        size = sum(math.prod(a.shape) * a.dtype.itemsize for a in (*args, *outs))
    spaces = [pltpu.VMEM] * len(outs)
    if smem_out is not None:
        spaces[smem_out] = pltpu.SMEM
    for i in hbm_out:
        spaces[i] = pltpu.HBM
    return pl.pallas_call(
        body,
        out_shape=outs,
        in_specs=[pl.BlockSpec(memory_space=pltpu.VMEM)] * len(args),
        out_specs=tuple(pl.BlockSpec(memory_space=s) for s in spaces),
        scratch_shapes=scratch,
        cost_estimate=pl.CostEstimate(flops=flops, bytes_accessed=size, transcendentals=exps),
        compiler_params=pltpu.CompilerParams(vmem_limit_bytes=20 * 1024 * 1024),
        name=name,
    )(*args)


def copies_body(source, out, sems):
    copies = [
        pltpu.make_async_copy(source, out.at[i], sems.at[i]) for i in range(out.shape[0])
    ]
    for copy in copies:
        copy.start()
    for copy in copies:
        copy.wait()


def join_body(near, far, out):
    rows = near.shape[0]
    out[:rows, :] = near[...]
    out[rows:, :] = far[...]


def pair_row(mine, seen):
    first = lax.axis_index("xl") == 0
    left = mine[...].astype(F32)[None, :]
    right = seen[...].astype(F32)[None, :]
    return jnp.concatenate(
        [jnp.where(first, left, right), jnp.where(first, right, left)], axis=1
    )


def score_body(steps, inv_root, *refs):
    n_z = 2 * len(steps)
    pieces, refs = refs[:n_z], refs[n_z:]
    image, pair_mine, pair_seen, pair_out, scores, text, hold, cross = refs
    pair = pair_row(pair_mine, pair_seen)
    pair_out[...] = pair
    rows = pieces[0].shape[0] // 2
    size = image.shape[0]
    ids = labels(n_z, rows)
    found = jnp.zeros((1, size), F32)
    z = lax.axis_index("z")
    high = jnp.zeros(pieces[0].shape, F32)
    for h in range(2):
        for i, q in enumerate(steps):
            piece = pieces[h * n_z // 2 + i]
            high = jnp.maximum(high, jnp.abs(piece[...].astype(F32)))
            for k in range(2):
                to = lax.rem(z + lean(q, z, n_z) + (k + 2) * n_z // 2, n_z)
                start = (h * n_z + to) * rows
                text[pl.ds(pl.multiple_of(start, 16), rows), :] = piece[
                    k * rows : (k + 1) * rows, :
                ]
    lanes = []
    step = 256
    for r in range(0, size, step):
        tile = (
            lax.dot_general(
                image[r : r + step, :],
                text[...],
                (((1,), (1,)), ((), ())),
                preferred_element_type=F32,
            )
            * inv_root
        )
        scores[r : r + step, :] = tile
        top = jnp.max(tile, axis=1, keepdims=True)
        part = jnp.log(jnp.sum(jnp.exp(tile - top), axis=1, keepdims=True))
        lanes.append(to_row(top + part))
        hit = to_column(pair[:, r : r + step]) == ids
        found += jnp.sum(jnp.where(hit, tile, 0.0), axis=0, keepdims=True)
    tile = scores[...]
    top = jnp.max(tile, axis=0, keepdims=True)
    col = top + jnp.log(jnp.sum(jnp.exp(tile - top), axis=0, keepdims=True))
    image_max = jnp.max(jnp.abs(image[...].astype(F32)))
    zero = jnp.zeros((1, LANES), F32)
    rows_out = jnp.concatenate([*lanes, zero + jnp.max(high), zero], axis=1)
    cols_out = jnp.concatenate([col, zero + image_max, zero + jnp.sum(found)], axis=1)
    first = lax.axis_index("c") == 0
    hold[...] = jnp.where(first, cols_out, rows_out)
    cross[...] = jnp.where(first, rows_out, cols_out)


def crossed(cols):
    half = cols.shape[1] // 2
    return jnp.concatenate([cols[:, half:], cols[:, :half]], axis=1)


def meet_body(hold, seen, out):
    size = hold.shape[1] - 2 * LANES
    first = lax.axis_index("c") == 0
    mine, other = hold[:, :size], seen[:, :size]
    out[:, :size] = jnp.where(first, merge([mine, crossed(other)]), mine)
    out[:, size : 2 * size] = jnp.where(first, 0.0, other)
    high = jnp.maximum(hold[:, size : size + LANES], seen[:, size : size + LANES])
    total = hold[:, size + LANES :] + seen[:, size + LANES :]
    out[:, 2 * size :] = jnp.concatenate([high, total], axis=1)


def round_body(last, mine, one, two, three, *outs):
    size = mine.shape[1] // 2 - LANES
    first = lax.axis_index("c") == 0
    parts = [mine[:, : 2 * size], one[:, : 2 * size]]
    for ref in (two, three):
        part = ref[:, : 2 * size]
        parts.append(jnp.where(first, -1e38, part) if last else part)
    lse = merge(parts)
    refs = (mine, one, two, three)
    at = slice(2 * size, 2 * size + LANES)
    high = functools.reduce(jnp.maximum, [ref[:, at] for ref in refs])
    total = sum(ref[:, 2 * size + LANES :] for ref in refs)
    outs[0][...] = jnp.concatenate([lse, high, total], axis=1)
    if last:
        kept = jnp.where(first, lse[:, :size], lse[:, size:])
        outs[1][...] = jnp.concatenate([kept, high, total], axis=1)


def labels(n_z, rows):
    half = n_z * rows
    n_xl, n_c, n_xh = (lax.axis_size(a) for a in ("xl", "c", "xh"))
    block = (lax.axis_index("y") * n_xh + lax.axis_index("xh")) * n_xl + lax.axis_index("xl")
    core = lax.axis_index("c")
    slot = lax.broadcasted_iota(jnp.int32, (1, 2 * half), 1)
    own = slot < half
    within = jnp.where(own, slot, slot - half)
    holder = jnp.floor((within.astype(F32) + 0.5) * (1.0 / rows)).astype(jnp.int32)
    ids = ((block * n_z + holder) * n_c + jnp.where(own, core, 1 - core)) * rows
    return (ids + within - holder * rows).astype(F32)


def grad_body(n_z, inv_root, *refs):
    mine, seen, scores, text, image, pair = refs[:6]
    terms, own, other, sent, grads, held, crossing, sems = refs[6:]
    size = grads.shape[0]
    half = own.shape[0]
    rows = half // n_z
    _, tall, _ = sent.shape
    ids = labels(n_z, rows)
    first = lax.axis_index("c") == 0
    seen_lse, seen_high = seen[:, :size], seen[:, size : size + LANES]
    mine_lse, mine_high = mine[:, :size], mine[:, 2 * size : 2 * size + LANES]
    col_lse = jnp.where(first, mine_lse, crossed(seen_lse))
    row_lse = jnp.where(first, seen_lse, mine_lse)
    image_max = jnp.where(first, mine_high, seen_high)
    text_max = jnp.where(first, seen_high, mine_high)
    found = jnp.where(first, mine[:, 2 * size + LANES :], seen[:, size + LANES :])
    row_terms = jnp.broadcast_to(jnp.sum(row_lse, axis=1, keepdims=True), (1, LANES))
    col_terms = jnp.sum(col_lse, axis=1, keepdims=True) - 2.0 * found
    terms[...] = jnp.concatenate(
        [row_terms, text_max, image_max, jnp.zeros((5, LANES), F32)], axis=0
    )
    row_column = to_column(row_lse)
    pair_column = to_column(pair[...])
    extra = split3(col_terms)
    scale = inverse(text_max[:, :1]) * inv_root
    step = size // 4
    copies = []
    for r in range(0, size, step):
        at = slice(r, r + step)
        tile = scores[at, :]
        probs = 0.5 * (jnp.exp(tile - row_column[at, :]) + jnp.exp(tile - col_lse))
        grad = (probs - jnp.where(pair_column[at, :] == ids, 1.0, 0.0)).astype(BF16)
        grads[at, :] = grad
        part = encode(jnp.dot(grad, text[...], preferred_element_type=F32) * scale)
        for p in range(step // rows):
            to = r // rows + p
            for k in range(text.shape[1] // LANES):
                held[to, k * rows : (k + 1) * rows, :] = part[
                    p * rows : (p + 1) * rows, k * LANES : (k + 1) * LANES
                ]
            held[to, tall - EXTRA :, :] = extra
            copies.append(pltpu.make_async_copy(held.at[to], sent.at[to], sems.at[to]))
            copies[-1].start()
    scale = inverse(image_max[:, :1]) * inv_root
    extra = split3(row_terms)
    crossing[half:, :] = jnp.concatenate([extra] * (own.shape[1] // LANES), axis=1)
    for start in (half, 0):
        part = lax.dot_general(
            grads[:, start : start + half],
            image[...],
            (((0,), (0,)), ((), ())),
            preferred_element_type=F32,
        )
        if start == 0:
            own[...] = encode(part * scale)
        else:
            crossing[:half, :] = encode(part * scale)
            copies.append(pltpu.make_async_copy(crossing, other, sems.at[sent.shape[0]]))
            copies[-1].start()
    for copy in copies:
        copy.wait()


def pack(pay, blocks, extra):
    rows, width = blocks[0].shape
    at = 0
    for block in blocks:
        coded = encode(block)
        for k in range(width // LANES):
            pay[at : at + rows, :] = coded[:, k * LANES : (k + 1) * LANES]
            at += rows
    pay[at:, :] = extra


def send_body(steps, own, seen, terms, keep, total, *pays):
    n_z = 2 * len(steps)
    rows = keep.shape[0] // 2
    z = lax.axis_index("z")
    half = own.shape[0]
    tail = seen[half:, :LANES].astype(F32)
    row_terms = terms[0:1, :] + jnp.sum(tail, axis=0, keepdims=True)
    total[...] = row_terms
    extra = split3(row_terms)
    for i, q in enumerate(steps):
        blocks = []
        for k in range(2):
            to = lax.rem(z + lean(q, z, n_z) + (k + 2) * n_z // 2, n_z)
            start = to * rows
            at = pl.ds(pl.multiple_of(start, 16), rows)
            blocks.append(decode(own[at, :]) + decode(seen[at, :]))
        if i == 0:
            keep[:rows, :] = blocks[0]
            keep[rows:, :] = blocks[1]
        else:
            pack(pays[i - 1], blocks, extra)


def unpack(pays, at, rows, width):
    return jnp.concatenate(
        [
            sum(decode(p[at + k * rows : at + (k + 1) * rows, :]) for p in pays)
            for k in range(width // LANES)
        ],
        axis=1,
    )


def tails(pays):
    tail = sum(p[p.shape[0] - EXTRA :, :].astype(F32) for p in pays)
    return jnp.sum(tail, axis=0, keepdims=True)


def relay_body(keep, total, *refs):
    pays, near, far, total_out = refs[:-3], refs[-3], refs[-2], refs[-1]
    rows, width = near.shape
    near[...] = keep[:rows, :] + unpack(pays, 0, rows, width)
    sums = total[...] + tails(pays)
    total_out[...] = sums
    block = keep[rows:, :] + unpack(pays, rows * width // LANES, rows, width)
    pack(far, [block], split3(sums))


def text_sum_body(near, total, terms, pay, out, side):
    rows, width = out.shape
    unit = terms[2:3, :1]
    unit = jnp.where(unit > 0, unit, 1.0)
    out[...] = unit * (near[...] + unpack([pay], 0, rows, width))
    side[...] = total[...] + tails([pay])


def image_sum_body(pairs, got, terms, side, out, loss):
    rows, width = out.shape
    unit = terms[1:2, :1]
    unit = jnp.where(unit > 0, unit, 1.0)
    pays = [got.at[p] for p in range(got.shape[0])]
    for k in range(width // LANES):
        at = slice(k * rows, (k + 1) * rows)
        out[:, k * LANES : (k + 1) * LANES] = unit * sum(decode(p[at, :]) for p in pays)
    full = side[...] + tails(pays)
    loss[0, 0] = jnp.max(full) / (2.0 * pairs)


def shards(image_embed, text_embed, pair_index):
    rows, width = image_embed.shape
    n_xl, n_z, n_c, n_y, n_xh = (lax.axis_size(a) for a in ("xl", "z", "c", "y", "xh"))
    n_plane = n_xl * n_y * n_xh
    size = n_plane * rows
    half = n_z * rows
    pairs = size * n_z * n_c
    inv_root = width ** (-0.5)
    shape = jax.ShapeDtypeStruct
    tall = width // LANES * rows + EXTRA

    pair_seen = lax.ppermute(pair_index, "xl", SWAP)
    (copies,) = call(
        copies_body,
        (pltpu.HBM((n_plane, rows, width), BF16),),
        (image_embed,),
        "copies",
        hbm_out=(0,),
        scratch=[pltpu.SemaphoreType.DMA((n_plane,))],
    )
    image = lax.all_to_all(copies, PLANE, 0, 0).reshape(size, width)

    steps = [q if q <= n_z // 4 else q - n_z // 2 for q in range(n_z // 2)]
    far = turn(text_embed, "z", n_z // 2)
    (joined,) = call(
        join_body, (shape((2 * rows, width), BF16),), (text_embed, far), "join", 10**11
    )
    pieces = [joined] + [turn_z(joined, q, True) for q in steps[1:]]
    pieces = pieces + [lax.ppermute(piece, "c", SWAP) for piece in pieces]

    flops = 2 * size * size * width
    pair, scores, text, hold, cross = call(
        functools.partial(score_body, steps, inv_root),
        (
            shape((1, size), F32),
            shape((size, size), F32),
            shape((size, width), BF16),
            shape((1, size + 2 * LANES), F32),
            shape((1, size + 2 * LANES), F32),
        ),
        (*pieces, image, pair_index, pair_seen),
        "scores",
        flops,
        2 * size * size,
    )
    full = shape((1, 2 * size + 2 * LANES), F32)
    (stats,) = call(meet_body, (full,), (hold, lax.ppermute(cross, "c", SWAP)), "meet")
    around = [turn_both(stats, q, q, 0) for q in (1, -1, 2)]
    (stats,) = call(functools.partial(round_body, False), (full,), (stats, *around), "round")
    far_z = (n_z // 2, None, None)
    around = [turn_both(stats, f, 0, q) for f, q in zip(far_z, (1, -1, 2))]
    stats, cross = call(
        functools.partial(round_body, True), (full, shape(cross.shape, F32)), (stats, *around), "last"
    )
    seen = lax.ppermute(cross, "c", SWAP)

    terms, text_own, text_other, image_sent = call(
        functools.partial(grad_body, n_z, inv_root),
        (
            shape((8, LANES), F32),
            shape((half, width), BF16),
            pltpu.HBM((half + EXTRA, width), BF16),
            pltpu.HBM((n_plane, tall, LANES), BF16),
        ),
        (stats, seen, scores, text, image, pair),
        "grads",
        2 * flops,
        2 * size * size,
        hbm_out=(2, 3),
        scratch=[
            pltpu.VMEM((size, size), BF16),
            pltpu.VMEM((n_plane, tall, LANES), BF16),
            pltpu.VMEM((half + EXTRA, width), BF16),
            pltpu.SemaphoreType.DMA((n_plane + 1,)),
        ],
    )
    image_got = lax.all_to_all(image_sent, PLANE, 0, 0)
    keep, total, *pays = call(
        functools.partial(send_body, steps),
        (shape((2 * rows, width), F32), shape((1, LANES), F32))
        + (shape((2 * tall - EXTRA, LANES), BF16),) * len(steps[1:]),
        (text_own, lax.ppermute(text_other, "c", SWAP), terms),
        "send",
        10**10,
        size=1,
    )
    pays = [turn_z(pay, q, False) for q, pay in zip(steps[1:], pays)]
    near, far, total = call(
        relay_body,
        (shape((rows, width), F32), shape((tall, LANES), BF16), shape((1, LANES), F32)),
        (keep, total, *pays),
        "relay",
        size=1,
    )
    grad_text, side = call(
        text_sum_body,
        (shape((rows, width), F32), shape((1, LANES), F32)),
        (near, total, terms, turn(far, "z", n_z // 2)),
        "text_sum",
        size=1,
    )
    grad_image, loss = call(
        functools.partial(image_sum_body, pairs),
        (shape((rows, width), F32), shape((1, 1), F32)),
        (image_got, terms, side),
        "image_sum",
        smem_out=1,
    )
    return (loss[0, 0], grad_image, grad_text)


def solution(mesh):
    fine = Mesh(mesh.devices.reshape(2, 8, 2, 4, 2), ("xl", "z", "c", "y", "xh"))
    image_spec = P(("xl", "z", "c", "y", "xh"), None)
    text_spec = P(("y", "xh", "xl", "z", "c"), None)
    return jax.shard_map(
        shards,
        mesh=fine,
        in_specs=(image_spec, text_spec, P(("xl", "z", "c"))),
        out_specs=(P(), image_spec, text_spec),
        check_vma=False,
    )
```

```python
import functools
import math

import jax
import jax.numpy as jnp
from jax import lax
from jax.experimental import pallas as pl
from jax.experimental.pallas import tpu as pltpu
from jax.sharding import Mesh, PartitionSpec as P

AXES = ("xl", "z", "c", "y", "xh")
PLANE = ("xl", "y", "xh")
SWAP = [(0, 1), (1, 0)]
LANES = 128
EXTRA = 16
F32 = jnp.float32
BF16 = jnp.bfloat16


def turn(x, axis, step):
    count = lax.axis_size(axis)
    return lax.ppermute(x, axis, [(i, (i + step) % count) for i in range(count)])


def lean(q, z, count):
    return q * (1 - 2 * (z % 2)) if abs(q) == count // 4 else q


def turn_z(x, q, back):
    count = lax.axis_size("z")
    pairs = [((i + lean(q, i, count)) % count, i) for i in range(count)]
    return lax.ppermute(x, "z", pairs if back else [(b, a) for a, b in pairs])


def turn_both(x, step_z, step_x, step_y):
    sizes = [lax.axis_size(a) for a in AXES]
    n_xl, n_z, n_c, n_y, n_xh = sizes
    n_x = n_xl * n_xh
    pairs = []
    for i in range(math.prod(sizes)):
        rest, xh = divmod(i, n_xh)
        rest, y = divmod(rest, n_y)
        rest, c = divmod(rest, n_c)
        xl, z = divmod(rest, n_z)
        if c == 0:
            if step_z is None:
                continue
            z = (z + step_z) % n_z
        else:
            xh, xl = divmod((xh * n_xl + xl + step_x) % n_x, n_xl)
            y = (y + step_y) % n_y
        pairs.append((i, (((xl * n_z + z) * n_c + c) * n_y + y) * n_xh + xh))
    return lax.ppermute(x, AXES, pairs)


def merge(parts):
    high = functools.reduce(jnp.maximum, parts)
    return high + jnp.log(sum(jnp.exp(p - high) for p in parts))


def encode(scaled):
    square = scaled * scaled
    fourth = square * square
    return jnp.where(scaled < 0, -fourth, fourth).astype(BF16)


def decode(x):
    wide = x.astype(F32)
    half = lax.rsqrt(jnp.maximum(jnp.abs(wide), 1e-37))
    return wide * half * (half * lax.rsqrt(half))


def split3(value):
    high = value.astype(BF16).astype(F32)
    mid = (value - high).astype(BF16).astype(F32)
    low = value - high - mid
    row = lax.broadcasted_iota(jnp.int32, (EXTRA, LANES), 0)
    parts = jnp.where(row == 0, high, jnp.where(row == 1, mid, jnp.where(row == 2, low, 0.0)))
    return parts.astype(BF16)


def inverse(value):
    return jnp.where(value > 0, 1.0 / value, 1.0)


def to_column(row):
    return jnp.transpose(jnp.broadcast_to(row, (LANES, row.shape[1])))[:, :1]


def to_row(column):
    return jnp.transpose(jnp.broadcast_to(column, (column.shape[0], LANES)))[:1, :]


def call(
    body, outs, args, name, flops=0, exps=0, smem_out=None, size=None, hbm_out=(), scratch=()
):
    if size is None:
        size = sum(math.prod(a.shape) * a.dtype.itemsize for a in (*args, *outs))
    spaces = [pltpu.VMEM] * len(outs)
    if smem_out is not None:
        spaces[smem_out] = pltpu.SMEM
    for i in hbm_out:
        spaces[i] = pltpu.HBM
    return pl.pallas_call(
        body,
        out_shape=outs,
        in_specs=[pl.BlockSpec(memory_space=pltpu.VMEM)] * len(args),
        out_specs=tuple(pl.BlockSpec(memory_space=s) for s in spaces),
        scratch_shapes=scratch,
        cost_estimate=pl.CostEstimate(flops=flops, bytes_accessed=size, transcendentals=exps),
        compiler_params=pltpu.CompilerParams(vmem_limit_bytes=20 * 1024 * 1024),
        name=name,
    )(*args)


def copies_body(source, out, sems):
    copies = [
        pltpu.make_async_copy(source, out.at[i], sems.at[i]) for i in range(out.shape[0])
    ]
    for copy in copies:
        copy.start()
    for copy in copies:
        copy.wait()


def join_body(near, far, out):
    rows = near.shape[0]
    out[:rows, :] = near[...]
    out[rows:, :] = far[...]


def pair_row(mine, seen):
    first = lax.axis_index("xl") == 0
    left = mine[...].astype(F32)[None, :]
    right = seen[...].astype(F32)[None, :]
    return jnp.concatenate(
        [jnp.where(first, left, right), jnp.where(first, right, left)], axis=1
    )


def score_body(steps, inv_root, *refs):
    n_z = 2 * len(steps)
    pieces, refs = refs[:n_z], refs[n_z:]
    image, pair_mine, pair_seen, pair_out, scores, text, hold, cross = refs
    pair = pair_row(pair_mine, pair_seen)
    pair_out[...] = pair
    rows = pieces[0].shape[0] // 2
    size = image.shape[0]
    ids = labels(n_z, rows)
    found = jnp.zeros((1, size), F32)
    z = lax.axis_index("z")
    high = jnp.zeros(pieces[0].shape, F32)
    for h in range(2):
        for i, q in enumerate(steps):
            piece = pieces[h * n_z // 2 + i]
            high = jnp.maximum(high, jnp.abs(piece[...].astype(F32)))
            for k in range(2):
                to = lax.rem(z + lean(q, z, n_z) + (k + 2) * n_z // 2, n_z)
                start = (h * n_z + to) * rows
                text[pl.ds(pl.multiple_of(start, 16), rows), :] = piece[
                    k * rows : (k + 1) * rows, :
                ]
    lanes = []
    step = 256
    for r in range(0, size, step):
        tile = (
            lax.dot_general(
                image[r : r + step, :],
                text[...],
                (((1,), (1,)), ((), ())),
                preferred_element_type=F32,
            )
            * inv_root
        )
        scores[r : r + step, :] = tile
        top = jnp.max(tile, axis=1, keepdims=True)
        part = jnp.log(jnp.sum(jnp.exp(tile - top), axis=1, keepdims=True))
        lanes.append(to_row(top + part))
        hit = to_column(pair[:, r : r + step]) == ids
        found += jnp.sum(jnp.where(hit, tile, 0.0), axis=0, keepdims=True)
    tile = scores[...]
    top = jnp.max(tile, axis=0, keepdims=True)
    col = top + jnp.log(jnp.sum(jnp.exp(tile - top), axis=0, keepdims=True))
    image_max = jnp.max(jnp.abs(image[...].astype(F32)))
    zero = jnp.zeros((1, LANES), F32)
    rows_out = jnp.concatenate([*lanes, zero + jnp.max(high), zero], axis=1)
    cols_out = jnp.concatenate([col, zero + image_max, zero + jnp.sum(found)], axis=1)
    first = lax.axis_index("c") == 0
    hold[...] = jnp.where(first, cols_out, rows_out)
    cross[...] = jnp.where(first, rows_out, cols_out)


def crossed(cols):
    half = cols.shape[1] // 2
    return jnp.concatenate([cols[:, half:], cols[:, :half]], axis=1)


def meet_body(hold, seen, out):
    size = hold.shape[1] - 2 * LANES
    first = lax.axis_index("c") == 0
    mine, other = hold[:, :size], seen[:, :size]
    out[:, :size] = jnp.where(first, merge([mine, crossed(other)]), mine)
    out[:, size : 2 * size] = jnp.where(first, 0.0, other)
    high = jnp.maximum(hold[:, size : size + LANES], seen[:, size : size + LANES])
    total = hold[:, size + LANES :] + seen[:, size + LANES :]
    out[:, 2 * size :] = jnp.concatenate([high, total], axis=1)


def round_body(last, mine, one, two, three, *outs):
    size = mine.shape[1] // 2 - LANES
    first = lax.axis_index("c") == 0
    parts = [mine[:, : 2 * size], one[:, : 2 * size]]
    for ref in (two, three):
        part = ref[:, : 2 * size]
        parts.append(jnp.where(first, -1e38, part) if last else part)
    lse = merge(parts)
    refs = (mine, one, two, three)
    at = slice(2 * size, 2 * size + LANES)
    high = functools.reduce(jnp.maximum, [ref[:, at] for ref in refs])
    total = sum(ref[:, 2 * size + LANES :] for ref in refs)
    outs[0][...] = jnp.concatenate([lse, high, total], axis=1)
    if last:
        kept = jnp.where(first, lse[:, :size], lse[:, size:])
        outs[1][...] = jnp.concatenate([kept, high, total], axis=1)


def labels(n_z, rows):
    half = n_z * rows
    n_xl, n_c, n_xh = (lax.axis_size(a) for a in ("xl", "c", "xh"))
    block = (lax.axis_index("y") * n_xh + lax.axis_index("xh")) * n_xl + lax.axis_index("xl")
    core = lax.axis_index("c")
    slot = lax.broadcasted_iota(jnp.int32, (1, 2 * half), 1)
    own = slot < half
    within = jnp.where(own, slot, slot - half)
    holder = jnp.floor((within.astype(F32) + 0.5) * (1.0 / rows)).astype(jnp.int32)
    ids = ((block * n_z + holder) * n_c + jnp.where(own, core, 1 - core)) * rows
    return (ids + within - holder * rows).astype(F32)


def image_body(n_z, inv_root, *refs):
    mine, seen, scores, text, pair = refs[:5]
    terms, grads, sent, kept, held, sems = refs[5:]
    size = scores.shape[0]
    n_plane, tall, _ = sent.shape
    rows = size // n_plane
    ids = labels(n_z, rows)
    first = lax.axis_index("c") == 0
    seen_lse, seen_high = seen[:, :size], seen[:, size : size + LANES]
    mine_lse, mine_high = mine[:, :size], mine[:, 2 * size : 2 * size + LANES]
    col_lse = jnp.where(first, mine_lse, crossed(seen_lse))
    row_lse = jnp.where(first, seen_lse, mine_lse)
    image_max = jnp.where(first, mine_high, seen_high)
    text_max = jnp.where(first, seen_high, mine_high)
    found = jnp.where(first, mine[:, 2 * size + LANES :], seen[:, size + LANES :])
    row_terms = jnp.broadcast_to(jnp.sum(row_lse, axis=1, keepdims=True), (1, LANES))
    col_terms = jnp.sum(col_lse, axis=1, keepdims=True) - 2.0 * found
    terms[...] = jnp.concatenate(
        [row_terms, text_max, image_max, jnp.zeros((5, LANES), F32)], axis=0
    )
    row_column = to_column(row_lse)
    pair_column = to_column(pair[...])
    extra = split3(col_terms)
    scale = inverse(text_max[:, :1]) * inv_root
    step = size // 4
    copies = []
    for r in range(0, size, step):
        at = pl.ds(r, step)
        tile = scores[at, :]
        probs = 0.5 * (jnp.exp(tile - row_column[r : r + step, :]) + jnp.exp(tile - col_lse))
        hit = pair_column[r : r + step, :] == ids
        grad = (probs - jnp.where(hit, 1.0, 0.0)).astype(BF16)
        kept[at, :] = grad
        sem = sems.at[n_plane + r // step]
        copies.append(pltpu.make_async_copy(kept.at[at], grads.at[at], sem))
        copies[-1].start()
        part = encode(jnp.dot(grad, text[...], preferred_element_type=F32) * scale)
        for p in range(step // rows):
            to = r // rows + p
            for k in range(text.shape[1] // LANES):
                held[to, k * rows : (k + 1) * rows, :] = part[
                    p * rows : (p + 1) * rows, k * LANES : (k + 1) * LANES
                ]
            held[to, tall - EXTRA :, :] = extra
            copies.append(pltpu.make_async_copy(held.at[to], sent.at[to], sems.at[to]))
            copies[-1].start()
    for copy in copies:
        copy.wait()


def text_body(inv_root, grads, image, terms, terms_seen, own, other):
    half = own.shape[0]
    scale = inverse(terms_seen[2:3, :1]) * inv_root
    for out, start in ((other, half), (own, 0)):
        part = lax.dot_general(
            grads[:, start : start + half],
            image[...],
            (((0,), (0,)), ((), ())),
            preferred_element_type=F32,
        )
        out[:half, :] = encode(part * scale) if out.dtype == BF16 else part * scale


def pack(pay, blocks, extra):
    rows, width = blocks[0].shape
    at = 0
    for block in blocks:
        coded = encode(block)
        for k in range(width // LANES):
            pay[at : at + rows, :] = coded[:, k * LANES : (k + 1) * LANES]
            at += rows
    pay[at:, :] = extra


def place(step, n_z, rows):
    slot = lax.rem(lax.axis_index("z") + step + n_z, n_z)
    return pl.ds(pl.multiple_of(slot * rows, 16), rows)


def send_body(n_z, own, seen, terms, terms_seen, sums, total, *pays):
    rows = own.shape[0] // n_z
    row_terms = terms[0:1, :] + terms_seen[0:1, :]
    total[...] = row_terms
    extra = split3(row_terms)
    sums[...] = own[...] + decode(seen[...])
    for pay, step in zip(pays, (n_z // 2, 1 - n_z // 2)):
        pack(pay, [sums[place(step, n_z, rows), :]], extra)


def unpack(pays, at, rows, width):
    return jnp.concatenate(
        [
            sum(decode(p[at + k * rows : at + (k + 1) * rows, :]) for p in pays)
            for k in range(width // LANES)
        ],
        axis=1,
    )


def tails(pays):
    tail = sum(p[p.shape[0] - EXTRA :, :].astype(F32) for p in pays)
    return jnp.sum(tail, axis=0, keepdims=True)


def relay_body(steps, sums, total, *refs):
    n_z = 2 * steps[0][1]
    rows, width = sums.shape[0] // n_z, sums.shape[1]
    count = len(refs) // 2
    for pay, out, (step, _) in zip(refs[:count], refs[count:], steps):
        block = sums[place(step, n_z, rows), :] + unpack([pay], 0, rows, width)
        pack(out, [block], split3(total[...] + tails([pay])))


def text_sum_body(sums, total, terms, up, down, out, side):
    rows, width = out.shape
    n_z = sums.shape[0] // rows
    unit = terms[2:3, :1]
    unit = jnp.where(unit > 0, unit, 1.0)
    out[...] = unit * (sums[place(0, n_z, rows), :] + unpack([up, down], 0, rows, width))
    side[...] = total[...] + tails([up, down])


def image_sum_body(pairs, got, terms, side, out, loss):
    rows, width = out.shape
    unit = terms[1:2, :1]
    unit = jnp.where(unit > 0, unit, 1.0)
    pays = [got.at[p] for p in range(got.shape[0])]
    for k in range(width // LANES):
        at = slice(k * rows, (k + 1) * rows)
        out[:, k * LANES : (k + 1) * LANES] = unit * sum(decode(p[at, :]) for p in pays)
    full = side[...] + tails(pays)
    loss[0, 0] = jnp.max(full) / (2.0 * pairs)


def shards(image_embed, text_embed, pair_index):
    rows, width = image_embed.shape
    n_xl, n_z, n_c, n_y, n_xh = (lax.axis_size(a) for a in ("xl", "z", "c", "y", "xh"))
    n_plane = n_xl * n_y * n_xh
    size = n_plane * rows
    half = n_z * rows
    pairs = size * n_z * n_c
    inv_root = width ** (-0.5)
    shape = jax.ShapeDtypeStruct
    tall = width // LANES * rows + EXTRA

    pair_seen = lax.ppermute(pair_index, "xl", SWAP)
    (copies,) = call(
        copies_body,
        (pltpu.HBM((n_plane, rows, width), BF16),),
        (image_embed,),
        "copies",
        hbm_out=(0,),
        scratch=[pltpu.SemaphoreType.DMA((n_plane,))],
    )
    image = lax.all_to_all(copies, PLANE, 0, 0).reshape(size, width)

    steps = [q if q <= n_z // 4 else q - n_z // 2 for q in range(n_z // 2)]
    far = turn(text_embed, "z", n_z // 2)
    (joined,) = call(
        join_body, (shape((2 * rows, width), BF16),), (text_embed, far), "join", 10**11
    )
    pieces = [joined] + [turn_z(joined, q, True) for q in steps[1:]]
    pieces = pieces + [lax.ppermute(piece, "c", SWAP) for piece in pieces]

    flops = 2 * size * size * width
    pair, scores, text, hold, cross = call(
        functools.partial(score_body, steps, inv_root),
        (
            shape((1, size), F32),
            shape((size, size), F32),
            shape((size, width), BF16),
            shape((1, size + 2 * LANES), F32),
            shape((1, size + 2 * LANES), F32),
        ),
        (*pieces, image, pair_index, pair_seen),
        "scores",
        flops,
        2 * size * size,
    )
    full = shape((1, 2 * size + 2 * LANES), F32)
    (stats,) = call(meet_body, (full,), (hold, lax.ppermute(cross, "c", SWAP)), "meet")
    around = [turn_both(stats, q, q, 0) for q in (1, -1, 2)]
    (stats,) = call(functools.partial(round_body, False), (full,), (stats, *around), "round")
    far_z = (n_z // 2, None, None)
    around = [turn_both(stats, f, 0, q) for f, q in zip(far_z, (1, -1, 2))]
    stats, cross = call(
        functools.partial(round_body, True), (full, shape(cross.shape, F32)), (stats, *around), "last"
    )
    seen = lax.ppermute(cross, "c", SWAP)

    terms, grads, image_sent = call(
        functools.partial(image_body, n_z, inv_root),
        (
            shape((8, LANES), F32),
            pltpu.HBM((size, size), BF16),
            pltpu.HBM((n_plane, tall, LANES), BF16),
        ),
        (stats, seen, scores, text, pair),
        "image_grad",
        flops,
        2 * size * size,
        hbm_out=(1, 2),
        scratch=[
            pltpu.VMEM((size, size), BF16),
            pltpu.VMEM((n_plane, tall, LANES), BF16),
            pltpu.SemaphoreType.DMA((n_plane + 4,)),
        ],
    )
    image_got = lax.all_to_all(image_sent, PLANE, 0, 0)
    terms_seen = lax.ppermute(terms, "c", SWAP)
    text_own, text_other = call(
        functools.partial(text_body, inv_root),
        (shape((half, width), F32), shape((half, width), BF16)),
        (grads, image, terms, terms_seen),
        "text_grad",
        10**11,
        size=1,
    )
    pay_shape = shape((tall, LANES), BF16)
    sums, total, up, down = call(
        functools.partial(send_body, n_z),
        (shape((half, width), F32), shape((1, LANES), F32), pay_shape, pay_shape),
        (text_own, lax.ppermute(text_other, "c", SWAP), terms, terms_seen),
        "send",
        size=1,
    )
    up, down = turn(up, "z", 1), turn(down, "z", -1)
    for left in range(n_z // 2 - 1, 0, -1):
        hops = [(left, n_z // 2), (1 - left, n_z // 2)][: 2 if left > 1 else 1]
        moved = call(
            functools.partial(relay_body, hops),
            (pay_shape,) * len(hops),
            (sums, total, up, down)[: 2 + len(hops)],
            "relay",
            size=1,
        )
        up = turn(moved[0], "z", 1)
        if left > 1:
            down = turn(moved[1], "z", -1)
    grad_text, side = call(
        text_sum_body,
        (shape((rows, width), F32), shape((1, LANES), F32)),
        (sums, total, terms, up, down),
        "text_sum",
        size=1,
    )
    grad_image, loss = call(
        functools.partial(image_sum_body, pairs),
        (shape((rows, width), F32), shape((1, 1), F32)),
        (image_got, terms, side),
        "image_sum",
        smem_out=1,
    )
    return (loss[0, 0], grad_image, grad_text)


def solution(mesh):
    fine = Mesh(mesh.devices.reshape(2, 8, 2, 4, 2), ("xl", "z", "c", "y", "xh"))
    image_spec = P(("xl", "z", "c", "y", "xh"), None)
    text_spec = P(("y", "xh", "xl", "z", "c"), None)
    return jax.shard_map(
        shards,
        mesh=fine,
        in_specs=(image_spec, text_spec, P(("xl", "z", "c"))),
        out_specs=(P(), image_spec, text_spec),
        check_vma=False,
    )
```

```python
import functools
import math

import jax
import jax.numpy as jnp
from jax import lax
from jax.experimental import pallas as pl
from jax.experimental.pallas import tpu as pltpu
from jax.sharding import Mesh, PartitionSpec as P

AXES = ("xl", "z", "c", "y", "xh")
PLANE = ("xl", "y", "xh")
SWAP = [(0, 1), (1, 0)]
LANES = 128
EXTRA = 16
F32 = jnp.float32
BF16 = jnp.bfloat16


def turn(x, axis, step):
    count = lax.axis_size(axis)
    return lax.ppermute(x, axis, [(i, (i + step) % count) for i in range(count)])


def lean(q, z, count):
    return q * (1 - 2 * (z % 2)) if abs(q) == count // 4 else q


def turn_z(x, q, back):
    count = lax.axis_size("z")
    pairs = [((i + lean(q, i, count)) % count, i) for i in range(count)]
    return lax.ppermute(x, "z", pairs if back else [(b, a) for a, b in pairs])


def turn_both(x, step_z, step_x, step_y):
    sizes = [lax.axis_size(a) for a in AXES]
    n_xl, n_z, n_c, n_y, n_xh = sizes
    n_x = n_xl * n_xh
    pairs = []
    for i in range(math.prod(sizes)):
        rest, xh = divmod(i, n_xh)
        rest, y = divmod(rest, n_y)
        rest, c = divmod(rest, n_c)
        xl, z = divmod(rest, n_z)
        if c == 0:
            if step_z is None:
                continue
            z = (z + step_z) % n_z
        else:
            xh, xl = divmod((xh * n_xl + xl + step_x) % n_x, n_xl)
            y = (y + step_y) % n_y
        pairs.append((i, (((xl * n_z + z) * n_c + c) * n_y + y) * n_xh + xh))
    return lax.ppermute(x, AXES, pairs)


def merge(parts):
    high = functools.reduce(jnp.maximum, parts)
    return high + jnp.log(sum(jnp.exp(p - high) for p in parts))


def encode(scaled):
    return ((scaled * scaled) * (scaled * jnp.abs(scaled))).astype(BF16)


def decode(x):
    wide = x.astype(F32)
    half = lax.rsqrt(jnp.maximum(jnp.abs(wide), 1e-37))
    return wide * half * (half * lax.rsqrt(half))


def split3(value):
    high = value.astype(BF16).astype(F32)
    mid = (value - high).astype(BF16).astype(F32)
    low = value - high - mid
    row = lax.broadcasted_iota(jnp.int32, (EXTRA, LANES), 0)
    parts = jnp.where(row == 0, high, jnp.where(row == 1, mid, jnp.where(row == 2, low, 0.0)))
    return parts.astype(BF16)


def inverse(value):
    return jnp.where(value > 0, 1.0 / value, 1.0)


def to_column(row):
    return jnp.transpose(jnp.broadcast_to(row, (LANES, row.shape[1])))[:, :1]


def to_row(column):
    return jnp.transpose(jnp.broadcast_to(column, (column.shape[0], LANES)))[:1, :]


def call(
    body, outs, args, name, flops=0, exps=0, smem_out=None, size=None, hbm_out=(), scratch=()
):
    if size is None:
        size = sum(math.prod(a.shape) * a.dtype.itemsize for a in (*args, *outs))
    spaces = [pltpu.VMEM] * len(outs)
    if smem_out is not None:
        spaces[smem_out] = pltpu.SMEM
    for i in hbm_out:
        spaces[i] = pltpu.HBM
    return pl.pallas_call(
        body,
        out_shape=outs,
        in_specs=[pl.BlockSpec(memory_space=pltpu.VMEM)] * len(args),
        out_specs=tuple(pl.BlockSpec(memory_space=s) for s in spaces),
        scratch_shapes=scratch,
        cost_estimate=pl.CostEstimate(flops=flops, bytes_accessed=size, transcendentals=exps),
        compiler_params=pltpu.CompilerParams(vmem_limit_bytes=20 * 1024 * 1024),
        name=name,
    )(*args)


def copies_body(source, out, sems):
    copies = [
        pltpu.make_async_copy(source, out.at[i], sems.at[i]) for i in range(out.shape[0])
    ]
    for copy in copies:
        copy.start()
    for copy in copies:
        copy.wait()


def join_body(near, far, out):
    rows = near.shape[0]
    out[:rows, :] = near[...]
    out[rows:, :] = far[...]


def pair_row(mine, seen):
    first = lax.axis_index("xl") == 0
    left = mine[...].astype(F32)[None, :]
    right = seen[...].astype(F32)[None, :]
    return jnp.concatenate(
        [jnp.where(first, left, right), jnp.where(first, right, left)], axis=1
    )


def score_body(steps, inv_root, *refs):
    n_z = 2 * len(steps)
    pieces, refs = refs[:n_z], refs[n_z:]
    image, pair_mine, pair_seen, pair_out, scores, text, hold, cross = refs
    pair = pair_row(pair_mine, pair_seen)
    pair_out[...] = pair
    rows = pieces[0].shape[0] // 2
    size = image.shape[0]
    ids = labels(n_z, rows)
    found = jnp.zeros((1, size), F32)
    z = lax.axis_index("z")
    high = jnp.zeros(pieces[0].shape, F32)
    for h in range(2):
        for i, q in enumerate(steps):
            piece = pieces[h * n_z // 2 + i]
            high = jnp.maximum(high, jnp.abs(piece[...].astype(F32)))
            for k in range(2):
                to = lax.rem(z + lean(q, z, n_z) + (k + 2) * n_z // 2, n_z)
                start = (h * n_z + to) * rows
                text[pl.ds(pl.multiple_of(start, 16), rows), :] = piece[
                    k * rows : (k + 1) * rows, :
                ]
    lanes = []
    step = 256
    for r in range(0, size, step):
        tile = (
            lax.dot_general(
                image[r : r + step, :],
                text[...],
                (((1,), (1,)), ((), ())),
                preferred_element_type=F32,
            )
            * inv_root
        )
        scores[r : r + step, :] = tile
        top = jnp.max(tile, axis=1, keepdims=True)
        part = jnp.log(jnp.sum(jnp.exp(tile - top), axis=1, keepdims=True))
        lanes.append(to_row(top + part))
        hit = to_column(pair[:, r : r + step]) == ids
        found += jnp.sum(jnp.where(hit, tile, 0.0), axis=0, keepdims=True)
    tile = scores[...]
    top = jnp.max(tile, axis=0, keepdims=True)
    col = top + jnp.log(jnp.sum(jnp.exp(tile - top), axis=0, keepdims=True))
    image_max = jnp.max(jnp.abs(image[...].astype(F32)))
    zero = jnp.zeros((1, LANES), F32)
    rows_out = jnp.concatenate([*lanes, zero + jnp.max(high), zero], axis=1)
    cols_out = jnp.concatenate([col, zero + image_max, zero + jnp.sum(found)], axis=1)
    first = lax.axis_index("c") == 0
    hold[...] = jnp.where(first, cols_out, rows_out)
    cross[...] = jnp.where(first, rows_out, cols_out)


def crossed(cols):
    half = cols.shape[1] // 2
    return jnp.concatenate([cols[:, half:], cols[:, :half]], axis=1)


def meet_body(hold, seen, out):
    size = hold.shape[1] - 2 * LANES
    first = lax.axis_index("c") == 0
    mine, other = hold[:, :size], seen[:, :size]
    out[:, :size] = jnp.where(first, merge([mine, crossed(other)]), mine)
    out[:, size : 2 * size] = jnp.where(first, 0.0, other)
    high = jnp.maximum(hold[:, size : size + LANES], seen[:, size : size + LANES])
    total = hold[:, size + LANES :] + seen[:, size + LANES :]
    out[:, 2 * size :] = jnp.concatenate([high, total], axis=1)


def round_body(last, mine, one, two, three, *outs):
    size = mine.shape[1] // 2 - LANES
    first = lax.axis_index("c") == 0
    parts = [mine[:, : 2 * size], three[:, : 2 * size]]
    for ref in (one, two):
        part = ref[:, : 2 * size]
        parts.append(jnp.where(first, -1e38, part) if last else part)
    lse = merge(parts)
    refs = (mine, one, two, three)
    at = slice(2 * size, 2 * size + LANES)
    high = functools.reduce(jnp.maximum, [ref[:, at] for ref in refs])
    total = sum(ref[:, 2 * size + LANES :] for ref in refs)
    outs[0][...] = jnp.concatenate([lse, high, total], axis=1)
    if last:
        kept = jnp.where(first, lse[:, :size], lse[:, size:])
        outs[1][...] = jnp.concatenate([kept, high, total], axis=1)


def labels(n_z, rows):
    half = n_z * rows
    n_xl, n_c, n_xh = (lax.axis_size(a) for a in ("xl", "c", "xh"))
    block = (lax.axis_index("y") * n_xh + lax.axis_index("xh")) * n_xl + lax.axis_index("xl")
    core = lax.axis_index("c")
    slot = lax.broadcasted_iota(jnp.int32, (1, 2 * half), 1)
    own = slot < half
    within = jnp.where(own, slot, slot - half)
    holder = jnp.floor((within.astype(F32) + 0.5) * (1.0 / rows)).astype(jnp.int32)
    ids = ((block * n_z + holder) * n_c + jnp.where(own, core, 1 - core)) * rows
    return (ids + within - holder * rows).astype(F32)


def grad_body(n_z, inv_root, *refs):
    mine, seen, scores, text, image, pair = refs[:6]
    terms, own, other, sent, grads, held, crossing, sems = refs[6:]
    size = grads.shape[0]
    half = own.shape[0]
    rows = half // n_z
    _, tall, _ = sent.shape
    ids = labels(n_z, rows)
    first = lax.axis_index("c") == 0
    seen_lse, seen_high = seen[:, :size], seen[:, size : size + LANES]
    mine_lse, mine_high = mine[:, :size], mine[:, 2 * size : 2 * size + LANES]
    col_lse = jnp.where(first, mine_lse, crossed(seen_lse))
    row_lse = jnp.where(first, seen_lse, mine_lse)
    image_max = jnp.where(first, mine_high, seen_high)
    text_max = jnp.where(first, seen_high, mine_high)
    found = jnp.where(first, mine[:, 2 * size + LANES :], seen[:, size + LANES :])
    row_terms = jnp.broadcast_to(jnp.sum(row_lse, axis=1, keepdims=True), (1, LANES))
    col_terms = jnp.sum(col_lse, axis=1, keepdims=True) - 2.0 * found
    terms[...] = jnp.concatenate(
        [row_terms, text_max, image_max, jnp.zeros((5, LANES), F32)], axis=0
    )
    row_column = to_column(row_lse + math.log(2.0))
    col_row = col_lse + math.log(2.0)
    pair_column = to_column(pair[...])
    extra = split3(col_terms)
    scale = inverse(text_max[:, :1]) * inv_root
    step = size // 4
    copies = []
    for r in range(0, size, step):
        at = slice(r, r + step)
        tile = scores[at, :]
        probs = jnp.exp(tile - row_column[at, :]) + jnp.exp(tile - col_row)
        grad = (probs - jnp.where(pair_column[at, :] == ids, 1.0, 0.0)).astype(BF16)
        grads[at, :] = grad
        part = encode(jnp.dot(grad, text[...], preferred_element_type=F32) * scale)
        for p in range(step // rows):
            to = r // rows + p
            for k in range(text.shape[1] // LANES):
                held[to, k * rows : (k + 1) * rows, :] = part[
                    p * rows : (p + 1) * rows, k * LANES : (k + 1) * LANES
                ]
            held[to, tall - EXTRA :, :] = extra
            copies.append(pltpu.make_async_copy(held.at[to], sent.at[to], sems.at[to]))
            copies[-1].start()
    scale = inverse(image_max[:, :1]) * inv_root
    extra = split3(row_terms)
    crossing[half:, :] = jnp.concatenate([extra] * (own.shape[1] // LANES), axis=1)
    for start in (half, 0):
        part = lax.dot_general(
            grads[:, start : start + half],
            image[...],
            (((0,), (0,)), ((), ())),
            preferred_element_type=F32,
        )
        if start == 0:
            own[...] = encode(part * scale)
        else:
            crossing[:half, :] = encode(part * scale)
            copies.append(pltpu.make_async_copy(crossing, other, sems.at[sent.shape[0]]))
            copies[-1].start()
    for copy in copies:
        copy.wait()


def pack(pay, blocks, extra):
    rows, width = blocks[0].shape
    at = 0
    for block in blocks:
        coded = encode(block)
        for k in range(width // LANES):
            pay[at : at + rows, :] = coded[:, k * LANES : (k + 1) * LANES]
            at += rows
    pay[at:, :] = extra


def send_body(steps, own, seen, terms, keep, total, *pays):
    n_z = 2 * len(steps)
    rows = keep.shape[0] // 2
    z = lax.axis_index("z")
    half = own.shape[0]
    tail = seen[half:, :LANES].astype(F32)
    row_terms = terms[0:1, :] + jnp.sum(tail, axis=0, keepdims=True)
    total[...] = row_terms
    extra = split3(row_terms)
    for i, q in enumerate(steps):
        blocks = []
        for k in range(2):
            to = lax.rem(z + lean(q, z, n_z) + (k + 2) * n_z // 2, n_z)
            start = to * rows
            at = pl.ds(pl.multiple_of(start, 16), rows)
            blocks.append(decode(own[at, :]) + decode(seen[at, :]))
        if i == 0:
            keep[:rows, :] = blocks[0]
            keep[rows:, :] = blocks[1]
        else:
            pack(pays[i - 1], blocks, extra)


def unpack(pays, at, rows, width):
    return jnp.concatenate(
        [
            sum(decode(p[at + k * rows : at + (k + 1) * rows, :]) for p in pays)
            for k in range(width // LANES)
        ],
        axis=1,
    )


def tails(pays):
    tail = sum(p[p.shape[0] - EXTRA :, :].astype(F32) for p in pays)
    return jnp.sum(tail, axis=0, keepdims=True)


def relay_body(keep, total, *refs):
    pays, near, far, total_out = refs[:-3], refs[-3], refs[-2], refs[-1]
    rows, width = near.shape
    near[...] = keep[:rows, :] + unpack(pays, 0, rows, width)
    sums = total[...] + tails(pays)
    total_out[...] = sums
    block = keep[rows:, :] + unpack(pays, rows * width // LANES, rows, width)
    pack(far, [block], split3(sums))


def text_sum_body(near, total, terms, pay, out, side):
    rows, width = out.shape
    unit = terms[2:3, :1]
    unit = jnp.where(unit > 0, unit, 1.0)
    out[...] = unit * (near[...] + unpack([pay], 0, rows, width))
    side[...] = total[...] + tails([pay])


def image_sum_body(pairs, got, terms, side, out, loss):
    rows, width = out.shape
    unit = terms[1:2, :1]
    unit = jnp.where(unit > 0, unit, 1.0)
    pays = [got.at[p] for p in range(got.shape[0])]
    for k in range(width // LANES):
        at = slice(k * rows, (k + 1) * rows)
        out[:, k * LANES : (k + 1) * LANES] = unit * sum(decode(p[at, :]) for p in pays)
    full = side[...] + tails(pays)
    loss[0, 0] = jnp.max(full) / (2.0 * pairs)


def shards(image_embed, text_embed, pair_index):
    rows, width = image_embed.shape
    n_xl, n_z, n_c, n_y, n_xh = (lax.axis_size(a) for a in ("xl", "z", "c", "y", "xh"))
    n_plane = n_xl * n_y * n_xh
    size = n_plane * rows
    half = n_z * rows
    pairs = size * n_z * n_c
    inv_root = width ** (-0.5)
    shape = jax.ShapeDtypeStruct
    tall = width // LANES * rows + EXTRA

    pair_seen = lax.ppermute(pair_index, "xl", SWAP)
    (copies,) = call(
        copies_body,
        (pltpu.HBM((n_plane, rows, width), BF16),),
        (image_embed,),
        "copies",
        hbm_out=(0,),
        scratch=[pltpu.SemaphoreType.DMA((n_plane,))],
    )
    image = lax.all_to_all(copies, PLANE, 0, 0).reshape(size, width)

    steps = [q if q <= n_z // 4 else q - n_z // 2 for q in range(n_z // 2)]
    far = turn(text_embed, "z", n_z // 2)
    (joined,) = call(
        join_body, (shape((2 * rows, width), BF16),), (text_embed, far), "join", 10**11
    )
    pieces = [joined] + [turn_z(joined, q, True) for q in steps[1:]]
    pieces = pieces + [lax.ppermute(piece, "c", SWAP) for piece in pieces]

    flops = 2 * size * size * width
    pair, scores, text, hold, cross = call(
        functools.partial(score_body, steps, inv_root),
        (
            shape((1, size), F32),
            shape((size, size), F32),
            shape((size, width), BF16),
            shape((1, size + 2 * LANES), F32),
            shape((1, size + 2 * LANES), F32),
        ),
        (*pieces, image, pair_index, pair_seen),
        "scores",
        flops,
        2 * size * size,
    )
    full = shape((1, 2 * size + 2 * LANES), F32)
    (stats,) = call(meet_body, (full,), (hold, lax.ppermute(cross, "c", SWAP)), "meet")
    around = [turn_both(stats, q, q, 0) for q in (1, -1, 2)]
    (stats,) = call(functools.partial(round_body, False), (full,), (stats, *around), "round")
    far_z = (None, None, n_z // 2)
    around = [turn_both(stats, f, 0, q) for f, q in zip(far_z, (1, -1, 2))]
    stats, cross = call(
        functools.partial(round_body, True), (full, shape(cross.shape, F32)), (stats, *around), "last"
    )
    seen = lax.ppermute(cross, "c", SWAP)

    terms, text_own, text_other, image_sent = call(
        functools.partial(grad_body, n_z, inv_root),
        (
            shape((8, LANES), F32),
            shape((half, width), BF16),
            pltpu.HBM((half + EXTRA, width), BF16),
            pltpu.HBM((n_plane, tall, LANES), BF16),
        ),
        (stats, seen, scores, text, image, pair),
        "grads",
        2 * flops,
        2 * size * size,
        hbm_out=(2, 3),
        scratch=[
            pltpu.VMEM((size, size), BF16),
            pltpu.VMEM((n_plane, tall, LANES), BF16),
            pltpu.VMEM((half + EXTRA, width), BF16),
            pltpu.SemaphoreType.DMA((n_plane + 1,)),
        ],
    )
    image_got = lax.all_to_all(image_sent, PLANE, 0, 0)
    keep, total, *pays = call(
        functools.partial(send_body, steps),
        (shape((2 * rows, width), F32), shape((1, LANES), F32))
        + (shape((2 * tall - EXTRA, LANES), BF16),) * len(steps[1:]),
        (text_own, lax.ppermute(text_other, "c", SWAP), terms),
        "send",
        10**10,
        size=1,
    )
    pays = [turn_z(pay, q, False) for q, pay in zip(steps[1:], pays)]
    near, far, total = call(
        relay_body,
        (shape((rows, width), F32), shape((tall, LANES), BF16), shape((1, LANES), F32)),
        (keep, total, *pays),
        "relay",
        size=1,
    )
    grad_text, side = call(
        text_sum_body,
        (shape((rows, width), F32), shape((1, LANES), F32)),
        (near, total, terms, turn(far, "z", n_z // 2)),
        "text_sum",
        size=1,
    )
    grad_image, loss = call(
        functools.partial(image_sum_body, pairs),
        (shape((rows, width), F32), shape((1, 1), F32)),
        (image_got, terms, side),
        "image_sum",
        smem_out=1,
    )
    return (loss[0, 0], grad_image, grad_text)


def solution(mesh):
    fine = Mesh(mesh.devices.reshape(2, 8, 2, 4, 2), ("xl", "z", "c", "y", "xh"))
    image_spec = P(("xl", "z", "c", "y", "xh"), None)
    text_spec = P(("y", "xh", "xl", "z", "c"), None)
    return jax.shard_map(
        shards,
        mesh=fine,
        in_specs=(image_spec, text_spec, P(("xl", "z", "c"))),
        out_specs=(P(), image_spec, text_spec),
        check_vma=False,
    )
```

```python
import functools
import math

import jax
import jax.numpy as jnp
from jax import lax
from jax.experimental import pallas as pl
from jax.experimental.pallas import tpu as pltpu
from jax.sharding import Mesh, PartitionSpec as P

AXES = ("xl", "z", "c", "y", "xh")
PLANE = ("xl", "y", "xh")
SWAP = [(0, 1), (1, 0)]
LANES = 128
EXTRA = 16
F32 = jnp.float32
BF16 = jnp.bfloat16


def turn(x, axis, step):
    count = lax.axis_size(axis)
    return lax.ppermute(x, axis, [(i, (i + step) % count) for i in range(count)])


def lean(q, z, count):
    return q * (1 - 2 * (z % 2)) if abs(q) == count // 4 else q


def turn_z(x, q, back):
    count = lax.axis_size("z")
    pairs = [((i + lean(q, i, count)) % count, i) for i in range(count)]
    return lax.ppermute(x, "z", pairs if back else [(b, a) for a, b in pairs])


def turn_both(x, step_z, step_x, step_y):
    sizes = [lax.axis_size(a) for a in AXES]
    n_xl, n_z, n_c, n_y, n_xh = sizes
    n_x = n_xl * n_xh
    pairs = []
    for i in range(math.prod(sizes)):
        rest, xh = divmod(i, n_xh)
        rest, y = divmod(rest, n_y)
        rest, c = divmod(rest, n_c)
        xl, z = divmod(rest, n_z)
        if c == 0:
            if step_z is None:
                continue
            z = (z + step_z) % n_z
        else:
            xh, xl = divmod((xh * n_xl + xl + step_x) % n_x, n_xl)
            y = (y + step_y) % n_y
        pairs.append((i, (((xl * n_z + z) * n_c + c) * n_y + y) * n_xh + xh))
    return lax.ppermute(x, AXES, pairs)


def merge(parts):
    high = functools.reduce(jnp.maximum, parts)
    return high + jnp.log2(sum(jnp.exp2(p - high) for p in parts))


def encode(scaled):
    return ((scaled * scaled) * (scaled * jnp.abs(scaled))).astype(BF16)


def decode(x):
    wide = x.astype(F32)
    half = lax.rsqrt(jnp.maximum(jnp.abs(wide), 1e-37))
    return wide * half * (half * lax.rsqrt(half))


def split3(value):
    high = value.astype(BF16).astype(F32)
    mid = (value - high).astype(BF16).astype(F32)
    low = value - high - mid
    row = lax.broadcasted_iota(jnp.int32, (EXTRA, LANES), 0)
    parts = jnp.where(row == 0, high, jnp.where(row == 1, mid, jnp.where(row == 2, low, 0.0)))
    return parts.astype(BF16)


def inverse(value):
    return jnp.where(value > 0, 1.0 / value, 1.0)


def to_column(row):
    return jnp.transpose(jnp.broadcast_to(row, (LANES, row.shape[1])))[:, :1]


def to_row(column):
    return jnp.transpose(jnp.broadcast_to(column, (column.shape[0], LANES)))[:1, :]


def call(
    body, outs, args, name, flops=0, exps=0, smem_out=None, size=None, hbm_out=(), scratch=()
):
    if size is None:
        size = sum(math.prod(a.shape) * a.dtype.itemsize for a in (*args, *outs))
    spaces = [pltpu.VMEM] * len(outs)
    if smem_out is not None:
        spaces[smem_out] = pltpu.SMEM
    for i in hbm_out:
        spaces[i] = pltpu.HBM
    return pl.pallas_call(
        body,
        out_shape=outs,
        in_specs=[pl.BlockSpec(memory_space=pltpu.VMEM)] * len(args),
        out_specs=tuple(pl.BlockSpec(memory_space=s) for s in spaces),
        scratch_shapes=scratch,
        cost_estimate=pl.CostEstimate(flops=flops, bytes_accessed=size, transcendentals=exps),
        compiler_params=pltpu.CompilerParams(vmem_limit_bytes=20 * 1024 * 1024),
        name=name,
    )(*args)


def copies_body(source, out, held, sems):
    count = out.shape[0]
    load = pltpu.make_async_copy(source, held, sems.at[count])
    load.start()
    load.wait()
    copies = [pltpu.make_async_copy(held, out.at[i], sems.at[i]) for i in range(count)]
    for copy in copies:
        copy.start()
    for copy in copies:
        copy.wait()


def join_body(near, far, out):
    rows = near.shape[0]
    out[:rows, :] = near[...]
    out[rows:, :] = far[...]


def pair_row(mine, seen):
    first = lax.axis_index("xl") == 0
    left = mine[...].astype(F32)[None, :]
    right = seen[...].astype(F32)[None, :]
    return jnp.concatenate(
        [jnp.where(first, left, right), jnp.where(first, right, left)], axis=1
    )


def score_body(steps, inv_root, *refs):
    n_z = 2 * len(steps)
    pieces, refs = refs[:n_z], refs[n_z:]
    image, pair_mine, pair_seen, pair_out, scores, text, hold, cross = refs
    pair = pair_row(pair_mine, pair_seen)
    pair_out[...] = pair
    rows = pieces[0].shape[0] // 2
    size = image.shape[0]
    ids = labels(n_z, rows)
    found = jnp.zeros((1, size), F32)
    z = lax.axis_index("z")
    high = jnp.zeros(pieces[0].shape, F32)
    for h in range(2):
        for i, q in enumerate(steps):
            piece = pieces[h * n_z // 2 + i]
            high = jnp.maximum(high, jnp.abs(piece[...].astype(F32)))
            for k in range(2):
                to = lax.rem(z + lean(q, z, n_z) + (k + 2) * n_z // 2, n_z)
                start = (h * n_z + to) * rows
                text[pl.ds(pl.multiple_of(start, 16), rows), :] = piece[
                    k * rows : (k + 1) * rows, :
                ]
    lanes = []
    col_top = jnp.full((1, size), -1e38, F32)
    step = 256
    for r in range(0, size, step):
        tile = (
            lax.dot_general(
                image[r : r + step, :],
                text[...],
                (((1,), (1,)), ((), ())),
                preferred_element_type=F32,
            )
            * (inv_root / math.log(2.0))
        )
        scores[r : r + step, :] = tile
        col_top = jnp.maximum(col_top, jnp.max(tile, axis=0, keepdims=True))
        top = jnp.max(tile, axis=1, keepdims=True)
        part = jnp.log2(jnp.sum(jnp.exp2(tile - top), axis=1, keepdims=True))
        lanes.append(to_row(top + part))
        hit = to_column(pair[:, r : r + step]) == ids
        found += jnp.sum(jnp.where(hit, tile, 0.0), axis=0, keepdims=True)
    mass = jnp.exp2(scores[...] - col_top)
    col = col_top + jnp.log2(jnp.sum(mass, axis=0, keepdims=True))
    image_max = jnp.max(jnp.abs(image[...].astype(F32)))
    zero = jnp.zeros((1, LANES), F32)
    rows_out = jnp.concatenate([*lanes, zero + jnp.max(high), zero], axis=1)
    cols_out = jnp.concatenate([col, zero + image_max, zero + jnp.sum(found)], axis=1)
    first = lax.axis_index("c") == 0
    hold[...] = jnp.where(first, cols_out, rows_out)
    cross[...] = jnp.where(first, rows_out, cols_out)


def crossed(cols):
    half = cols.shape[1] // 2
    return jnp.concatenate([cols[:, half:], cols[:, :half]], axis=1)


def meet_body(hold, seen, out):
    size = hold.shape[1] - 2 * LANES
    first = lax.axis_index("c") == 0
    mine, other = hold[:, :size], seen[:, :size]
    out[:, :size] = jnp.where(first, merge([mine, crossed(other)]), mine)
    out[:, size : 2 * size] = jnp.where(first, 0.0, other)
    high = jnp.maximum(hold[:, size : size + LANES], seen[:, size : size + LANES])
    total = hold[:, size + LANES :] + seen[:, size + LANES :]
    out[:, 2 * size :] = jnp.concatenate([high, total], axis=1)


def round_body(last, mine, one, two, three, *outs):
    size = mine.shape[1] // 2 - LANES
    first = lax.axis_index("c") == 0
    parts = [mine[:, : 2 * size], three[:, : 2 * size]]
    for ref in (one, two):
        part = ref[:, : 2 * size]
        parts.append(jnp.where(first, -1e38, part) if last else part)
    lse = merge(parts)
    refs = (mine, one, two, three)
    at = slice(2 * size, 2 * size + LANES)
    high = functools.reduce(jnp.maximum, [ref[:, at] for ref in refs])
    total = sum(ref[:, 2 * size + LANES :] for ref in refs)
    outs[0][...] = jnp.concatenate([lse, high, total], axis=1)
    if last:
        kept = jnp.where(first, lse[:, :size], lse[:, size:])
        outs[1][...] = jnp.concatenate([kept, high, total], axis=1)


def labels(n_z, rows):
    half = n_z * rows
    n_xl, n_c, n_xh = (lax.axis_size(a) for a in ("xl", "c", "xh"))
    block = (lax.axis_index("y") * n_xh + lax.axis_index("xh")) * n_xl + lax.axis_index("xl")
    core = lax.axis_index("c")
    slot = lax.broadcasted_iota(jnp.int32, (1, 2 * half), 1)
    own = slot < half
    within = jnp.where(own, slot, slot - half)
    holder = jnp.floor((within.astype(F32) + 0.5) * (1.0 / rows)).astype(jnp.int32)
    ids = ((block * n_z + holder) * n_c + jnp.where(own, core, 1 - core)) * rows
    return (ids + within - holder * rows).astype(F32)


def grad_body(n_z, inv_root, *refs):
    mine, seen, scores, text, image, pair = refs[:6]
    terms, own, other, sent, grads, held, crossing, sems = refs[6:]
    size = grads.shape[0]
    half = own.shape[0]
    rows = half // n_z
    _, tall, _ = sent.shape
    ids = labels(n_z, rows)
    first = lax.axis_index("c") == 0
    seen_lse, seen_high = seen[:, :size], seen[:, size : size + LANES]
    mine_lse, mine_high = mine[:, :size], mine[:, 2 * size : 2 * size + LANES]
    col_lse = jnp.where(first, mine_lse, crossed(seen_lse))
    row_lse = jnp.where(first, seen_lse, mine_lse)
    image_max = jnp.where(first, mine_high, seen_high)
    text_max = jnp.where(first, seen_high, mine_high)
    found = jnp.where(first, mine[:, 2 * size + LANES :], seen[:, size + LANES :])
    row_terms = jnp.broadcast_to(jnp.sum(row_lse, axis=1, keepdims=True), (1, LANES))
    col_terms = jnp.sum(col_lse, axis=1, keepdims=True) - 2.0 * found
    terms[...] = jnp.concatenate(
        [row_terms, text_max, image_max, jnp.zeros((5, LANES), F32)], axis=0
    )
    row_column = to_column(row_lse + 1.0)
    col_row = col_lse + 1.0
    pair_column = to_column(pair[...])
    extra = split3(col_terms)
    scale = inverse(text_max[:, :1]) * inv_root
    step = size // 4
    copies = []
    for r in range(0, size, step):
        at = slice(r, r + step)
        tile = scores[at, :]
        probs = jnp.exp2(tile - row_column[at, :]) + jnp.exp2(tile - col_row)
        grad = (probs - jnp.where(pair_column[at, :] == ids, 1.0, 0.0)).astype(BF16)
        grads[at, :] = grad
        part = encode(jnp.dot(grad, text[...], preferred_element_type=F32) * scale)
        for p in range(step // rows):
            to = r // rows + p
            for k in range(text.shape[1] // LANES):
                held[to, k * rows : (k + 1) * rows, :] = part[
                    p * rows : (p + 1) * rows, k * LANES : (k + 1) * LANES
                ]
            held[to, tall - EXTRA :, :] = extra
            copies.append(pltpu.make_async_copy(held.at[to], sent.at[to], sems.at[to]))
            copies[-1].start()
    scale = inverse(image_max[:, :1]) * inv_root
    extra = split3(row_terms)
    crossing[half:, :] = jnp.concatenate([extra] * (own.shape[1] // LANES), axis=1)
    for start in (half, 0):
        part = lax.dot_general(
            grads[:, start : start + half],
            image[...],
            (((0,), (0,)), ((), ())),
            preferred_element_type=F32,
        )
        if start == 0:
            own[...] = encode(part * scale)
        else:
            crossing[:half, :] = encode(part * scale)
            copies.append(pltpu.make_async_copy(crossing, other, sems.at[sent.shape[0]]))
            copies[-1].start()
    for copy in copies:
        copy.wait()


def pack(pay, blocks, extra):
    rows, width = blocks[0].shape
    at = 0
    for block in blocks:
        coded = encode(block)
        for k in range(width // LANES):
            pay[at : at + rows, :] = coded[:, k * LANES : (k + 1) * LANES]
            at += rows
    pay[at:, :] = extra


def send_body(steps, own, seen, terms, keep, total, *pays):
    n_z = 2 * len(steps)
    rows = keep.shape[0] // 2
    z = lax.axis_index("z")
    half = own.shape[0]
    tail = seen[half:, :LANES].astype(F32)
    row_terms = terms[0:1, :] + jnp.sum(tail, axis=0, keepdims=True)
    total[...] = row_terms
    extra = split3(row_terms)
    for i, q in enumerate(steps):
        blocks = []
        for k in range(2):
            to = lax.rem(z + lean(q, z, n_z) + (k + 2) * n_z // 2, n_z)
            start = to * rows
            at = pl.ds(pl.multiple_of(start, 16), rows)
            blocks.append(decode(own[at, :]) + decode(seen[at, :]))
        if i == 0:
            keep[:rows, :] = blocks[0]
            keep[rows:, :] = blocks[1]
        else:
            pack(pays[i - 1], blocks, extra)


def unpack(pays, at, rows, width):
    return jnp.concatenate(
        [
            sum(decode(p[at + k * rows : at + (k + 1) * rows, :]) for p in pays)
            for k in range(width // LANES)
        ],
        axis=1,
    )


def tails(pays):
    tail = sum(p[p.shape[0] - EXTRA :, :].astype(F32) for p in pays)
    return jnp.sum(tail, axis=0, keepdims=True)


def relay_body(keep, total, *refs):
    pays, near, far, total_out = refs[:-3], refs[-3], refs[-2], refs[-1]
    rows, width = near.shape
    near[...] = keep[:rows, :] + unpack(pays, 0, rows, width)
    sums = total[...] + tails(pays)
    total_out[...] = sums
    block = keep[rows:, :] + unpack(pays, rows * width // LANES, rows, width)
    pack(far, [block], split3(sums))


def text_sum_body(pairs, near, total, terms, side, pay, out, loss):
    rows, width = out.shape
    unit = terms[2:3, :1]
    unit = jnp.where(unit > 0, unit, 1.0)
    out[...] = unit * (near[...] + unpack([pay], 0, rows, width))
    full = total[...] + side[...] + tails([pay])
    loss[0, 0] = jnp.max(full) * (math.log(2.0) / (2.0 * pairs))


def image_sum_body(got, terms, out, side):
    rows, width = out.shape
    unit = terms[1:2, :1]
    unit = jnp.where(unit > 0, unit, 1.0)
    pays = [got.at[p] for p in range(got.shape[0])]
    for k in range(width // LANES):
        at = slice(k * rows, (k + 1) * rows)
        out[:, k * LANES : (k + 1) * LANES] = unit * sum(decode(p[at, :]) for p in pays)
    side[...] = tails(pays)


def shards(image_embed, text_embed, pair_index):
    rows, width = image_embed.shape
    n_xl, n_z, n_c, n_y, n_xh = (lax.axis_size(a) for a in ("xl", "z", "c", "y", "xh"))
    n_plane = n_xl * n_y * n_xh
    size = n_plane * rows
    half = n_z * rows
    pairs = size * n_z * n_c
    inv_root = width ** (-0.5)
    shape = jax.ShapeDtypeStruct
    tall = width // LANES * rows + EXTRA

    pair_seen = lax.ppermute(pair_index, "xl", SWAP)
    copies = pl.pallas_call(
        copies_body,
        out_shape=pltpu.HBM((n_plane, rows, width), BF16),
        in_specs=[pl.BlockSpec(memory_space=pl.ANY)],
        out_specs=pl.BlockSpec(memory_space=pltpu.HBM),
        scratch_shapes=[pltpu.VMEM((rows, width), BF16), pltpu.SemaphoreType.DMA((n_plane + 1,))],
        name="copies",
    )(image_embed)
    image = lax.all_to_all(copies, PLANE, 0, 0).reshape(size, width)

    steps = [q if q <= n_z // 4 else q - n_z // 2 for q in range(n_z // 2)]
    far = turn(text_embed, "z", n_z // 2)
    (joined,) = call(
        join_body, (shape((2 * rows, width), BF16),), (text_embed, far), "join", 10**11
    )
    pieces = [joined] + [turn_z(joined, q, True) for q in steps[1:]]
    pieces = pieces + [lax.ppermute(piece, "c", SWAP) for piece in pieces]

    flops = 2 * size * size * width
    pair, scores, text, hold, cross = call(
        functools.partial(score_body, steps, inv_root),
        (
            shape((1, size), F32),
            shape((size, size), F32),
            shape((size, width), BF16),
            shape((1, size + 2 * LANES), F32),
            shape((1, size + 2 * LANES), F32),
        ),
        (*pieces, image, pair_index, pair_seen),
        "scores",
        flops,
        2 * size * size,
    )
    full = shape((1, 2 * size + 2 * LANES), F32)
    (stats,) = call(meet_body, (full,), (hold, lax.ppermute(cross, "c", SWAP)), "meet")
    around = [turn_both(stats, q, q, 0) for q in (1, -1, 2)]
    (stats,) = call(functools.partial(round_body, False), (full,), (stats, *around), "round")
    far_z = (None, None, n_z // 2)
    around = [turn_both(stats, f, 0, q) for f, q in zip(far_z, (1, -1, 2))]
    stats, cross = call(
        functools.partial(round_body, True), (full, shape(cross.shape, F32)), (stats, *around), "last"
    )
    seen = lax.ppermute(cross, "c", SWAP)

    terms, text_own, text_other, image_sent = call(
        functools.partial(grad_body, n_z, inv_root),
        (
            shape((8, LANES), F32),
            shape((half, width), BF16),
            pltpu.HBM((half + EXTRA, width), BF16),
            pltpu.HBM((n_plane, tall, LANES), BF16),
        ),
        (stats, seen, scores, text, image, pair),
        "grads",
        2 * flops,
        2 * size * size,
        hbm_out=(2, 3),
        scratch=[
            pltpu.VMEM((size, size), BF16),
            pltpu.VMEM((n_plane, tall, LANES), BF16),
            pltpu.VMEM((half + EXTRA, width), BF16),
            pltpu.SemaphoreType.DMA((n_plane + 1,)),
        ],
    )
    image_got = lax.all_to_all(image_sent, PLANE, 0, 0)
    keep, total, *pays = call(
        functools.partial(send_body, steps),
        (shape((2 * rows, width), F32), shape((1, LANES), F32))
        + (shape((2 * tall - EXTRA, LANES), BF16),) * len(steps[1:]),
        (text_own, lax.ppermute(text_other, "c", SWAP), terms),
        "send",
        10**10,
        size=1,
    )
    pays = [turn_z(pay, q, False) for q, pay in zip(steps[1:], pays)]
    near, far, total = call(
        relay_body,
        (shape((rows, width), F32), shape((tall, LANES), BF16), shape((1, LANES), F32)),
        (keep, total, *pays),
        "relay",
        size=1,
    )
    grad_image, side = call(
        image_sum_body,
        (shape((rows, width), F32), shape((1, LANES), F32)),
        (image_got, terms),
        "image_sum",
        size=1,
    )
    grad_text, loss = call(
        functools.partial(text_sum_body, pairs),
        (shape((rows, width), F32), shape((1, 1), F32)),
        (near, total, terms, side, turn(far, "z", n_z // 2)),
        "text_sum",
        smem_out=1,
        size=1,
    )
    return (loss[0, 0], grad_image, grad_text)


def solution(mesh):
    fine = Mesh(mesh.devices.reshape(2, 8, 2, 4, 2), ("xl", "z", "c", "y", "xh"))
    image_spec = P(("xl", "z", "c", "y", "xh"), None)
    text_spec = P(("y", "xh", "xl", "z", "c"), None)
    return jax.shard_map(
        shards,
        mesh=fine,
        in_specs=(image_spec, text_spec, P(("xl", "z", "c"))),
        out_specs=(P(), image_spec, text_spec),
        check_vma=False,
    )
```

```python
import functools
import math

import jax
import jax.numpy as jnp
from jax import lax
from jax.experimental import pallas as pl
from jax.experimental.pallas import tpu as pltpu
from jax.sharding import Mesh, PartitionSpec as P

AXES = ("xl", "z", "c", "y", "xh")
PLANE = ("xl", "y", "xh")
SWAP = [(0, 1), (1, 0)]
LANES = 128
EXTRA = 16
F32 = jnp.float32
BF16 = jnp.bfloat16


def turn(x, axis, step):
    count = lax.axis_size(axis)
    return lax.ppermute(x, axis, [(i, (i + step) % count) for i in range(count)])


def lean(q, z, count):
    return q * (1 - 2 * (z % 2)) if abs(q) == count // 4 else q


def turn_z(x, q, back):
    count = lax.axis_size("z")
    pairs = [((i + lean(q, i, count)) % count, i) for i in range(count)]
    return lax.ppermute(x, "z", pairs if back else [(b, a) for a, b in pairs])


def turn_both(x, step_z, step_x, step_y):
    sizes = [lax.axis_size(a) for a in AXES]
    n_xl, n_z, n_c, n_y, n_xh = sizes
    n_x = n_xl * n_xh
    pairs = []
    for i in range(math.prod(sizes)):
        rest, xh = divmod(i, n_xh)
        rest, y = divmod(rest, n_y)
        rest, c = divmod(rest, n_c)
        xl, z = divmod(rest, n_z)
        if c == 0:
            if step_z is None:
                continue
            z = (z + step_z) % n_z
        else:
            xh, xl = divmod((xh * n_xl + xl + step_x) % n_x, n_xl)
            y = (y + step_y) % n_y
        pairs.append((i, (((xl * n_z + z) * n_c + c) * n_y + y) * n_xh + xh))
    return lax.ppermute(x, AXES, pairs)


def merge(parts):
    high = functools.reduce(jnp.maximum, parts)
    return high + jnp.log2(sum(jnp.exp2(p - high) for p in parts))


def encode(scaled):
    return ((scaled * scaled) * (scaled * jnp.abs(scaled))).astype(BF16)


def decode(x):
    wide = x.astype(F32)
    half = lax.rsqrt(jnp.maximum(jnp.abs(wide), 1e-37))
    return wide * half * (half * lax.rsqrt(half))


def split3(value):
    high = value.astype(BF16).astype(F32)
    mid = (value - high).astype(BF16).astype(F32)
    low = value - high - mid
    row = lax.broadcasted_iota(jnp.int32, (EXTRA, LANES), 0)
    parts = jnp.where(row == 0, high, jnp.where(row == 1, mid, jnp.where(row == 2, low, 0.0)))
    return parts.astype(BF16)


def inverse(value):
    return jnp.where(value > 0, 1.0 / value, 1.0)


def to_column(row):
    return jnp.transpose(jnp.broadcast_to(row, (LANES, row.shape[1])))[:, :1]


def to_row(column):
    return jnp.transpose(jnp.broadcast_to(column, (column.shape[0], LANES)))[:1, :]


def call(
    body, outs, args, name, flops=0, exps=0, smem_out=None, size=None, hbm_out=(), scratch=()
):
    if size is None:
        size = sum(math.prod(a.shape) * a.dtype.itemsize for a in (*args, *outs))
    spaces = [pltpu.VMEM] * len(outs)
    if smem_out is not None:
        spaces[smem_out] = pltpu.SMEM
    for i in hbm_out:
        spaces[i] = pltpu.HBM
    return pl.pallas_call(
        body,
        out_shape=outs,
        in_specs=[pl.BlockSpec(memory_space=pltpu.VMEM)] * len(args),
        out_specs=tuple(pl.BlockSpec(memory_space=s) for s in spaces),
        scratch_shapes=scratch,
        cost_estimate=pl.CostEstimate(flops=flops, bytes_accessed=size, transcendentals=exps),
        compiler_params=pltpu.CompilerParams(vmem_limit_bytes=20 * 1024 * 1024),
        name=name,
    )(*args)


def copies_body(source, out, held, sems):
    count = out.shape[0]
    load = pltpu.make_async_copy(source, held, sems.at[count])
    load.start()
    load.wait()
    copies = [pltpu.make_async_copy(held, out.at[i], sems.at[i]) for i in range(count)]
    for copy in copies:
        copy.start()
    for copy in copies:
        copy.wait()


def join_body(near, far, out):
    rows = near.shape[0]
    out[:rows, :] = near[...]
    out[rows:, :] = far[...]


def pair_row(mine, seen):
    first = lax.axis_index("xl") == 0
    left = mine[...].astype(F32)[None, :]
    right = seen[...].astype(F32)[None, :]
    return jnp.concatenate(
        [jnp.where(first, left, right), jnp.where(first, right, left)], axis=1
    )


def score_body(steps, inv_root, *refs):
    n_z = 2 * len(steps)
    pieces, refs = refs[:n_z], refs[n_z:]
    image, pair_mine, pair_seen, pair_out, scores, text, hold, cross = refs
    pair = pair_row(pair_mine, pair_seen)
    pair_out[...] = pair
    rows = pieces[0].shape[0] // 2
    size = image.shape[0]
    ids = labels(n_z, rows)
    found = jnp.zeros((1, size), F32)
    z = lax.axis_index("z")
    high = jnp.zeros(pieces[0].shape, F32)
    for h in range(2):
        for i, q in enumerate(steps):
            piece = pieces[h * n_z // 2 + i]
            high = jnp.maximum(high, jnp.abs(piece[...].astype(F32)))
            for k in range(2):
                to = lax.rem(z + lean(q, z, n_z) + (k + 2) * n_z // 2, n_z)
                start = (h * n_z + to) * rows
                text[pl.ds(pl.multiple_of(start, 16), rows), :] = piece[
                    k * rows : (k + 1) * rows, :
                ]
    lanes = []
    col_top = jnp.full((1, size), -1e38, F32)
    step = 256
    for r in range(0, size, step):
        tile = (
            lax.dot_general(
                image[r : r + step, :],
                text[...],
                (((1,), (1,)), ((), ())),
                preferred_element_type=F32,
            )
            * (inv_root / math.log(2.0))
        )
        scores[r : r + step, :] = tile
        col_top = jnp.maximum(col_top, jnp.max(tile, axis=0, keepdims=True))
        top = jnp.max(tile, axis=1, keepdims=True)
        part = jnp.log2(jnp.sum(jnp.exp2(tile - top), axis=1, keepdims=True))
        lanes.append(to_row(top + part))
        hit = to_column(pair[:, r : r + step]) == ids
        found += jnp.sum(jnp.where(hit, tile, 0.0), axis=0, keepdims=True)
    mass = jnp.exp2(scores[...] - col_top)
    col = col_top + jnp.log2(jnp.sum(mass, axis=0, keepdims=True))
    image_max = jnp.max(jnp.abs(image[...].astype(F32)))
    zero = jnp.zeros((1, LANES), F32)
    rows_out = jnp.concatenate([*lanes, zero + jnp.max(high), zero], axis=1)
    cols_out = jnp.concatenate([col, zero + image_max, zero + jnp.sum(found)], axis=1)
    first = lax.axis_index("c") == 0
    hold[...] = jnp.where(first, cols_out, rows_out)
    cross[...] = jnp.where(first, rows_out, cols_out)


def crossed(cols):
    half = cols.shape[1] // 2
    return jnp.concatenate([cols[:, half:], cols[:, :half]], axis=1)


def meet_body(hold, seen, out):
    size = hold.shape[1] - 2 * LANES
    first = lax.axis_index("c") == 0
    mine, other = hold[:, :size], seen[:, :size]
    out[:, :size] = jnp.where(first, merge([mine, crossed(other)]), mine)
    out[:, size : 2 * size] = jnp.where(first, 0.0, other)
    high = jnp.maximum(hold[:, size : size + LANES], seen[:, size : size + LANES])
    total = hold[:, size + LANES :] + seen[:, size + LANES :]
    out[:, 2 * size :] = jnp.concatenate([high, total], axis=1)


def round_body(last, mine, one, two, three, *outs):
    size = mine.shape[1] // 2 - LANES
    first = lax.axis_index("c") == 0
    parts = [mine[:, : 2 * size], three[:, : 2 * size]]
    for ref in (one, two):
        part = ref[:, : 2 * size]
        parts.append(jnp.where(first, -1e38, part) if last else part)
    lse = merge(parts)
    refs = (mine, one, two, three)
    at = slice(2 * size, 2 * size + LANES)
    high = functools.reduce(jnp.maximum, [ref[:, at] for ref in refs])
    total = sum(ref[:, 2 * size + LANES :] for ref in refs)
    outs[0][...] = jnp.concatenate([lse, high, total], axis=1)
    if last:
        kept = jnp.where(first, lse[:, :size], lse[:, size:])
        outs[1][...] = jnp.concatenate([kept, high, total], axis=1)


def labels(n_z, rows):
    half = n_z * rows
    n_xl, n_c, n_xh = (lax.axis_size(a) for a in ("xl", "c", "xh"))
    block = (lax.axis_index("y") * n_xh + lax.axis_index("xh")) * n_xl + lax.axis_index("xl")
    core = lax.axis_index("c")
    slot = lax.broadcasted_iota(jnp.int32, (1, 2 * half), 1)
    own = slot < half
    within = jnp.where(own, slot, slot - half)
    holder = jnp.floor((within.astype(F32) + 0.5) * (1.0 / rows)).astype(jnp.int32)
    ids = ((block * n_z + holder) * n_c + jnp.where(own, core, 1 - core)) * rows
    return (ids + within - holder * rows).astype(F32)


def grad_body(n_z, inv_root, *refs):
    mine, seen, scores, text, image, pair = refs[:6]
    terms, own, other, sent, grads, held, crossing, sems = refs[6:]
    size = grads.shape[0]
    half = own.shape[0]
    rows = half // n_z
    _, tall, _ = sent.shape
    ids = labels(n_z, rows)
    first = lax.axis_index("c") == 0
    seen_lse, seen_high = seen[:, :size], seen[:, size : size + LANES]
    mine_lse, mine_high = mine[:, :size], mine[:, 2 * size : 2 * size + LANES]
    col_lse = jnp.where(first, mine_lse, crossed(seen_lse))
    row_lse = jnp.where(first, seen_lse, mine_lse)
    image_max = jnp.where(first, mine_high, seen_high)
    text_max = jnp.where(first, seen_high, mine_high)
    found = jnp.where(first, mine[:, 2 * size + LANES :], seen[:, size + LANES :])
    row_terms = jnp.broadcast_to(jnp.sum(row_lse, axis=1, keepdims=True), (1, LANES))
    col_terms = jnp.sum(col_lse, axis=1, keepdims=True) - 2.0 * found
    terms[...] = jnp.concatenate(
        [row_terms, text_max, image_max, jnp.zeros((5, LANES), F32)], axis=0
    )
    row_column = to_column(row_lse + 1.0)
    col_row = col_lse + 1.0
    pair_column = to_column(pair[...])
    extra = split3(col_terms)
    scale = inverse(text_max[:, :1]) * inv_root
    step = size // 4
    copies = []
    for r in range(0, size, step):
        at = slice(r, r + step)
        tile = scores[at, :]
        probs = jnp.exp2(tile - row_column[at, :]) + jnp.exp2(tile - col_row)
        grad = (probs - jnp.where(pair_column[at, :] == ids, 1.0, 0.0)).astype(BF16)
        grads[at, :] = grad
        part = encode(jnp.dot(grad, text[...], preferred_element_type=F32) * scale)
        for p in range(step // rows):
            to = r // rows + p
            for k in range(text.shape[1] // LANES):
                held[to, k * rows : (k + 1) * rows, :] = part[
                    p * rows : (p + 1) * rows, k * LANES : (k + 1) * LANES
                ]
            held[to, tall - EXTRA :, :] = extra
            copies.append(pltpu.make_async_copy(held.at[to], sent.at[to], sems.at[to]))
            copies[-1].start()
    scale = inverse(image_max[:, :1]) * inv_root
    extra = split3(row_terms)
    crossing[half:, :] = jnp.concatenate([extra] * (own.shape[1] // LANES), axis=1)
    for start in (half, 0):
        part = lax.dot_general(
            grads[:, start : start + half],
            image[...],
            (((0,), (0,)), ((), ())),
            preferred_element_type=F32,
        )
        if start == 0:
            own[...] = encode(part * scale)
        else:
            crossing[:half, :] = encode(part * scale)
            copies.append(pltpu.make_async_copy(crossing, other, sems.at[sent.shape[0]]))
            copies[-1].start()
    for copy in copies:
        copy.wait()


def pack(pay, blocks, extra):
    rows, width = blocks[0].shape
    at = 0
    for block in blocks:
        coded = encode(block)
        for k in range(width // LANES):
            pay[at : at + rows, :] = coded[:, k * LANES : (k + 1) * LANES]
            at += rows
    pay[at:, :] = extra


def send_body(steps, own, seen, terms, keep, total, *pays):
    n_z = 2 * len(steps)
    rows = keep.shape[0] // 2
    z = lax.axis_index("z")
    half = own.shape[0]
    tail = seen[half:, :LANES].astype(F32)
    row_terms = terms[0:1, :] + jnp.sum(tail, axis=0, keepdims=True)
    total[...] = row_terms
    extra = split3(row_terms)
    for i, q in enumerate(steps):
        blocks = []
        for k in range(2):
            to = lax.rem(z + lean(q, z, n_z) + (k + 2) * n_z // 2, n_z)
            start = to * rows
            at = pl.ds(pl.multiple_of(start, 16), rows)
            blocks.append(decode(own[at, :]) + decode(seen[at, :]))
        if i == 0:
            keep[:rows, :] = blocks[0]
            keep[rows:, :] = blocks[1]
        else:
            pack(pays[i - 1], blocks, extra)


def unpack(pays, at, rows, width):
    return jnp.concatenate(
        [
            sum(decode(p[at + k * rows : at + (k + 1) * rows, :]) for p in pays)
            for k in range(width // LANES)
        ],
        axis=1,
    )


def tails(pays):
    tail = sum(p[p.shape[0] - EXTRA :, :].astype(F32) for p in pays)
    return jnp.sum(tail, axis=0, keepdims=True)


def relay_body(keep, total, *refs):
    pays, near, far, total_out = refs[:-3], refs[-3], refs[-2], refs[-1]
    rows, width = near.shape
    near[...] = keep[:rows, :] + unpack(pays, 0, rows, width)
    sums = total[...] + tails(pays)
    total_out[...] = sums
    block = keep[rows:, :] + unpack(pays, rows * width // LANES, rows, width)
    pack(far, [block], split3(sums))


def text_sum_body(near, total, terms, pay, out, side):
    rows, width = out.shape
    unit = terms[2:3, :1]
    unit = jnp.where(unit > 0, unit, 1.0)
    out[...] = unit * (near[...] + unpack([pay], 0, rows, width))
    side[...] = total[...] + tails([pay])


def image_sum_body(pairs, got, terms, side, out, loss):
    rows, width = out.shape
    unit = terms[1:2, :1]
    unit = jnp.where(unit > 0, unit, 1.0)
    pays = [got.at[p] for p in range(got.shape[0])]
    for k in range(width // LANES):
        at = slice(k * rows, (k + 1) * rows)
        out[:, k * LANES : (k + 1) * LANES] = unit * sum(decode(p[at, :]) for p in pays)
    full = side[...] + tails(pays)
    loss[0, 0] = jnp.max(full) * (math.log(2.0) / (2.0 * pairs))


def shards(image_embed, text_embed, pair_index):
    rows, width = image_embed.shape
    n_xl, n_z, n_c, n_y, n_xh = (lax.axis_size(a) for a in ("xl", "z", "c", "y", "xh"))
    n_plane = n_xl * n_y * n_xh
    size = n_plane * rows
    half = n_z * rows
    pairs = size * n_z * n_c
    inv_root = width ** (-0.5)
    shape = jax.ShapeDtypeStruct
    tall = width // LANES * rows + EXTRA

    pair_seen = lax.ppermute(pair_index, "xl", SWAP)
    copies = pl.pallas_call(
        copies_body,
        out_shape=pltpu.HBM((n_plane, rows, width), BF16),
        in_specs=[pl.BlockSpec(memory_space=pl.ANY)],
        out_specs=pl.BlockSpec(memory_space=pltpu.HBM),
        scratch_shapes=[pltpu.VMEM((rows, width), BF16), pltpu.SemaphoreType.DMA((n_plane + 1,))],
        name="copies",
    )(image_embed)
    image = lax.all_to_all(copies, PLANE, 0, 0).reshape(size, width)

    steps = [q if q <= n_z // 4 else q - n_z // 2 for q in range(n_z // 2)]
    far = turn(text_embed, "z", n_z // 2)
    (joined,) = call(
        join_body, (shape((2 * rows, width), BF16),), (text_embed, far), "join", 10**11
    )
    pieces = [joined] + [turn_z(joined, q, True) for q in steps[1:]]
    pieces = pieces + [lax.ppermute(piece, "c", SWAP) for piece in pieces]

    flops = 2 * size * size * width
    pair, scores, text, hold, cross = call(
        functools.partial(score_body, steps, inv_root),
        (
            shape((1, size), F32),
            shape((size, size), F32),
            shape((size, width), BF16),
            shape((1, size + 2 * LANES), F32),
            shape((1, size + 2 * LANES), F32),
        ),
        (*pieces, image, pair_index, pair_seen),
        "scores",
        flops,
        2 * size * size,
    )
    full = shape((1, 2 * size + 2 * LANES), F32)
    (stats,) = call(meet_body, (full,), (hold, lax.ppermute(cross, "c", SWAP)), "meet")
    around = [turn_both(stats, q, q, 0) for q in (1, -1, 2)]
    (stats,) = call(functools.partial(round_body, False), (full,), (stats, *around), "round")
    far_z = (None, None, n_z // 2)
    around = [turn_both(stats, f, 0, q) for f, q in zip(far_z, (1, -1, 2))]
    stats, cross = call(
        functools.partial(round_body, True), (full, shape(cross.shape, F32)), (stats, *around), "last"
    )
    seen = lax.ppermute(cross, "c", SWAP)

    terms, text_own, text_other, image_sent = call(
        functools.partial(grad_body, n_z, inv_root),
        (
            shape((8, LANES), F32),
            shape((half, width), BF16),
            pltpu.HBM((half + EXTRA, width), BF16),
            pltpu.HBM((n_plane, tall, LANES), BF16),
        ),
        (stats, seen, scores, text, image, pair),
        "grads",
        2 * flops,
        2 * size * size,
        hbm_out=(2, 3),
        scratch=[
            pltpu.VMEM((size, size), BF16),
            pltpu.VMEM((n_plane, tall, LANES), BF16),
            pltpu.VMEM((half + EXTRA, width), BF16),
            pltpu.SemaphoreType.DMA((n_plane + 1,)),
        ],
    )
    image_got = lax.all_to_all(image_sent, PLANE, 0, 0)
    keep, total, *pays = call(
        functools.partial(send_body, steps),
        (shape((2 * rows, width), F32), shape((1, LANES), F32))
        + (shape((2 * tall - EXTRA, LANES), BF16),) * len(steps[1:]),
        (text_own, lax.ppermute(text_other, "c", SWAP), terms),
        "send",
        10**10,
        size=1,
    )
    pays = [turn_z(pay, q, False) for q, pay in zip(steps[1:], pays)]
    near, far, total = call(
        relay_body,
        (shape((rows, width), F32), shape((tall, LANES), BF16), shape((1, LANES), F32)),
        (keep, total, *pays),
        "relay",
        size=1,
    )
    grad_text, side = call(
        text_sum_body,
        (shape((rows, width), F32), shape((1, LANES), F32)),
        (near, total, terms, turn(far, "z", n_z // 2)),
        "text_sum",
        size=1,
    )
    grad_image, loss = call(
        functools.partial(image_sum_body, pairs),
        (shape((rows, width), F32), shape((1, 1), F32)),
        (image_got, terms, side),
        "image_sum",
        smem_out=1,
    )
    return (loss[0, 0], grad_image, grad_text)


def solution(mesh):
    fine = Mesh(mesh.devices.reshape(2, 8, 2, 4, 2), ("xl", "z", "c", "y", "xh"))
    image_spec = P(("xl", "z", "c", "y", "xh"), None)
    text_spec = P(("y", "xh", "xl", "z", "c"), None)
    return jax.shard_map(
        shards,
        mesh=fine,
        in_specs=(image_spec, text_spec, P(("xl", "z", "c"))),
        out_specs=(P(), image_spec, text_spec),
        check_vma=False,
    )
```

```python
import functools
import math

import jax
import jax.numpy as jnp
from jax import lax
from jax.experimental import pallas as pl
from jax.experimental.pallas import tpu as pltpu
from jax.sharding import Mesh, PartitionSpec as P

AXES = ("xl", "z", "c", "y", "xh")
PLANE = ("xl", "y", "xh")
SWAP = [(0, 1), (1, 0)]
LANES = 128
EXTRA = 16
F32 = jnp.float32
BF16 = jnp.bfloat16


def turn(x, axis, step):
    count = lax.axis_size(axis)
    return lax.ppermute(x, axis, [(i, (i + step) % count) for i in range(count)])


def lean(q, z, count):
    return q * (1 - 2 * (z % 2)) if abs(q) == count // 4 else q


def turn_z(x, q, back):
    count = lax.axis_size("z")
    pairs = [((i + lean(q, i, count)) % count, i) for i in range(count)]
    return lax.ppermute(x, "z", pairs if back else [(b, a) for a, b in pairs])


def turn_both(x, step_z, step_x, step_y):
    sizes = [lax.axis_size(a) for a in AXES]
    n_xl, n_z, n_c, n_y, n_xh = sizes
    n_x = n_xl * n_xh
    pairs = []
    for i in range(math.prod(sizes)):
        rest, xh = divmod(i, n_xh)
        rest, y = divmod(rest, n_y)
        rest, c = divmod(rest, n_c)
        xl, z = divmod(rest, n_z)
        if c == 0:
            if step_z is None:
                continue
            z = (z + step_z) % n_z
        else:
            xh, xl = divmod((xh * n_xl + xl + step_x) % n_x, n_xl)
            y = (y + step_y) % n_y
        pairs.append((i, (((xl * n_z + z) * n_c + c) * n_y + y) * n_xh + xh))
    return lax.ppermute(x, AXES, pairs)


def merge(parts):
    high = functools.reduce(jnp.maximum, parts)
    return high + jnp.log2(sum(jnp.exp2(p - high) for p in parts))


def encode(scaled):
    return ((scaled * scaled) * (scaled * jnp.abs(scaled))).astype(BF16)


def decode(x):
    wide = x.astype(F32)
    half = lax.rsqrt(jnp.maximum(jnp.abs(wide), 1e-37))
    return wide * half * (half * lax.rsqrt(half))


def split3(value):
    high = value.astype(BF16).astype(F32)
    mid = (value - high).astype(BF16).astype(F32)
    low = value - high - mid
    row = lax.broadcasted_iota(jnp.int32, (EXTRA, LANES), 0)
    parts = jnp.where(row == 0, high, jnp.where(row == 1, mid, jnp.where(row == 2, low, 0.0)))
    return parts.astype(BF16)


def inverse(value):
    return jnp.where(value > 0, 1.0 / value, 1.0)


def to_column(row):
    return jnp.transpose(jnp.broadcast_to(row, (LANES, row.shape[1])))[:, :1]


def to_row(column):
    return jnp.transpose(jnp.broadcast_to(column, (column.shape[0], LANES)))[:1, :]


def call(
    body, outs, args, name, flops=0, exps=0, smem_out=None, size=None, hbm_out=(), scratch=()
):
    if size is None:
        size = sum(math.prod(a.shape) * a.dtype.itemsize for a in (*args, *outs))
    spaces = [pltpu.VMEM] * len(outs)
    if smem_out is not None:
        spaces[smem_out] = pltpu.SMEM
    for i in hbm_out:
        spaces[i] = pltpu.HBM
    return pl.pallas_call(
        body,
        out_shape=outs,
        in_specs=[pl.BlockSpec(memory_space=pltpu.VMEM)] * len(args),
        out_specs=tuple(pl.BlockSpec(memory_space=s) for s in spaces),
        scratch_shapes=scratch,
        cost_estimate=pl.CostEstimate(flops=flops, bytes_accessed=size, transcendentals=exps),
        compiler_params=pltpu.CompilerParams(vmem_limit_bytes=20 * 1024 * 1024),
        name=name,
    )(*args)


def copies_body(source, out, held, sems):
    count = out.shape[0]
    load = pltpu.make_async_copy(source, held, sems.at[count])
    load.start()
    load.wait()
    copies = [pltpu.make_async_copy(held, out.at[i], sems.at[i]) for i in range(count)]
    for copy in copies:
        copy.start()
    for copy in copies:
        copy.wait()


def join_body(near, far, out):
    rows = near.shape[0]
    out[:rows, :] = near[...]
    out[rows:, :] = far[...]


def pair_row(mine, seen):
    first = lax.axis_index("xl") == 0
    left = mine[...].astype(F32)[None, :]
    right = seen[...].astype(F32)[None, :]
    return jnp.concatenate(
        [jnp.where(first, left, right), jnp.where(first, right, left)], axis=1
    )


def score_body(steps, inv_root, *refs):
    n_z = 2 * len(steps)
    pieces, refs = refs[:n_z], refs[n_z:]
    image, pair_mine, pair_seen, pair_out, scores, text, hold, cross = refs
    pair = pair_row(pair_mine, pair_seen)
    pair_out[...] = pair
    rows = pieces[0].shape[0] // 2
    size = image.shape[0]
    ids = labels(n_z, rows)
    found = jnp.zeros((1, size), F32)
    z = lax.axis_index("z")
    high = jnp.zeros(pieces[0].shape, F32)
    for h in range(2):
        for i, q in enumerate(steps):
            piece = pieces[h * n_z // 2 + i]
            high = jnp.maximum(high, jnp.abs(piece[...].astype(F32)))
            for k in range(2):
                to = lax.rem(z + lean(q, z, n_z) + (k + 2) * n_z // 2, n_z)
                start = (h * n_z + to) * rows
                text[pl.ds(pl.multiple_of(start, 16), rows), :] = piece[
                    k * rows : (k + 1) * rows, :
                ]
    lanes = []
    col_top = jnp.full((1, size), -1e38, F32)
    step = 256
    for r in range(0, size, step):
        tile = (
            lax.dot_general(
                image[r : r + step, :],
                text[...],
                (((1,), (1,)), ((), ())),
                preferred_element_type=F32,
            )
            * (inv_root / math.log(2.0))
        )
        scores[r : r + step, :] = tile
        col_top = jnp.maximum(col_top, jnp.max(tile, axis=0, keepdims=True))
        top = jnp.max(tile, axis=1, keepdims=True)
        part = jnp.log2(jnp.sum(jnp.exp2(tile - top), axis=1, keepdims=True))
        lanes.append(to_row(top + part))
        hit = to_column(pair[:, r : r + step]) == ids
        found += jnp.sum(jnp.where(hit, tile, 0.0), axis=0, keepdims=True)
    mass = jnp.exp2(scores[...] - col_top)
    col = col_top + jnp.log2(jnp.sum(mass, axis=0, keepdims=True))
    image_max = jnp.max(jnp.abs(image[...].astype(F32)))
    zero = jnp.zeros((1, LANES), F32)
    rows_out = jnp.concatenate([*lanes, zero + jnp.max(high), zero], axis=1)
    cols_out = jnp.concatenate([col, zero + image_max, zero + jnp.sum(found)], axis=1)
    first = lax.axis_index("c") == 0
    hold[...] = jnp.where(first, cols_out, rows_out)
    cross[...] = jnp.where(first, rows_out, cols_out)


def crossed(cols):
    half = cols.shape[1] // 2
    return jnp.concatenate([cols[:, half:], cols[:, :half]], axis=1)


def meet_body(hold, seen, out):
    size = hold.shape[1] - 2 * LANES
    first = lax.axis_index("c") == 0
    mine, other = hold[:, :size], seen[:, :size]
    out[:, :size] = jnp.where(first, merge([mine, crossed(other)]), mine)
    out[:, size : 2 * size] = jnp.where(first, 0.0, other)
    high = jnp.maximum(hold[:, size : size + LANES], seen[:, size : size + LANES])
    total = hold[:, size + LANES :] + seen[:, size + LANES :]
    out[:, 2 * size :] = jnp.concatenate([high, total], axis=1)


def round_body(last, mine, one, two, three, *outs):
    size = mine.shape[1] // 2 - LANES
    first = lax.axis_index("c") == 0
    parts = [mine[:, : 2 * size], three[:, : 2 * size]]
    for ref in (one, two):
        part = ref[:, : 2 * size]
        parts.append(jnp.where(first, -1e38, part) if last else part)
    lse = merge(parts)
    refs = (mine, one, two, three)
    at = slice(2 * size, 2 * size + LANES)
    high = functools.reduce(jnp.maximum, [ref[:, at] for ref in refs])
    total = sum(ref[:, 2 * size + LANES :] for ref in refs)
    outs[0][...] = jnp.concatenate([lse, high, total], axis=1)
    if last:
        kept = jnp.where(first, lse[:, :size], lse[:, size:])
        outs[1][...] = jnp.concatenate([kept, high, total], axis=1)


def labels(n_z, rows):
    half = n_z * rows
    n_xl, n_c, n_xh = (lax.axis_size(a) for a in ("xl", "c", "xh"))
    block = (lax.axis_index("y") * n_xh + lax.axis_index("xh")) * n_xl + lax.axis_index("xl")
    core = lax.axis_index("c")
    slot = lax.broadcasted_iota(jnp.int32, (1, 2 * half), 1)
    own = slot < half
    within = jnp.where(own, slot, slot - half)
    holder = jnp.floor((within.astype(F32) + 0.5) * (1.0 / rows)).astype(jnp.int32)
    ids = ((block * n_z + holder) * n_c + jnp.where(own, core, 1 - core)) * rows
    return (ids + within - holder * rows).astype(F32)


def grad_body(n_z, inv_root, *refs):
    mine, seen, scores, text, image, pair = refs[:6]
    terms, own, other, sent, grads, held, crossing, sems = refs[6:]
    size = grads.shape[0]
    half = own.shape[0]
    rows = half // n_z
    _, tall, _ = sent.shape
    ids = labels(n_z, rows)
    first = lax.axis_index("c") == 0
    seen_lse, seen_high = seen[:, :size], seen[:, size : size + LANES]
    mine_lse, mine_high = mine[:, :size], mine[:, 2 * size : 2 * size + LANES]
    col_lse = jnp.where(first, mine_lse, crossed(seen_lse))
    row_lse = jnp.where(first, seen_lse, mine_lse)
    image_max = jnp.where(first, mine_high, seen_high)
    text_max = jnp.where(first, seen_high, mine_high)
    found = jnp.where(first, mine[:, 2 * size + LANES :], seen[:, size + LANES :])
    row_terms = jnp.broadcast_to(jnp.sum(row_lse, axis=1, keepdims=True), (1, LANES))
    col_terms = jnp.sum(col_lse, axis=1, keepdims=True) - 2.0 * found
    terms[...] = jnp.concatenate(
        [row_terms, text_max, image_max, jnp.zeros((5, LANES), F32)], axis=0
    )
    row_column = to_column(row_lse + 1.0)
    col_row = col_lse + 1.0
    pair_column = to_column(pair[...])
    extra = split3(col_terms)
    scale = inverse(text_max[:, :1]) * inv_root
    step = size // 4
    copies = []
    for r in range(0, size, step):
        at = slice(r, r + step)
        tile = scores[at, :]
        probs = jnp.exp2(tile - row_column[at, :]) + jnp.exp2(tile - col_row)
        grad = (probs - jnp.where(pair_column[at, :] == ids, 1.0, 0.0)).astype(BF16)
        grads[at, :] = grad
        part = encode(jnp.dot(grad, text[...], preferred_element_type=F32) * scale)
        for p in range(step // rows):
            to = r // rows + p
            for k in range(text.shape[1] // LANES):
                held[to, k * rows : (k + 1) * rows, :] = part[
                    p * rows : (p + 1) * rows, k * LANES : (k + 1) * LANES
                ]
            held[to, tall - EXTRA :, :] = extra
            copies.append(pltpu.make_async_copy(held.at[to], sent.at[to], sems.at[to]))
            copies[-1].start()
    scale = inverse(image_max[:, :1]) * inv_root
    extra = split3(row_terms)
    crossing[half:, :] = jnp.concatenate([extra] * (own.shape[1] // LANES), axis=1)
    for start in (half, 0):
        part = lax.dot_general(
            grads[:, start : start + half],
            image[...],
            (((0,), (0,)), ((), ())),
            preferred_element_type=F32,
        )
        if start == 0:
            own[...] = encode(part * scale)
        else:
            crossing[:half, :] = encode(part * scale)
            copies.append(pltpu.make_async_copy(crossing, other, sems.at[sent.shape[0]]))
            copies[-1].start()
    for copy in copies:
        copy.wait()


def pack(pay, blocks, extra):
    rows, width = blocks[0].shape
    at = 0
    for block in blocks:
        coded = encode(block)
        for k in range(width // LANES):
            pay[at : at + rows, :] = coded[:, k * LANES : (k + 1) * LANES]
            at += rows
    pay[at:, :] = extra


def send_body(steps, own, seen, terms, keep, total, *pays):
    n_z = 2 * len(steps)
    rows = keep.shape[0] // 2
    z = lax.axis_index("z")
    half = own.shape[0]
    tail = seen[half:, :LANES].astype(F32)
    row_terms = terms[0:1, :] + jnp.sum(tail, axis=0, keepdims=True)
    total[...] = row_terms
    extra = split3(row_terms)
    for i, q in enumerate(steps):
        blocks = []
        for k in range(2):
            to = lax.rem(z + lean(q, z, n_z) + (k + 2) * n_z // 2, n_z)
            start = to * rows
            at = pl.ds(pl.multiple_of(start, 16), rows)
            blocks.append(decode(own[at, :]) + decode(seen[at, :]))
        if i == 0:
            keep[:rows, :] = blocks[0]
            keep[rows:, :] = blocks[1]
        else:
            pack(pays[i - 1], blocks, extra)


def unpack(pays, at, rows, width):
    return jnp.concatenate(
        [
            sum(decode(p[at + k * rows : at + (k + 1) * rows, :]) for p in pays)
            for k in range(width // LANES)
        ],
        axis=1,
    )


def tails(pays):
    tail = sum(p[p.shape[0] - EXTRA :, :].astype(F32) for p in pays)
    return jnp.sum(tail, axis=0, keepdims=True)


def relay_body(keep, total, *refs):
    pays, near, far, total_out = refs[:-3], refs[-3], refs[-2], refs[-1]
    rows, width = near.shape
    near[...] = keep[:rows, :] + unpack(pays, 0, rows, width)
    sums = total[...] + tails(pays)
    total_out[...] = sums
    block = keep[rows:, :] + unpack(pays, rows * width // LANES, rows, width)
    pack(far, [block], split3(sums))


def text_sum_body(near, total, terms, pay, out, side):
    rows, width = out.shape
    unit = terms[2:3, :1]
    unit = jnp.where(unit > 0, unit, 1.0)
    out[...] = unit * (near[...] + unpack([pay], 0, rows, width))
    side[...] = total[...] + tails([pay])


def image_sum_body(pairs, got, terms, side, out, loss):
    rows, width = out.shape
    unit = terms[1:2, :1]
    unit = jnp.where(unit > 0, unit, 1.0)
    pays = [got.at[p] for p in range(got.shape[0])]
    for k in range(width // LANES):
        at = slice(k * rows, (k + 1) * rows)
        out[:, k * LANES : (k + 1) * LANES] = unit * sum(decode(p[at, :]) for p in pays)
    full = side[...] + tails(pays)
    loss[0, 0] = jnp.max(full) * (math.log(2.0) / (2.0 * pairs))


def shards(image_embed, text_embed, pair_index):
    rows, width = image_embed.shape
    n_xl, n_z, n_c, n_y, n_xh = (lax.axis_size(a) for a in ("xl", "z", "c", "y", "xh"))
    n_plane = n_xl * n_y * n_xh
    size = n_plane * rows
    half = n_z * rows
    pairs = size * n_z * n_c
    inv_root = width ** (-0.5)
    shape = jax.ShapeDtypeStruct
    tall = width // LANES * rows + EXTRA

    pair_seen = lax.ppermute(pair_index, "xl", SWAP)
    copies = pl.pallas_call(
        copies_body,
        out_shape=pltpu.HBM((n_plane, rows, width), BF16),
        in_specs=[pl.BlockSpec(memory_space=pl.ANY)],
        out_specs=pl.BlockSpec(memory_space=pltpu.HBM),
        scratch_shapes=[pltpu.VMEM((rows, width), BF16), pltpu.SemaphoreType.DMA((n_plane + 1,))],
        name="copies",
    )(image_embed)
    image = lax.all_to_all(copies, PLANE, 0, 0).reshape(size, width)

    signed = [q if q <= n_z // 4 else q - n_z // 2 for q in range(n_z // 2)]
    steps = sorted(signed, key=lambda q: (q != 0, -abs(q)))
    inward = [0, *steps[:0:-1]]
    far = turn(text_embed, "z", n_z // 2)
    (joined,) = call(
        join_body, (shape((2 * rows, width), BF16),), (text_embed, far), "join", 10**11
    )
    pieces = [joined] + [turn_z(joined, q, True) for q in inward[1:]]
    pieces = pieces + [lax.ppermute(piece, "c", SWAP) for piece in pieces]

    flops = 2 * size * size * width
    pair, scores, text, hold, cross = call(
        functools.partial(score_body, inward, inv_root),
        (
            shape((1, size), F32),
            shape((size, size), F32),
            shape((size, width), BF16),
            shape((1, size + 2 * LANES), F32),
            shape((1, size + 2 * LANES), F32),
        ),
        (*pieces, image, pair_index, pair_seen),
        "scores",
        flops,
        2 * size * size,
    )
    full = shape((1, 2 * size + 2 * LANES), F32)
    (stats,) = call(meet_body, (full,), (hold, lax.ppermute(cross, "c", SWAP)), "meet")
    around = [turn_both(stats, q, q, 0) for q in (1, -1, 2)]
    (stats,) = call(functools.partial(round_body, False), (full,), (stats, *around), "round")
    far_z = (None, None, n_z // 2)
    around = [turn_both(stats, f, 0, q) for f, q in zip(far_z, (1, -1, 2))]
    stats, cross = call(
        functools.partial(round_body, True), (full, shape(cross.shape, F32)), (stats, *around), "last"
    )
    seen = lax.ppermute(cross, "c", SWAP)

    terms, text_own, text_other, image_sent = call(
        functools.partial(grad_body, n_z, inv_root),
        (
            shape((8, LANES), F32),
            shape((half, width), BF16),
            pltpu.HBM((half + EXTRA, width), BF16),
            pltpu.HBM((n_plane, tall, LANES), BF16),
        ),
        (stats, seen, scores, text, image, pair),
        "grads",
        2 * flops,
        2 * size * size,
        hbm_out=(2, 3),
        scratch=[
            pltpu.VMEM((size, size), BF16),
            pltpu.VMEM((n_plane, tall, LANES), BF16),
            pltpu.VMEM((half + EXTRA, width), BF16),
            pltpu.SemaphoreType.DMA((n_plane + 1,)),
        ],
    )
    image_got = lax.all_to_all(image_sent, PLANE, 0, 0)
    keep, total, *pays = call(
        functools.partial(send_body, steps),
        (shape((2 * rows, width), F32), shape((1, LANES), F32))
        + (shape((2 * tall - EXTRA, LANES), BF16),) * len(steps[1:]),
        (text_own, lax.ppermute(text_other, "c", SWAP), terms),
        "send",
        10**10,
        size=1,
    )
    pays = [turn_z(pay, q, False) for q, pay in zip(steps[1:], pays)]
    near, far, total = call(
        relay_body,
        (shape((rows, width), F32), shape((tall, LANES), BF16), shape((1, LANES), F32)),
        (keep, total, *pays),
        "relay",
        size=1,
    )
    grad_text, side = call(
        text_sum_body,
        (shape((rows, width), F32), shape((1, LANES), F32)),
        (near, total, terms, turn(far, "z", n_z // 2)),
        "text_sum",
        size=1,
    )
    grad_image, loss = call(
        functools.partial(image_sum_body, pairs),
        (shape((rows, width), F32), shape((1, 1), F32)),
        (image_got, terms, side),
        "image_sum",
        smem_out=1,
    )
    return (loss[0, 0], grad_image, grad_text)


def solution(mesh):
    fine = Mesh(mesh.devices.reshape(2, 8, 2, 4, 2), ("xl", "z", "c", "y", "xh"))
    image_spec = P(("xl", "z", "c", "y", "xh"), None)
    text_spec = P(("y", "xh", "xl", "z", "c"), None)
    return jax.shard_map(
        shards,
        mesh=fine,
        in_specs=(image_spec, text_spec, P(("xl", "z", "c"))),
        out_specs=(P(), image_spec, text_spec),
        check_vma=False,
    )
```

```python
import functools
import math

import jax
import jax.numpy as jnp
from jax import lax
from jax.experimental import pallas as pl
from jax.experimental.pallas import tpu as pltpu
from jax.sharding import Mesh, PartitionSpec as P

AXES = ("xl", "z", "c", "y", "xh")
PLANE = ("xl", "y", "xh")
SWAP = [(0, 1), (1, 0)]
LANES = 128
EXTRA = 16
F32 = jnp.float32
BF16 = jnp.bfloat16


def turn(x, axis, step):
    count = lax.axis_size(axis)
    return lax.ppermute(x, axis, [(i, (i + step) % count) for i in range(count)])


def lean(q, z, count):
    return q * (1 - 2 * (z % 2)) if abs(q) == count // 4 else q


def turn_z(x, q, back):
    count = lax.axis_size("z")
    pairs = [((i + lean(q, i, count)) % count, i) for i in range(count)]
    return lax.ppermute(x, "z", pairs if back else [(b, a) for a, b in pairs])


def turn_both(x, step_z, step_x, step_y):
    sizes = [lax.axis_size(a) for a in AXES]
    n_xl, n_z, n_c, n_y, n_xh = sizes
    n_x = n_xl * n_xh
    pairs = []
    for i in range(math.prod(sizes)):
        rest, xh = divmod(i, n_xh)
        rest, y = divmod(rest, n_y)
        rest, c = divmod(rest, n_c)
        xl, z = divmod(rest, n_z)
        if c == 0:
            if step_z is None:
                continue
            z = (z + step_z) % n_z
        else:
            xh, xl = divmod((xh * n_xl + xl + step_x) % n_x, n_xl)
            y = (y + step_y) % n_y
        pairs.append((i, (((xl * n_z + z) * n_c + c) * n_y + y) * n_xh + xh))
    return lax.ppermute(x, AXES, pairs)


def merge(parts):
    high = functools.reduce(jnp.maximum, parts)
    return high + jnp.log2(sum(jnp.exp2(p - high) for p in parts))


def encode(scaled):
    return ((scaled * scaled) * (scaled * jnp.abs(scaled))).astype(BF16)


def decode(x):
    wide = x.astype(F32)
    half = lax.rsqrt(jnp.maximum(jnp.abs(wide), 1e-37))
    return wide * half * (half * lax.rsqrt(half))


def split3(value):
    high = value.astype(BF16).astype(F32)
    mid = (value - high).astype(BF16).astype(F32)
    low = value - high - mid
    row = lax.broadcasted_iota(jnp.int32, (EXTRA, LANES), 0)
    parts = jnp.where(row == 0, high, jnp.where(row == 1, mid, jnp.where(row == 2, low, 0.0)))
    return parts.astype(BF16)


def inverse(value):
    return jnp.where(value > 0, 1.0 / value, 1.0)


def to_column(row):
    return jnp.transpose(jnp.broadcast_to(row, (LANES, row.shape[1])))[:, :1]


def to_row(column):
    return jnp.transpose(jnp.broadcast_to(column, (column.shape[0], LANES)))[:1, :]


def call(
    body, outs, args, name, flops=0, exps=0, smem_out=None, size=None, hbm_out=(), scratch=()
):
    if size is None:
        size = sum(math.prod(a.shape) * a.dtype.itemsize for a in (*args, *outs))
    spaces = [pltpu.VMEM] * len(outs)
    if smem_out is not None:
        spaces[smem_out] = pltpu.SMEM
    for i in hbm_out:
        spaces[i] = pltpu.HBM
    return pl.pallas_call(
        body,
        out_shape=outs,
        in_specs=[pl.BlockSpec(memory_space=pltpu.VMEM)] * len(args),
        out_specs=tuple(pl.BlockSpec(memory_space=s) for s in spaces),
        scratch_shapes=scratch,
        cost_estimate=pl.CostEstimate(flops=flops, bytes_accessed=size, transcendentals=exps),
        compiler_params=pltpu.CompilerParams(vmem_limit_bytes=20 * 1024 * 1024),
        name=name,
    )(*args)


def copies_body(source, out, held, sems):
    count = out.shape[0]
    load = pltpu.make_async_copy(source, held, sems.at[count])
    load.start()
    load.wait()
    copies = [pltpu.make_async_copy(held, out.at[i], sems.at[i]) for i in range(count)]
    for copy in copies:
        copy.start()
    for copy in copies:
        copy.wait()


def join_body(near, far, out):
    rows = near.shape[0]
    out[:rows, :] = near[...]
    out[rows:, :] = far[...]


def pair_row(mine, seen):
    first = lax.axis_index("xl") == 0
    left = mine[...].astype(F32)[None, :]
    right = seen[...].astype(F32)[None, :]
    return jnp.concatenate(
        [jnp.where(first, left, right), jnp.where(first, right, left)], axis=1
    )


def score_body(steps, inv_root, *refs):
    n_z = 2 * len(steps)
    pieces, refs = refs[:n_z], refs[n_z:]
    image, pair_mine, pair_seen, pair_out, scores, text, hold, cross = refs
    pair = pair_row(pair_mine, pair_seen)
    pair_out[...] = pair
    rows = pieces[0].shape[0] // 2
    size = image.shape[0]
    ids = labels(n_z, rows)
    found = jnp.zeros((1, size), F32)
    z = lax.axis_index("z")
    high = jnp.zeros(pieces[0].shape, BF16)
    for h in range(2):
        for i, q in enumerate(steps):
            piece = pieces[h * n_z // 2 + i]
            if h == 0:
                high = jnp.maximum(high, jnp.abs(piece[...]))
            for k in range(2):
                to = lax.rem(z + lean(q, z, n_z) + (k + 2) * n_z // 2, n_z)
                start = (h * n_z + to) * rows
                text[pl.ds(pl.multiple_of(start, 16), rows), :] = piece[
                    k * rows : (k + 1) * rows, :
                ]
    lanes = []
    col_top = jnp.full((1, size), -1e38, F32)
    step = 256
    for r in range(0, size, step):
        tile = (
            lax.dot_general(
                image[r : r + step, :],
                text[...],
                (((1,), (1,)), ((), ())),
                preferred_element_type=F32,
            )
            * (inv_root / math.log(2.0))
        )
        scores[r : r + step, :] = tile
        col_top = jnp.maximum(col_top, jnp.max(tile, axis=0, keepdims=True))
        top = jnp.max(tile, axis=1, keepdims=True)
        part = jnp.log2(jnp.sum(jnp.exp2(tile - top), axis=1, keepdims=True))
        lanes.append(to_row(top + part))
        hit = to_column(pair[:, r : r + step]) == ids
        found += jnp.sum(jnp.where(hit, tile, 0.0), axis=0, keepdims=True)
    mass = jnp.exp2(scores[...] - col_top)
    col = col_top + jnp.log2(jnp.sum(mass, axis=0, keepdims=True))
    wide = jnp.zeros((rows, image.shape[1]), BF16)
    for r in range(0, size, rows):
        wide = jnp.maximum(wide, jnp.abs(image[r : r + rows, :]))
    image_max = jnp.max(wide.astype(F32))
    zero = jnp.zeros((1, LANES), F32)
    rows_out = jnp.concatenate([*lanes, zero + jnp.max(high.astype(F32)), zero], axis=1)
    cols_out = jnp.concatenate([col, zero + image_max, zero + jnp.sum(found)], axis=1)
    first = lax.axis_index("c") == 0
    hold[...] = jnp.where(first, cols_out, rows_out)
    cross[...] = jnp.where(first, rows_out, cols_out)


def crossed(cols):
    half = cols.shape[1] // 2
    return jnp.concatenate([cols[:, half:], cols[:, :half]], axis=1)


def meet_body(hold, seen, out):
    size = hold.shape[1] - 2 * LANES
    first = lax.axis_index("c") == 0
    mine, other = hold[:, :size], seen[:, :size]
    out[:, :size] = jnp.where(first, merge([mine, crossed(other)]), mine)
    out[:, size : 2 * size] = jnp.where(first, 0.0, other)
    high = jnp.maximum(hold[:, size : size + LANES], seen[:, size : size + LANES])
    total = hold[:, size + LANES :] + seen[:, size + LANES :]
    out[:, 2 * size :] = jnp.concatenate([high, total], axis=1)


def round_body(last, mine, one, two, three, *outs):
    size = mine.shape[1] // 2 - LANES
    first = lax.axis_index("c") == 0
    parts = [mine[:, : 2 * size], three[:, : 2 * size]]
    for ref in (one, two):
        part = ref[:, : 2 * size]
        parts.append(jnp.where(first, -1e38, part) if last else part)
    lse = merge(parts)
    refs = (mine, one, two, three)
    at = slice(2 * size, 2 * size + LANES)
    high = functools.reduce(jnp.maximum, [ref[:, at] for ref in refs])
    total = sum(ref[:, 2 * size + LANES :] for ref in refs)
    outs[0][...] = jnp.concatenate([lse, high, total], axis=1)
    if last:
        kept = jnp.where(first, lse[:, :size], lse[:, size:])
        outs[1][...] = jnp.concatenate([kept, high, total], axis=1)


def labels(n_z, rows):
    half = n_z * rows
    n_xl, n_c, n_xh = (lax.axis_size(a) for a in ("xl", "c", "xh"))
    block = (lax.axis_index("y") * n_xh + lax.axis_index("xh")) * n_xl + lax.axis_index("xl")
    core = lax.axis_index("c")
    slot = lax.broadcasted_iota(jnp.int32, (1, 2 * half), 1)
    own = slot < half
    within = jnp.where(own, slot, slot - half)
    holder = jnp.floor((within.astype(F32) + 0.5) * (1.0 / rows)).astype(jnp.int32)
    ids = ((block * n_z + holder) * n_c + jnp.where(own, core, 1 - core)) * rows
    return (ids + within - holder * rows).astype(F32)


def grad_body(n_z, inv_root, *refs):
    mine, seen, scores, text, image, pair = refs[:6]
    terms, own, other, sent, grads, held, crossing, sems = refs[6:]
    size = grads.shape[0]
    half = own.shape[0]
    rows = half // n_z
    _, tall, _ = sent.shape
    ids = labels(n_z, rows)
    first = lax.axis_index("c") == 0
    seen_lse, seen_high = seen[:, :size], seen[:, size : size + LANES]
    mine_lse, mine_high = mine[:, :size], mine[:, 2 * size : 2 * size + LANES]
    col_lse = jnp.where(first, mine_lse, crossed(seen_lse))
    row_lse = jnp.where(first, seen_lse, mine_lse)
    image_max = jnp.where(first, mine_high, seen_high)
    text_max = jnp.where(first, seen_high, mine_high)
    found = jnp.where(first, mine[:, 2 * size + LANES :], seen[:, size + LANES :])
    row_terms = jnp.broadcast_to(jnp.sum(row_lse, axis=1, keepdims=True), (1, LANES))
    col_terms = jnp.sum(col_lse, axis=1, keepdims=True) - 2.0 * found
    terms[...] = jnp.concatenate(
        [row_terms, text_max, image_max, jnp.zeros((5, LANES), F32)], axis=0
    )
    row_column = to_column(row_lse + 1.0)
    col_row = col_lse + 1.0
    pair_column = to_column(pair[...])
    extra = split3(col_terms)
    scale = inverse(text_max[:, :1]) * inv_root
    step = size // 4
    copies = []
    for r in range(0, size, step):
        at = slice(r, r + step)
        tile = scores[at, :]
        probs = jnp.exp2(tile - row_column[at, :]) + jnp.exp2(tile - col_row)
        grad = (probs - jnp.where(pair_column[at, :] == ids, 1.0, 0.0)).astype(BF16)
        grads[at, :] = grad
        part = encode(jnp.dot(grad, text[...], preferred_element_type=F32) * scale)
        for p in range(step // rows):
            to = r // rows + p
            for k in range(text.shape[1] // LANES):
                held[to, k * rows : (k + 1) * rows, :] = part[
                    p * rows : (p + 1) * rows, k * LANES : (k + 1) * LANES
                ]
            held[to, tall - EXTRA :, :] = extra
            copies.append(pltpu.make_async_copy(held.at[to], sent.at[to], sems.at[to]))
            copies[-1].start()
    scale = inverse(image_max[:, :1]) * inv_root
    extra = split3(row_terms)
    crossing[half:, :] = jnp.concatenate([extra] * (own.shape[1] // LANES), axis=1)
    for start in (half, 0):
        part = lax.dot_general(
            grads[:, start : start + half],
            image[...],
            (((0,), (0,)), ((), ())),
            preferred_element_type=F32,
        )
        if start == 0:
            own[...] = encode(part * scale)
        else:
            crossing[:half, :] = encode(part * scale)
            copies.append(pltpu.make_async_copy(crossing, other, sems.at[sent.shape[0]]))
            copies[-1].start()
    for copy in copies:
        copy.wait()


def pack(pay, blocks, extra):
    rows, width = blocks[0].shape
    at = 0
    for block in blocks:
        coded = encode(block)
        for k in range(width // LANES):
            pay[at : at + rows, :] = coded[:, k * LANES : (k + 1) * LANES]
            at += rows
    pay[at:, :] = extra


def send_body(steps, own, seen, terms, keep, total, *pays):
    n_z = 2 * len(steps)
    rows = keep.shape[0] // 2
    z = lax.axis_index("z")
    half = own.shape[0]
    tail = seen[half:, :LANES].astype(F32)
    row_terms = terms[0:1, :] + jnp.sum(tail, axis=0, keepdims=True)
    total[...] = row_terms
    extra = split3(row_terms)
    for i, q in enumerate(steps):
        blocks = []
        for k in range(2):
            to = lax.rem(z + lean(q, z, n_z) + (k + 2) * n_z // 2, n_z)
            start = to * rows
            at = pl.ds(pl.multiple_of(start, 16), rows)
            blocks.append(decode(own[at, :]) + decode(seen[at, :]))
        if i == 0:
            keep[:rows, :] = blocks[0]
            keep[rows:, :] = blocks[1]
        else:
            pack(pays[i - 1], blocks, extra)


def unpack(pays, at, rows, width):
    return jnp.concatenate(
        [
            sum(decode(p[at + k * rows : at + (k + 1) * rows, :]) for p in pays)
            for k in range(width // LANES)
        ],
        axis=1,
    )


def tails(pays):
    tail = sum(p[p.shape[0] - EXTRA :, :].astype(F32) for p in pays)
    return jnp.sum(tail, axis=0, keepdims=True)


def relay_body(keep, total, *refs):
    pays, near, far, total_out = refs[:-3], refs[-3], refs[-2], refs[-1]
    rows, width = near.shape
    near[...] = keep[:rows, :] + unpack(pays, 0, rows, width)
    sums = total[...] + tails(pays)
    total_out[...] = sums
    block = keep[rows:, :] + unpack(pays, rows * width // LANES, rows, width)
    pack(far, [block], split3(sums))


def text_sum_body(near, total, terms, pay, out, side):
    rows, width = out.shape
    unit = terms[2:3, :1]
    unit = jnp.where(unit > 0, unit, 1.0)
    out[...] = unit * (near[...] + unpack([pay], 0, rows, width))
    side[...] = total[...] + tails([pay])


def image_sum_body(pairs, got, terms, side, out, loss):
    rows, width = out.shape
    unit = terms[1:2, :1]
    unit = jnp.where(unit > 0, unit, 1.0)
    pays = [got.at[p] for p in range(got.shape[0])]
    for k in range(width // LANES):
        at = slice(k * rows, (k + 1) * rows)
        out[:, k * LANES : (k + 1) * LANES] = unit * sum(decode(p[at, :]) for p in pays)
    full = side[...] + tails(pays)
    loss[0, 0] = jnp.max(full) * (math.log(2.0) / (2.0 * pairs))


def shards(image_embed, text_embed, pair_index):
    rows, width = image_embed.shape
    n_xl, n_z, n_c, n_y, n_xh = (lax.axis_size(a) for a in ("xl", "z", "c", "y", "xh"))
    n_plane = n_xl * n_y * n_xh
    size = n_plane * rows
    half = n_z * rows
    pairs = size * n_z * n_c
    inv_root = width ** (-0.5)
    shape = jax.ShapeDtypeStruct
    tall = width // LANES * rows + EXTRA

    pair_seen = lax.ppermute(pair_index, "xl", SWAP)
    copies = pl.pallas_call(
        copies_body,
        out_shape=pltpu.HBM((n_plane, rows, width), BF16),
        in_specs=[pl.BlockSpec(memory_space=pl.ANY)],
        out_specs=pl.BlockSpec(memory_space=pltpu.HBM),
        scratch_shapes=[pltpu.VMEM((rows, width), BF16), pltpu.SemaphoreType.DMA((n_plane + 1,))],
        name="copies",
    )(image_embed)
    image = lax.all_to_all(copies, PLANE, 0, 0).reshape(size, width)

    signed = [q if q <= n_z // 4 else q - n_z // 2 for q in range(n_z // 2)]
    steps = sorted(signed, key=lambda q: (q != 0, -abs(q)))
    inward = [0, *steps[:0:-1]]
    far = turn(text_embed, "z", n_z // 2)
    (joined,) = call(
        join_body, (shape((2 * rows, width), BF16),), (text_embed, far), "join", 10**11
    )
    pieces = [joined] + [turn_z(joined, q, True) for q in inward[1:]]
    pieces = pieces + [lax.ppermute(piece, "c", SWAP) for piece in pieces]

    flops = 2 * size * size * width
    pair, scores, text, hold, cross = call(
        functools.partial(score_body, inward, inv_root),
        (
            shape((1, size), F32),
            shape((size, size), F32),
            shape((size, width), BF16),
            shape((1, size + 2 * LANES), F32),
            shape((1, size + 2 * LANES), F32),
        ),
        (*pieces, image, pair_index, pair_seen),
        "scores",
        flops,
        2 * size * size,
    )
    full = shape((1, 2 * size + 2 * LANES), F32)
    (stats,) = call(meet_body, (full,), (hold, lax.ppermute(cross, "c", SWAP)), "meet")
    around = [turn_both(stats, q, q, 0) for q in (1, -1, 2)]
    (stats,) = call(functools.partial(round_body, False), (full,), (stats, *around), "round")
    far_z = (None, None, n_z // 2)
    around = [turn_both(stats, f, 0, q) for f, q in zip(far_z, (1, -1, 2))]
    stats, cross = call(
        functools.partial(round_body, True), (full, shape(cross.shape, F32)), (stats, *around), "last"
    )
    seen = lax.ppermute(cross, "c", SWAP)

    terms, text_own, text_other, image_sent = call(
        functools.partial(grad_body, n_z, inv_root),
        (
            shape((8, LANES), F32),
            shape((half, width), BF16),
            pltpu.HBM((half + EXTRA, width), BF16),
            pltpu.HBM((n_plane, tall, LANES), BF16),
        ),
        (stats, seen, scores, text, image, pair),
        "grads",
        2 * flops,
        2 * size * size,
        hbm_out=(2, 3),
        scratch=[
            pltpu.VMEM((size, size), BF16),
            pltpu.VMEM((n_plane, tall, LANES), BF16),
            pltpu.VMEM((half + EXTRA, width), BF16),
            pltpu.SemaphoreType.DMA((n_plane + 1,)),
        ],
    )
    image_got = lax.all_to_all(image_sent, PLANE, 0, 0)
    keep, total, *pays = call(
        functools.partial(send_body, steps),
        (shape((2 * rows, width), F32), shape((1, LANES), F32))
        + (shape((2 * tall - EXTRA, LANES), BF16),) * len(steps[1:]),
        (text_own, lax.ppermute(text_other, "c", SWAP), terms),
        "send",
        10**10,
        size=1,
    )
    pays = [turn_z(pay, q, False) for q, pay in zip(steps[1:], pays)]
    near, far, total = call(
        relay_body,
        (shape((rows, width), F32), shape((tall, LANES), BF16), shape((1, LANES), F32)),
        (keep, total, *pays),
        "relay",
        size=1,
    )
    grad_text, side = call(
        text_sum_body,
        (shape((rows, width), F32), shape((1, LANES), F32)),
        (near, total, terms, turn(far, "z", n_z // 2)),
        "text_sum",
        size=1,
    )
    grad_image, loss = call(
        functools.partial(image_sum_body, pairs),
        (shape((rows, width), F32), shape((1, 1), F32)),
        (image_got, terms, side),
        "image_sum",
        smem_out=1,
    )
    return (loss[0, 0], grad_image, grad_text)


def solution(mesh):
    fine = Mesh(mesh.devices.reshape(2, 8, 2, 4, 2), ("xl", "z", "c", "y", "xh"))
    image_spec = P(("xl", "z", "c", "y", "xh"), None)
    text_spec = P(("y", "xh", "xl", "z", "c"), None)
    return jax.shard_map(
        shards,
        mesh=fine,
        in_specs=(image_spec, text_spec, P(("xl", "z", "c"))),
        out_specs=(P(), image_spec, text_spec),
        check_vma=False,
    )
```

```python
import functools
import math

import jax
import jax.numpy as jnp
from jax import lax
from jax.experimental import pallas as pl
from jax.experimental.pallas import tpu as pltpu
from jax.sharding import Mesh, PartitionSpec as P

AXES = ("xl", "z", "c", "y", "xh")
PLANE = ("xl", "y", "xh")
SWAP = [(0, 1), (1, 0)]
LANES = 128
EXTRA = 16
F32 = jnp.float32
BF16 = jnp.bfloat16


def turn(x, axis, step):
    count = lax.axis_size(axis)
    return lax.ppermute(x, axis, [(i, (i + step) % count) for i in range(count)])


def lean(q, z, count):
    return q * (1 - 2 * (z % 2)) if abs(q) == count // 4 else q


def turn_z(x, q, back):
    count = lax.axis_size("z")
    pairs = [((i + lean(q, i, count)) % count, i) for i in range(count)]
    return lax.ppermute(x, "z", pairs if back else [(b, a) for a, b in pairs])


def turn_both(x, step_z, step_x, step_y):
    sizes = [lax.axis_size(a) for a in AXES]
    n_xl, n_z, n_c, n_y, n_xh = sizes
    n_x = n_xl * n_xh
    pairs = []
    for i in range(math.prod(sizes)):
        rest, xh = divmod(i, n_xh)
        rest, y = divmod(rest, n_y)
        rest, c = divmod(rest, n_c)
        xl, z = divmod(rest, n_z)
        if c == 0:
            if step_z is None:
                continue
            z = (z + step_z) % n_z
        else:
            xh, xl = divmod((xh * n_xl + xl + step_x) % n_x, n_xl)
            y = (y + step_y) % n_y
        pairs.append((i, (((xl * n_z + z) * n_c + c) * n_y + y) * n_xh + xh))
    return lax.ppermute(x, AXES, pairs)


def merge(parts):
    high = functools.reduce(jnp.maximum, parts)
    return high + jnp.log2(sum(jnp.exp2(p - high) for p in parts))


def encode(scaled):
    return ((scaled * scaled) * (scaled * jnp.abs(scaled))).astype(BF16)


def decode(x):
    wide = x.astype(F32)
    half = lax.rsqrt(jnp.maximum(jnp.abs(wide), 1e-37))
    return wide * half * (half * lax.rsqrt(half))


def split3(value):
    high = value.astype(BF16).astype(F32)
    mid = (value - high).astype(BF16).astype(F32)
    low = value - high - mid
    row = lax.broadcasted_iota(jnp.int32, (EXTRA, LANES), 0)
    parts = jnp.where(row == 0, high, jnp.where(row == 1, mid, jnp.where(row == 2, low, 0.0)))
    return parts.astype(BF16)


def inverse(value):
    return jnp.where(value > 0, 1.0 / value, 1.0)


def to_column(row):
    return jnp.transpose(jnp.broadcast_to(row, (LANES, row.shape[1])))[:, :1]


def to_row(column):
    return jnp.transpose(jnp.broadcast_to(column, (column.shape[0], LANES)))[:1, :]


def call(
    body, outs, args, name, flops=0, exps=0, smem_out=None, size=None, hbm_out=(), scratch=()
):
    if size is None:
        size = sum(math.prod(a.shape) * a.dtype.itemsize for a in (*args, *outs))
    spaces = [pltpu.VMEM] * len(outs)
    if smem_out is not None:
        spaces[smem_out] = pltpu.SMEM
    for i in hbm_out:
        spaces[i] = pltpu.HBM
    return pl.pallas_call(
        body,
        out_shape=outs,
        in_specs=[pl.BlockSpec(memory_space=pltpu.VMEM)] * len(args),
        out_specs=tuple(pl.BlockSpec(memory_space=s) for s in spaces),
        scratch_shapes=scratch,
        cost_estimate=pl.CostEstimate(flops=flops, bytes_accessed=size, transcendentals=exps),
        compiler_params=pltpu.CompilerParams(vmem_limit_bytes=20 * 1024 * 1024),
        name=name,
    )(*args)


def copies_body(source, out, held, sems):
    count = out.shape[0]
    load = pltpu.make_async_copy(source, held, sems.at[count])
    load.start()
    load.wait()
    copies = [pltpu.make_async_copy(held, out.at[i], sems.at[i]) for i in range(count)]
    for copy in copies:
        copy.start()
    for copy in copies:
        copy.wait()


def join_body(near, far, out):
    rows = near.shape[0]
    out[:rows, :] = near[...]
    out[rows:, :] = far[...]


def pair_row(mine, seen):
    first = lax.axis_index("xl") == 0
    left = mine[...].astype(F32)[None, :]
    right = seen[...].astype(F32)[None, :]
    return jnp.concatenate(
        [jnp.where(first, left, right), jnp.where(first, right, left)], axis=1
    )


def score_body(steps, inv_root, *refs):
    n_z = 2 * len(steps)
    pieces, refs = refs[:n_z], refs[n_z:]
    image, pair_mine, pair_seen, pair_out, scores, text, hold, cross = refs
    pair = pair_row(pair_mine, pair_seen)
    pair_out[...] = pair
    rows = pieces[0].shape[0] // 2
    size = image.shape[0]
    ids = labels(n_z, rows)
    found = jnp.zeros((1, size), F32)
    z = lax.axis_index("z")
    high = jnp.zeros(pieces[0].shape, F32)
    for h in range(2):
        for i, q in enumerate(steps):
            piece = pieces[h * n_z // 2 + i]
            high = jnp.maximum(high, jnp.abs(piece[...].astype(F32)))
            for k in range(2):
                to = lax.rem(z + lean(q, z, n_z) + (k + 2) * n_z // 2, n_z)
                start = (h * n_z + to) * rows
                text[pl.ds(pl.multiple_of(start, 16), rows), :] = piece[
                    k * rows : (k + 1) * rows, :
                ]
    lanes = []
    col_top = jnp.full((1, size), -1e38, F32)
    step = 256
    for r in range(0, size, step):
        tile = (
            lax.dot_general(
                image[r : r + step, :],
                text[...],
                (((1,), (1,)), ((), ())),
                preferred_element_type=F32,
            )
            * (inv_root / math.log(2.0))
        )
        scores[r : r + step, :] = tile
        col_top = jnp.maximum(col_top, jnp.max(tile, axis=0, keepdims=True))
        top = jnp.max(tile, axis=1, keepdims=True)
        part = jnp.log2(jnp.sum(jnp.exp2(tile - top), axis=1, keepdims=True))
        lanes.append(to_row(top + part))
        hit = to_column(pair[:, r : r + step]) == ids
        found += jnp.sum(jnp.where(hit, tile, 0.0), axis=0, keepdims=True)
    mass = jnp.exp2(scores[...] - col_top)
    col = col_top + jnp.log2(jnp.sum(mass, axis=0, keepdims=True))
    image_max = jnp.max(jnp.abs(image[...].astype(F32)))
    zero = jnp.zeros((1, LANES), F32)
    rows_out = jnp.concatenate([*lanes, zero + jnp.max(high), zero], axis=1)
    cols_out = jnp.concatenate([col, zero + image_max, zero + jnp.sum(found)], axis=1)
    first = lax.axis_index("c") == 0
    hold[...] = jnp.where(first, cols_out, rows_out)
    cross[...] = jnp.where(first, rows_out, cols_out)


def crossed(cols):
    half = cols.shape[1] // 2
    return jnp.concatenate([cols[:, half:], cols[:, :half]], axis=1)


def meet_body(hold, seen, out):
    size = hold.shape[1] - 2 * LANES
    first = lax.axis_index("c") == 0
    mine, other = hold[:, :size], seen[:, :size]
    out[:, :size] = jnp.where(first, merge([mine, crossed(other)]), mine)
    out[:, size : 2 * size] = jnp.where(first, 0.0, other)
    high = jnp.maximum(hold[:, size : size + LANES], seen[:, size : size + LANES])
    total = hold[:, size + LANES :] + seen[:, size + LANES :]
    out[:, 2 * size :] = jnp.concatenate([high, total], axis=1)


def round_body(last, mine, one, two, three, *outs):
    size = mine.shape[1] // 2 - LANES
    first = lax.axis_index("c") == 0
    parts = [mine[:, : 2 * size], three[:, : 2 * size]]
    for ref in (one, two):
        part = ref[:, : 2 * size]
        parts.append(jnp.where(first, -1e38, part) if last else part)
    lse = merge(parts)
    refs = (mine, one, two, three)
    at = slice(2 * size, 2 * size + LANES)
    high = functools.reduce(jnp.maximum, [ref[:, at] for ref in refs])
    total = sum(ref[:, 2 * size + LANES :] for ref in refs)
    outs[0][...] = jnp.concatenate([lse, high, total], axis=1)
    if last:
        kept = jnp.where(first, lse[:, :size], lse[:, size:])
        outs[1][...] = jnp.concatenate([kept, high, total], axis=1)


def labels(n_z, rows):
    half = n_z * rows
    n_xl, n_c, n_xh = (lax.axis_size(a) for a in ("xl", "c", "xh"))
    block = (lax.axis_index("y") * n_xh + lax.axis_index("xh")) * n_xl + lax.axis_index("xl")
    core = lax.axis_index("c")
    slot = lax.broadcasted_iota(jnp.int32, (1, 2 * half), 1)
    own = slot < half
    within = jnp.where(own, slot, slot - half)
    holder = jnp.floor((within.astype(F32) + 0.5) * (1.0 / rows)).astype(jnp.int32)
    ids = ((block * n_z + holder) * n_c + jnp.where(own, core, 1 - core)) * rows
    return (ids + within - holder * rows).astype(F32)


def grad_body(n_z, inv_root, *refs):
    mine, seen, scores, text, image, pair = refs[:6]
    terms, own, other, sent, grads, held, crossing, sems = refs[6:]
    size = grads.shape[0]
    half = own.shape[0]
    rows = half // n_z
    _, tall, _ = sent.shape
    ids = labels(n_z, rows)
    first = lax.axis_index("c") == 0
    seen_lse, seen_high = seen[:, :size], seen[:, size : size + LANES]
    mine_lse, mine_high = mine[:, :size], mine[:, 2 * size : 2 * size + LANES]
    col_lse = jnp.where(first, mine_lse, crossed(seen_lse))
    row_lse = jnp.where(first, seen_lse, mine_lse)
    image_max = jnp.where(first, mine_high, seen_high)
    text_max = jnp.where(first, seen_high, mine_high)
    found = jnp.where(first, mine[:, 2 * size + LANES :], seen[:, size + LANES :])
    row_terms = jnp.broadcast_to(jnp.sum(row_lse, axis=1, keepdims=True), (1, LANES))
    col_terms = jnp.sum(col_lse, axis=1, keepdims=True) - 2.0 * found
    terms[...] = jnp.concatenate(
        [row_terms, text_max, image_max, jnp.zeros((5, LANES), F32)], axis=0
    )
    row_column = to_column(row_lse + 1.0)
    col_row = col_lse + 1.0
    pair_column = to_column(pair[...])
    extra = split3(col_terms)
    scale = inverse(text_max[:, :1]) * inv_root
    step = size // 4
    copies = []
    for r in range(0, size, step):
        at = slice(r, r + step)
        tile = scores[at, :]
        probs = jnp.exp2(tile - row_column[at, :]) + jnp.exp2(tile - col_row)
        grad = (probs - jnp.where(pair_column[at, :] == ids, 1.0, 0.0)).astype(BF16)
        grads[at, :] = grad
        part = encode(jnp.dot(grad, text[...], preferred_element_type=F32) * scale)
        for p in range(step // rows):
            to = r // rows + p
            for k in range(text.shape[1] // LANES):
                held[to, k * rows : (k + 1) * rows, :] = part[
                    p * rows : (p + 1) * rows, k * LANES : (k + 1) * LANES
                ]
            held[to, tall - EXTRA :, :] = extra
            copies.append(pltpu.make_async_copy(held.at[to], sent.at[to], sems.at[to]))
            copies[-1].start()
    scale = inverse(image_max[:, :1]) * inv_root
    extra = split3(row_terms)
    crossing[half:, :] = jnp.concatenate([extra] * (own.shape[1] // LANES), axis=1)
    for start in (half, 0):
        part = lax.dot_general(
            grads[:, start : start + half],
            image[...],
            (((0,), (0,)), ((), ())),
            preferred_element_type=F32,
        )
        if start == 0:
            own[...] = encode(part * scale)
        else:
            crossing[:half, :] = encode(part * scale)
            copies.append(pltpu.make_async_copy(crossing, other, sems.at[sent.shape[0]]))
            copies[-1].start()
    for copy in copies:
        copy.wait()


def pack(pay, blocks, extra):
    rows, width = blocks[0].shape
    at = 0
    for block in blocks:
        coded = encode(block)
        for k in range(width // LANES):
            pay[at : at + rows, :] = coded[:, k * LANES : (k + 1) * LANES]
            at += rows
    pay[at:, :] = extra


def send_body(steps, own, seen, terms, keep, total, *pays):
    n_z = 2 * len(steps)
    rows = keep.shape[0] // 2
    z = lax.axis_index("z")
    half = own.shape[0]
    tail = seen[half:, :LANES].astype(F32)
    row_terms = terms[0:1, :] + jnp.sum(tail, axis=0, keepdims=True)
    total[...] = row_terms
    extra = split3(row_terms)
    for i, q in enumerate(steps):
        blocks = []
        for k in range(2):
            to = lax.rem(z + lean(q, z, n_z) + (k + 2) * n_z // 2, n_z)
            start = to * rows
            at = pl.ds(pl.multiple_of(start, 16), rows)
            blocks.append(decode(own[at, :]) + decode(seen[at, :]))
        if i == 0:
            keep[:rows, :] = blocks[0]
            keep[rows:, :] = blocks[1]
        else:
            pack(pays[i - 1], blocks, extra)


def unpack(pays, at, rows, width):
    return jnp.concatenate(
        [
            sum(decode(p[at + k * rows : at + (k + 1) * rows, :]) for p in pays)
            for k in range(width // LANES)
        ],
        axis=1,
    )


def tails(pays):
    tail = sum(p[p.shape[0] - EXTRA :, :].astype(F32) for p in pays)
    return jnp.sum(tail, axis=0, keepdims=True)


def relay_body(keep, total, *refs):
    pays, near, far, total_out = refs[:-3], refs[-3], refs[-2], refs[-1]
    rows, width = near.shape
    near[...] = keep[:rows, :] + unpack(pays, 0, rows, width)
    sums = total[...] + tails(pays)
    total_out[...] = sums
    block = keep[rows:, :] + unpack(pays, rows * width // LANES, rows, width)
    pack(far, [block], split3(sums))


def text_sum_body(near, total, terms, pay, out, side):
    rows, width = out.shape
    unit = terms[2:3, :1]
    unit = jnp.where(unit > 0, unit, 1.0)
    out[...] = unit * (near[...] + unpack([pay], 0, rows, width))
    side[...] = total[...] + tails([pay])


def image_sum_body(pairs, got, terms, side, out, loss, held, sems):
    copies = []
    rows, width = out.shape
    unit = terms[1:2, :1]
    unit = jnp.where(unit > 0, unit, 1.0)
    pays = [got.at[p] for p in range(got.shape[0])]
    for k in range(width // LANES):
        at = slice(k * rows, (k + 1) * rows)
        lanes = pl.ds(k * LANES, LANES)
        held[:, lanes] = unit * sum(decode(p[at, :]) for p in pays)
        copies.append(pltpu.make_async_copy(held.at[:, lanes], out.at[:, lanes], sems.at[k]))
        copies[-1].start()
    full = side[...] + tails(pays)
    loss[0, 0] = jnp.max(full) * (math.log(2.0) / (2.0 * pairs))
    for copy in copies:
        copy.wait()


def shards(image_embed, text_embed, pair_index):
    rows, width = image_embed.shape
    n_xl, n_z, n_c, n_y, n_xh = (lax.axis_size(a) for a in ("xl", "z", "c", "y", "xh"))
    n_plane = n_xl * n_y * n_xh
    size = n_plane * rows
    half = n_z * rows
    pairs = size * n_z * n_c
    inv_root = width ** (-0.5)
    shape = jax.ShapeDtypeStruct
    tall = width // LANES * rows + EXTRA

    pair_seen = lax.ppermute(pair_index, "xl", SWAP)
    copies = pl.pallas_call(
        copies_body,
        out_shape=pltpu.HBM((n_plane, rows, width), BF16),
        in_specs=[pl.BlockSpec(memory_space=pl.ANY)],
        out_specs=pl.BlockSpec(memory_space=pltpu.HBM),
        scratch_shapes=[pltpu.VMEM((rows, width), BF16), pltpu.SemaphoreType.DMA((n_plane + 1,))],
        name="copies",
    )(image_embed)
    image = lax.all_to_all(copies, PLANE, 0, 0).reshape(size, width)

    signed = [q if q <= n_z // 4 else q - n_z // 2 for q in range(n_z // 2)]
    steps = sorted(signed, key=lambda q: (q != 0, -abs(q)))
    inward = [0, *steps[:0:-1]]
    far = turn(text_embed, "z", n_z // 2)
    (joined,) = call(
        join_body, (shape((2 * rows, width), BF16),), (text_embed, far), "join", 10**11
    )
    pieces = [joined] + [turn_z(joined, q, True) for q in inward[1:]]
    pieces = pieces + [lax.ppermute(piece, "c", SWAP) for piece in pieces]

    flops = 2 * size * size * width
    pair, scores, text, hold, cross = call(
        functools.partial(score_body, inward, inv_root),
        (
            shape((1, size), F32),
            shape((size, size), F32),
            shape((size, width), BF16),
            shape((1, size + 2 * LANES), F32),
            shape((1, size + 2 * LANES), F32),
        ),
        (*pieces, image, pair_index, pair_seen),
        "scores",
        flops,
        2 * size * size,
    )
    full = shape((1, 2 * size + 2 * LANES), F32)
    (stats,) = call(meet_body, (full,), (hold, lax.ppermute(cross, "c", SWAP)), "meet")
    around = [turn_both(stats, q, q, 0) for q in (1, -1, 2)]
    (stats,) = call(functools.partial(round_body, False), (full,), (stats, *around), "round")
    far_z = (None, None, n_z // 2)
    around = [turn_both(stats, f, 0, q) for f, q in zip(far_z, (1, -1, 2))]
    stats, cross = call(
        functools.partial(round_body, True), (full, shape(cross.shape, F32)), (stats, *around), "last"
    )
    seen = lax.ppermute(cross, "c", SWAP)

    terms, text_own, text_other, image_sent = call(
        functools.partial(grad_body, n_z, inv_root),
        (
            shape((8, LANES), F32),
            shape((half, width), BF16),
            pltpu.HBM((half + EXTRA, width), BF16),
            pltpu.HBM((n_plane, tall, LANES), BF16),
        ),
        (stats, seen, scores, text, image, pair),
        "grads",
        2 * flops,
        2 * size * size,
        hbm_out=(2, 3),
        scratch=[
            pltpu.VMEM((size, size), BF16),
            pltpu.VMEM((n_plane, tall, LANES), BF16),
            pltpu.VMEM((half + EXTRA, width), BF16),
            pltpu.SemaphoreType.DMA((n_plane + 1,)),
        ],
    )
    image_got = lax.all_to_all(image_sent, PLANE, 0, 0)
    keep, total, *pays = call(
        functools.partial(send_body, steps),
        (shape((2 * rows, width), F32), shape((1, LANES), F32))
        + (shape((2 * tall - EXTRA, LANES), BF16),) * len(steps[1:]),
        (text_own, lax.ppermute(text_other, "c", SWAP), terms),
        "send",
        10**10,
        size=1,
    )
    pays = [turn_z(pay, q, False) for q, pay in zip(steps[1:], pays)]
    near, far, total = call(
        relay_body,
        (shape((rows, width), F32), shape((tall, LANES), BF16), shape((1, LANES), F32)),
        (keep, total, *pays),
        "relay",
        size=1,
    )
    grad_text, side = call(
        text_sum_body,
        (shape((rows, width), F32), shape((1, LANES), F32)),
        (near, total, terms, turn(far, "z", n_z // 2)),
        "text_sum",
        size=1,
    )
    grad_image, loss = call(
        functools.partial(image_sum_body, pairs),
        (shape((rows, width), F32), shape((1, 1), F32)),
        (image_got, terms, side),
        "image_sum",
        smem_out=1,
        hbm_out=(0,),
        scratch=[pltpu.VMEM((rows, width), F32), pltpu.SemaphoreType.DMA((width // LANES,))],
    )
    return (loss[0, 0], grad_image, grad_text)


def solution(mesh):
    fine = Mesh(mesh.devices.reshape(2, 8, 2, 4, 2), ("xl", "z", "c", "y", "xh"))
    image_spec = P(("xl", "z", "c", "y", "xh"), None)
    text_spec = P(("y", "xh", "xl", "z", "c"), None)
    return jax.shard_map(
        shards,
        mesh=fine,
        in_specs=(image_spec, text_spec, P(("xl", "z", "c"))),
        out_specs=(P(), image_spec, text_spec),
        check_vma=False,
    )
```
